128 devices in a mesh: gx: 8 (over y, core), gy: 16 (over x, z).
Axes of the slice: x: 4, y: 4, z: 4, core: 2. Of those that a mesh axis runs over, the one named last changes fastest.
Arguments:
- psi_now: float32 [2, 8, 3072, 3072], P(None, None, 'gy', 'gx'), may hold values from -6 to 6
- potential: float32 [8, 3072, 3072], P(None, 'gy', 'gx'), may hold values from -10 to 0
- surf_cells: int32 [16, 8, 16], P('gy', 'gx'), may hold values from 385 to 73342, as said below
- surf_count: int32 [16, 8], P('gy', 'gx'), may hold values from 0 to 16, as said below
- block_count: int32 [128], replicated, may hold values from 0 to 4, as said below
- block_order: int32 [128], replicated, may hold values from 0 to 127, each once
- amplitude: float32 [512, 128, 2, 128], P(('gx', 'gy')), may hold values from -6 to 6
Outputs:
- psi_next: float32 [2, 8, 3072, 3072], P(None, None, 'gy', 'gx')
- amplitude_next: float32 [512, 128, 2, 128], P(('gx', 'gy'))
The draws below stay inside these ranges and needn't reach their ends.
Inputs may be any that keep to these rules, and one draw needn't show every extreme that they name: `surf_cells`: A flattened local cell y * 384 + x with 1 <= x <= 382 and 1 <= y <= 190. Live slots hold distinct cells within about half a cell of a circle of radius 1200 cells whose center lies near the middle of the grid; the other slots hold 385. `surf_count`: zero on tiles that the circle misses, at least 1 on the others; 16 on some tiles in every draw. `block_count`: the counts sum to 128; a sixteenth of the groups own 4 planes, an eighth own 2, the others 0 or 1; which groups is drawn.
All inputs are finite; a program needn't handle non-finite values.
Results may differ from the reference program's by a relative error of at most 0.00038.
Values sent between devices are 32-bit elements; how exact they have to be, the bound alone decides.
A program may use at most 256 MiB of HBM per device.

```python
import math
import jax
import jax.numpy as jnp
from jax import lax

CX = 384
CY = 192
CZ = 8
SXY = 16
KX = 128
KZ = 128
MAXB = 4
NX = 3072
NY = 3072
KY = 128
RAD = 1200
N_GX = 8
N_GY = 16


def surface_sample(key):
    base_key = jax.random.fold_in(key, 11)
    shift_key, score_key = jax.random.split(base_key)
    count_key = jax.random.fold_in(key, 37)
    limit_key, pick_key = jax.random.split(count_key)
    reach = min(NX, NY) // 48
    offset = jax.random.randint(shift_key, (2,), -reach, reach + 1)
    grid_rows = jnp.arange(NY, dtype=jnp.int32)
    grid_cols = jnp.arange(NX, dtype=jnp.int32)
    delta_y = grid_rows - NY // 2 - offset[0]
    delta_x = grid_cols - NX // 2 - offset[1]
    distance = delta_y[:, None] * delta_y[:, None] + delta_x[None, :] * delta_x[None, :]
    shell = jnp.abs(distance - RAD * RAD) <= RAD
    local_y = grid_rows % CY
    local_x = grid_cols % CX
    inner_y = (local_y >= 1) & (local_y <= CY - 2)
    inner_x = (local_x >= 1) & (local_x <= CX - 2)
    usable = shell & inner_y[:, None] & inner_x[None, :]
    flat_cell = local_y[:, None] * CX + local_x[None, :]
    noise = jax.random.randint(score_key, (NY, NX), 0, 4096)
    score = jnp.where(usable, noise * 524288 + flat_cell, -1)
    tiles_y = NY // CY
    tiles_x = NX // CX
    score = score.reshape(tiles_y, CY, tiles_x, CX).transpose(0, 2, 1, 3).reshape(tiles_y, tiles_x, CY * CX)
    usable_tiles = usable.astype(jnp.int32).reshape(tiles_y, CY, tiles_x, CX).transpose(0, 2, 1, 3).reshape(tiles_y, tiles_x, CY * CX)
    found = jnp.sum(usable_tiles, axis=2)
    limits = jax.random.randint(limit_key, (tiles_y, tiles_x), 1, SXY + 1)
    tile_total = tiles_y * tiles_x
    tile_ids = jnp.arange(tile_total, dtype=jnp.int32).reshape(tiles_y, tiles_x)
    ranks = jax.random.randint(pick_key, (tiles_y, tiles_x), 0, 1024)
    ranking = jnp.where(found >= SXY, ranks * tile_total + tile_ids, -1)
    widest = ranking == jnp.max(ranking)
    limits = jnp.where(widest, SXY, limits)
    live_count = jnp.minimum(found, limits).astype(jnp.int32)
    top_scores, top_cells = lax.top_k(score, SXY)
    slot_ids = jnp.arange(SXY, dtype=jnp.int32)
    chosen = jnp.where(slot_ids[None, None, :] < live_count[:, :, None], top_cells, CX + 1)
    return (chosen.astype(jnp.int32), live_count)


def draw_surf_cells(key, part):
    return surface_sample(key)[0]


def draw_surf_count(key, part):
    return surface_sample(key)[1]


def draw_block_count(key, part):
    own_key = jax.random.fold_in(key, 23)
    order = jax.random.permutation(own_key, KY)
    largest = KY // 16
    paired = KY // 8
    empty_groups = largest * (MAXB - 1) + paired
    ranking = jnp.arange(KY, dtype=jnp.int32)
    by_rank = jnp.where(ranking < largest, MAXB, jnp.where(ranking < largest + paired, 2, jnp.where(ranking < largest + paired + empty_groups, 0, 1)))
    return jnp.zeros((KY,), jnp.int32).at[order].set(by_rank.astype(jnp.int32))


def levels(key, dims, shards, low, top_value):
    def one(dim, parts):
        steps = jax.random.uniform(jax.random.fold_in(jax.random.fold_in(key, 6), dim), (parts,), jnp.float32, low / len(shards), top_value / len(shards))
        return jnp.repeat(jnp.exp(steps), dims[dim] // parts).reshape((-1,) + (1,) * (len(dims) - dim - 1))

    level = one(*shards[0])
    for cut in shards[1:]:
        level = level * one(*cut)
    return level


def centred(key, shape, deviation, most, shards=(), kind=jnp.bfloat16):
    result = jax.random.normal(key, shape, jnp.float32) * deviation
    if len(shards) > 0:
        result = levels(key, shape, shards, -0.22, 0.18) * result
    return jnp.clip(result, min=-most, max=most).astype(kind)


def setup_inputs(seed: int = 0) -> dict:
    streams_of = jax.random.split(jax.random.key(seed), 8)
    return {
        "psi_now": centred(streams_of[0], (2, CZ, NY, NX), 1.0, 6.0, ((2, 16), (3, 8)), jnp.float32),
        "potential": jnp.clip(-10.0 + 10.0 * jax.random.uniform(streams_of[1], (CZ, NY, NX), jnp.float32) ** levels(streams_of[1], (CZ, NY, NX), ((1, 16), (2, 8)), -0.2, 0.2), -10.0, 0.0),
        "surf_cells": draw_surf_cells(jax.random.fold_in(streams_of[7], 71), 0),
        "surf_count": draw_surf_count(jax.random.fold_in(streams_of[7], 71), 0),
        "block_count": draw_block_count(jax.random.fold_in(streams_of[7], 71), 0),
        "block_order": jax.random.permutation(streams_of[5], KY).astype(jnp.int32),
        "amplitude": centred(streams_of[6], (KY * MAXB, KX, 2, KZ), 1.0, 6.0, ((0, 128),), jnp.float32),
    }


spacing = 0.2
kinetic = 12.5
step_dt = 0.016
half_dt = 0.008
start_time = 100.0
field_peak = 0.05
field_freq = 0.057
k_span = 4.0
flux_weight = 0.0078125
highest = lax.Precision.HIGHEST

def field_at(moment):
    return field_peak * math.sin(field_freq * moment)

def drift_at(moment):
    return field_peak / (field_freq * field_freq) * math.sin(field_freq * moment)

def plane_heights(planes):
    return spacing * (jnp.arange(planes).astype(jnp.float32) - 0.5 * (planes - 1))

def momenta(points):
    return (jnp.arange(points).astype(jnp.float32) - 0.5 * (points - 1)) * (k_span / points)

def apply_hamiltonian(padded, potential, moment):
    center = padded[:, 1:-1, 1:-1]
    vertical = jnp.pad(center, ((1, 1), (0, 0), (0, 0)))
    beside = padded[:, 2:, 1:-1] + padded[:, :-2, 1:-1] + padded[:, 1:-1, 2:] + padded[:, 1:-1, :-2]
    beside = beside + vertical[2:] + vertical[:-2]
    heights = plane_heights(center.shape[0])[:, None, None]
    return -kinetic * (beside - 6.0 * center) + (potential + field_at(moment) * heights) * center

def rate_of(padded, potential, moment):
    return jnp.stack([apply_hamiltonian(padded[1], potential, moment), -apply_hamiltonian(padded[0], potential, moment)])

def normals(coord_x, coord_y):
    radius = jnp.sqrt(coord_x * coord_x + coord_y * coord_y)
    return (coord_x / radius, coord_y / radius)

def surface_values(wave_field, cell_ids, stride, normal_x, normal_y):
    flat_field = wave_field.reshape(wave_field.shape[0], wave_field.shape[1], -1)
    at_cell = jnp.take(flat_field, cell_ids, axis=2)
    across_x = jnp.take(flat_field, cell_ids + 1, axis=2) - jnp.take(flat_field, cell_ids - 1, axis=2)
    across_y = jnp.take(flat_field, cell_ids + stride, axis=2) - jnp.take(flat_field, cell_ids - stride, axis=2)
    slope = (normal_x * across_x + normal_y * across_y) / (2.0 * spacing)
    return (jnp.transpose(at_cell, (0, 2, 1)), jnp.transpose(slope, (0, 2, 1)))

def plane_modes(values, moment, mode_count):
    wave_z = momenta(mode_count)[:, None]
    heights = plane_heights(values.shape[2])[None, :]
    phase_all = 0.5 * wave_z * wave_z * moment + wave_z * drift_at(moment) - wave_z * heights
    cos_part = jnp.cos(phase_all).T
    sin_part = jnp.sin(phase_all).T
    real_part = jnp.dot(values[0], cos_part, precision=highest) - jnp.dot(values[1], sin_part, precision=highest)
    imag_part = jnp.dot(values[1], cos_part, precision=highest) + jnp.dot(values[0], sin_part, precision=highest)
    return jnp.stack([real_part, imag_part])

def rhs_matrix(mode_u, mode_d, normal_x, normal_y):
    side_x = (normal_x[None, None, :, None] * mode_u).astype(jnp.bfloat16)
    side_y = (normal_y[None, None, :, None] * mode_u).astype(jnp.bfloat16)
    slope_part = mode_d.astype(jnp.bfloat16)
    stacked = jnp.stack([side_x, side_y, slope_part], axis=3)
    sample_rows = stacked.shape[0] * stacked.shape[2]
    real_rows = stacked[:, 0].reshape(sample_rows, -1)
    imag_rows = stacked[:, 1].reshape(sample_rows, -1)
    upper_half = jnp.concatenate([real_rows, imag_rows], axis=1)
    lower_half = jnp.concatenate([-imag_rows, real_rows], axis=1)
    return jnp.concatenate([upper_half, lower_half], axis=0)

def left_matrix(wave_x, wave_y, coord_x, coord_y):
    sample_times = jnp.array([start_time, start_time + step_dt], dtype=jnp.float32)
    energy = 0.5 * (wave_x * wave_x + wave_y * wave_y)
    phase_all = energy[:, None, None] * sample_times[None, :, None] - wave_x[:, None, None] * coord_x[None, None, :] - wave_y[:, None, None] * coord_y[None, None, :]
    phase_all = phase_all.reshape(phase_all.shape[0], -1)
    return jnp.concatenate([jnp.cos(phase_all), jnp.sin(phase_all)], axis=1).astype(jnp.bfloat16)

def flux_increment(wave_x, wave_y, left_side, right_side, mode_count):
    product = jnp.dot(left_side, right_side, preferred_element_type=jnp.float32)
    row_count = product.shape[0]
    real_sets = product[:, :3 * mode_count].reshape(row_count, 3, mode_count)
    imag_sets = product[:, 3 * mode_count:].reshape(row_count, 3, mode_count)
    half_x = 0.5 * wave_x[:, None]
    half_y = 0.5 * wave_y[:, None]
    real_out = flux_weight * (half_x * real_sets[:, 0] + half_y * real_sets[:, 1] + 0.5 * imag_sets[:, 2])
    imag_out = flux_weight * (half_x * imag_sets[:, 0] + half_y * imag_sets[:, 1] - 0.5 * real_sets[:, 2])
    return jnp.stack([real_out, imag_out], axis=1)

def reference(psi_now, potential, surf_cells, surf_count, block_count, block_order, amplitude):
    padder = ((0, 0), (0, 0), (1, 1), (1, 1))
    later_time = start_time + step_dt
    rate_one = rate_of(jnp.pad(psi_now, padder), potential, start_time)
    section_field = psi_now + step_dt * rate_one
    rate_two = rate_of(jnp.pad(section_field, padder), potential, later_time)
    psi_next = psi_now + half_dt * (rate_one + rate_two)
    tile_row = jnp.arange(N_GY).astype(jnp.int32)[:, None, None]
    tile_col = jnp.arange(N_GX).astype(jnp.int32)[None, :, None]
    grid_y = (tile_row * CY + surf_cells // CX).reshape(-1)
    grid_x = (tile_col * CX + surf_cells % CX).reshape(-1)
    slot_ids = jnp.arange(SXY).astype(jnp.int32)
    live_mask = (slot_ids[None, None, :] < surf_count[:, :, None]).reshape(-1)
    coord_x = spacing * (grid_x.astype(jnp.float32) - (0.5 * NX - 0.5))
    coord_y = spacing * (grid_y.astype(jnp.float32) - (0.5 * NY - 0.5))
    normal_x, normal_y = normals(coord_x, coord_y)
    cell_ids = grid_y * NX + grid_x
    list_u = []
    list_d = []
    for wave_field, moment in ((psi_now, start_time), (psi_next, later_time)):
        at_cell, slope = surface_values(wave_field, cell_ids, NX, normal_x, normal_y)
        at_cell = jnp.where(live_mask[None, :, None], at_cell, 0.0)
        slope = jnp.where(live_mask[None, :, None], slope, 0.0)
        list_u.append(plane_modes(at_cell, moment, KZ))
        list_d.append(plane_modes(slope, moment, KZ))
    mode_u = jnp.stack(list_u)
    mode_d = jnp.stack(list_d)
    right_side = rhs_matrix(mode_u, mode_d, normal_x, normal_y)
    wave_x = momenta(KX)

    def per_plane(plane_wave):
        wave_y = jnp.zeros((KX,), jnp.float32) + plane_wave
        left_side = left_matrix(wave_x, wave_y, coord_x, coord_y)
        return flux_increment(wave_x, wave_y, left_side, right_side, KZ)
    increments = lax.map(per_plane, momenta(KY))
    offsets = (jnp.cumsum(block_count) - block_count).astype(jnp.int32)
    owner_slots = jnp.arange(MAXB).astype(jnp.int32)
    position = offsets[:, None] + owner_slots[None, :]
    filled = (owner_slots[None, :] < block_count[:, None]).reshape(-1)
    plane_ids = block_order[jnp.minimum(position, KY - 1).reshape(-1)]
    picked = increments[plane_ids]
    amplitude_next = amplitude + jnp.where(filled[:, None, None, None], picked, 0.0)
    return (psi_next, amplitude_next)
```

```python
import functools
import math

import jax
import jax.numpy as jnp
import numpy as np
from jax import lax
from jax.experimental import pallas as pl
from jax.experimental.pallas import tpu as pltpu
from jax.sharding import PartitionSpec as P

spacing = 0.2
kinetic = 12.5
step_dt = 0.016
half_dt = 0.008
start_time = 100.0
later_time = start_time + step_dt
field_peak = 0.05
field_freq = 0.057
k_span = 4.0
flux_weight = 0.0078125
MESH = pl.DeviceIdType.MESH
f32 = jnp.float32


def field_at(moment):
    return field_peak * math.sin(field_freq * moment)


def drift_at(moment):
    return field_peak / (field_freq * field_freq) * math.sin(field_freq * moment)


def mode_weights(planes, modes):
    wave = ((np.arange(modes) - 0.5 * (modes - 1)) * (k_span / modes)).astype(np.float32)
    height = np.float32(spacing) * (np.arange(planes) - 0.5 * (planes - 1)).astype(np.float32)
    out = np.zeros((2, 4 * planes, 4 * modes), np.float32)
    for t, moment in enumerate((start_time, later_time)):
        phase = (
            np.float32(0.5) * wave * wave * np.float32(moment) + wave * np.float32(drift_at(moment))
        )[None, :] - wave[None, :] * height[:, None]
        cos = np.cos(phase.astype(np.float64)).astype(np.float32)
        sin = np.sin(phase.astype(np.float64)).astype(np.float32)
        block = np.block([[cos, sin], [-sin, cos]])
        out[t, : 2 * planes, : 2 * modes] = block
        out[t, 2 * planes :, 2 * modes :] = block
    return out


def iota(shape, dim):
    return lax.broadcasted_iota(jnp.int32, shape, dim)


def step_kernel(
    x_count,
    y_count,
    cells_ref,
    count_ref,
    psi_hbm,
    pot_hbm,
    next_hbm,
    gather_0,
    gather_1,
    live_ref,
    psi_v,
    sec_v,
    pot_v,
    row_msg,
    row_got,
    col_msg,
    col_got,
    corner_got,
    ghost,
    load_sem,
    store_sem,
    row_send,
    row_recv,
    col_send,
    col_recv,
    corner_send,
    corner_recv,
    x_send,
    x_recv,
    y_send,
    y_recv,
):
    gx = lax.axis_index("gx")
    gy = lax.axis_index("gy")
    parts, rows, cols = psi_hbm.shape
    planes = parts // 2
    blocks = rows // 8
    lane_blocks = cols // 128
    top = 8

    def wrap(value, count):
        return lax.rem(value + count, count)

    west, east = wrap(gx - 1, x_count), wrap(gx + 1, x_count)
    north, south = wrap(gy - 1, y_count), wrap(gy + 1, y_count)
    loads = []
    for j in range(lane_blocks):
        sl = slice(128 * j, 128 * j + 128)
        loads.append(
            pltpu.make_async_copy(
                psi_hbm.at[:, :, sl], psi_v.at[j, :, top : top + rows, :], load_sem.at[0, j]
            )
        )
        loads.append(pltpu.make_async_copy(pot_hbm.at[:, :, sl], pot_v.at[j], load_sem.at[1, j]))
    for copy in loads:
        copy.start()

    barrier = pltpu.get_barrier_semaphore()
    for k in range(1, x_count):
        pl.semaphore_signal(barrier, inc=1, device_id=(wrap(gx + k, x_count), gy), device_id_type=MESH)
    for k in range(1, y_count):
        pl.semaphore_signal(barrier, inc=1, device_id=(gx, wrap(gy + k, y_count)), device_id_type=MESH)
    for sx in (west, east):
        for sy in (north, south):
            pl.semaphore_signal(barrier, inc=1, device_id=(sx, sy), device_id_type=MESH)

    for copy in loads:
        copy.wait()

    for side, (near, far) in enumerate(((top, top + 1), (top + rows - 1, top + rows - 2))):
        for j in range(lane_blocks):
            sl = slice(128 * j, 128 * j + 128)
            for p in range(parts):
                row_msg[side, p : p + 1, sl] = psi_v[j, p, near : near + 1, :]
                row_msg[side, parts + p : parts + p + 1, sl] = psi_v[j, p, far : far + 1, :]
            for z in range(planes):
                row_msg[side, 2 * parts + z : 2 * parts + z + 1, sl] = pot_v[
                    j, z, near - top : near - top + 1, :
                ]

    lane8 = iota((8, 128), 1)
    sub8 = iota((8, 128), 0)

    def pack(b, carry):
        r0 = pl.multiple_of(b * 8, 8)
        for side in range(2):
            j = 0 if side == 0 else lane_blocks - 1
            base = 0 if side == 0 else 2
            packed = jnp.zeros((8, 128), f32)
            for p in range(parts):
                block = psi_v[j, p, pl.ds(r0 + top, 8), :]
                packed = jnp.where(lane8 // 2 == p, pltpu.roll(block, (2 * p + base) % 128, 1), packed)
            for z in range(planes):
                block = pot_v[j, z, pl.ds(r0, 8), :]
                packed = jnp.where(
                    lane8 // 2 == 32 + z, pltpu.roll(block, (64 + 2 * z + base) % 128, 1), packed
                )
            col_msg[side, pl.ds(r0, 8), :] = packed
        return carry

    lax.fori_loop(0, blocks, pack, 0)

    pl.semaphore_wait(barrier, x_count - 1 + y_count - 1 + 4)

    halo = []
    for side, target in enumerate((north, south)):
        halo.append(
            pltpu.make_async_remote_copy(
                src_ref=row_msg.at[side],
                dst_ref=row_got.at[1 - side],
                send_sem=row_send.at[side],
                recv_sem=row_recv.at[1 - side],
                device_id=(gx, target),
                device_id_type=MESH,
            )
        )
    for side, target in enumerate((west, east)):
        halo.append(
            pltpu.make_async_remote_copy(
                src_ref=col_msg.at[side],
                dst_ref=col_got.at[1 - side],
                send_sem=col_send.at[side],
                recv_sem=col_recv.at[1 - side],
                device_id=(target, gy),
                device_id_type=MESH,
            )
        )
    for sy, ty in enumerate((north, south)):
        for sx, tx in enumerate((west, east)):
            lo = 0 if sx == 0 else cols - 128
            halo.append(
                pltpu.make_async_remote_copy(
                    src_ref=row_msg.at[sy, 0:parts, lo : lo + 128],
                    dst_ref=corner_got.at[2 * (1 - sy) + 1 - sx],
                    send_sem=corner_send.at[2 * sy + sx],
                    recv_sem=corner_recv.at[2 * (1 - sy) + 1 - sx],
                    device_id=(tx, ty),
                    device_id_type=MESH,
                )
            )
    for copy in halo:
        copy.start()

    lane_p = iota((parts, 128), 1)

    def take(slot, carry):
        out_u, out_d = carry
        cell = cells_ref[slot]
        y = cell // cols
        x = cell - y * cols
        alive = jnp.where(slot < count_ref[0], 1.0, 0.0).astype(f32)
        px = jnp.full((1, 128), spacing * ((gx * cols + x).astype(f32) - (0.5 * cols * x_count - 0.5)), f32)
        py = jnp.full((1, 128), spacing * ((gy * rows + y).astype(f32) - (0.5 * rows * y_count - 0.5)), f32)
        radius = jnp.sqrt(px * px + py * py)
        weight_x = px / radius / (2.0 * spacing) * alive
        weight_y = py / radius / (2.0 * spacing) * alive
        total_u = jnp.zeros((parts, 128), f32)
        total_d = jnp.zeros((parts, 128), f32)
        for j in range(lane_blocks):
            lane = iota((1, 128), 1) + 128 * j
            at = jnp.where(lane == x, alive, 0.0)
            along = jnp.where(lane == x + 1, weight_x, 0.0) - jnp.where(lane == x - 1, weight_x, 0.0)
            across = jnp.where(lane == x, weight_y, 0.0)
            flat = psi_v.at[j].reshape(parts * (rows + 16), 128)
            middle = flat[pl.ds(y + top, parts, stride=rows + 16), :]
            after = flat[pl.ds(y + top + 1, parts, stride=rows + 16), :]
            before = flat[pl.ds(y + top - 1, parts, stride=rows + 16), :]
            total_u = total_u + middle * at
            total_d = total_d + (middle * along + (after - before) * across)
        out_u = jnp.where(lane_p == slot, jnp.sum(total_u, axis=1, keepdims=True), out_u)
        out_d = jnp.where(lane_p == slot, jnp.sum(total_d, axis=1, keepdims=True), out_d)
        return out_u, out_d

    slots = cells_ref.shape[0]

    def surface(target, with_place):
        zero = jnp.zeros((parts, 128), f32)
        out_u, out_d = lax.fori_loop(0, slots, take, (zero, zero), unroll=4)
        turned = jnp.transpose(
            jnp.concatenate([out_u, out_d, jnp.zeros((128 - 2 * parts, 128), f32)], axis=0)
        )
        packed = jnp.where(lane8 < 64, turned[0:8], pltpu.roll(turned[8:16], 64, 1))
        if with_place:
            for slot in range(slots):
                cell = cells_ref[slot]
                y = cell // cols
                x = cell - y * cols
                px = spacing * ((gx * cols + x).astype(f32) - (0.5 * cols * x_count - 0.5))
                py = spacing * ((gy * rows + y).astype(f32) - (0.5 * rows * y_count - 0.5))
                base = 64 * (slot // 8) + 2 * parts
                row = sub8 == slot % 8
                packed = jnp.where(row & (lane8 == base), px, packed)
                packed = jnp.where(row & (lane8 == base + 1), py, packed)
            packed = jnp.where(lane8 == 2 * parts + 2, count_ref[0].astype(f32), packed)
        target[gy, gx] = packed

    def x_copy(buf, phase, k, source):
        return pltpu.make_async_remote_copy(
            src_ref=buf.at[gy, source],
            dst_ref=buf.at[gy, source],
            send_sem=x_send.at[phase, k],
            recv_sem=x_recv.at[phase, k],
            device_id=(wrap(gx + k, x_count), gy),
            device_id_type=MESH,
        )

    def y_copy(buf, phase, k, source):
        return pltpu.make_async_remote_copy(
            src_ref=buf.at[source],
            dst_ref=buf.at[source],
            send_sem=y_send.at[phase, k],
            recv_sem=y_recv.at[phase, k],
            device_id=(gx, wrap(gy + k, y_count)),
            device_id_type=MESH,
        )

    def x_start(buf, phase):
        for k in range(1, x_count):
            x_copy(buf, phase, k, gx).start()

    def x_wait(buf, phase):
        for k in range(1, x_count):
            x_copy(buf, phase, k, wrap(gx - k, x_count)).wait_recv()

    def y_start(buf, phase):
        for k in range(1, y_count):
            y_copy(buf, phase, k, gy).start()

    def y_wait(buf, phase):
        for k in range(1, y_count):
            y_copy(buf, phase, k, wrap(gy - k, y_count)).wait_recv()

    def sends_wait(buf, phase):
        for k in range(1, x_count):
            x_copy(buf, phase, k, gx).wait_send()
        for k in range(1, y_count):
            y_copy(buf, phase, k, gy).wait_send()

    surface(gather_0, True)
    x_start(gather_0, 0)

    for copy in halo:
        copy.wait_recv()

    keep_n = jnp.where(gy > 0, 1.0, 0.0).astype(f32)
    keep_s = jnp.where(gy < y_count - 1, 1.0, 0.0).astype(f32)
    keep_w = jnp.where(gx > 0, 1.0, 0.0).astype(f32)
    keep_e = jnp.where(gx < x_count - 1, 1.0, 0.0).astype(f32)
    field_1 = field_at(start_time)
    field_2 = field_at(later_time)

    def height(index):
        return spacing * (index.astype(f32) - 0.5 * (planes - 1))

    corner_cols = []
    for sy, keep_y in enumerate((keep_n, keep_s)):
        for sx, keep_x in enumerate((keep_w, keep_e)):
            lane = 127 if sx == 0 else 0
            corner_cols.append(corner_got[2 * sy + sx][:, lane : lane + 1] * (keep_y * keep_x))
    lane_row = iota((planes, cols), 1)
    sub_row = iota((planes, cols), 0)
    for side, keep in enumerate((keep_n, keep_s)):
        coeff = step_dt * (
            row_got[side, 2 * parts : 2 * parts + planes, :] + field_1 * height(sub_row) + 6.0 * kinetic
        )
        nears = []
        moves = []
        for part in range(2):
            sl = slice(part * planes, (part + 1) * planes)
            near = row_got[side, sl, :] * keep
            far = row_got[side, parts + part * planes : parts + (part + 1) * planes, :] * keep
            own = row_msg[side, sl, :]
            left = jnp.where(lane_row == 0, corner_cols[2 * side][sl], pltpu.roll(near, 1, 1))
            right = jnp.where(lane_row == cols - 1, corner_cols[2 * side + 1][sl], pltpu.roll(near, cols - 1, 1))
            below = jnp.where(sub_row == 0, 0.0, pltpu.roll(near, 1, 0))
            above = jnp.where(sub_row == planes - 1, 0.0, pltpu.roll(near, planes - 1, 0))
            beside = (far + own) + (left + right) + (below + above)
            nears.append(near)
            moves.append(coeff * near - (step_dt * kinetic) * beside)
        ghost_rows = (nears[0] + moves[1]) * keep, (nears[1] - moves[0]) * keep
        at = top - 1 if side == 0 else top + rows
        for part in range(2):
            for z in range(planes):
                for j in range(lane_blocks):
                    sl = slice(128 * j, 128 * j + 128)
                    psi_v[j, part * planes + z, at : at + 1, :] = nears[part][z : z + 1, sl]
                    sec_v[j, part * planes + z, at : at + 1, :] = ghost_rows[part][z : z + 1, sl]

    lane_c = iota((rows, 128), 1)
    sub_c = iota((rows, 128), 0)
    diag_lane = iota((parts, 128), 1)
    diag_sub = iota((parts, 128), 0)
    plane_c = (lane_c % (2 * planes)) // 2
    for side, keep in enumerate((keep_w, keep_e)):
        got = col_got[side] * keep
        mine = col_msg[side]
        inner = 1 if side == 0 else 127
        odd = 1 if side == 0 else 0
        hit = diag_lane == 2 * diag_sub + odd
        ends = [
            jnp.sum(jnp.where(hit, corner_cols[2 * sy + side], 0.0), axis=0, keepdims=True)
            for sy in range(2)
        ]
        upper = jnp.where(sub_c == 0, ends[0], pltpu.roll(got, 1, 0))
        lower = jnp.where(sub_c == rows - 1, ends[1], pltpu.roll(got, rows - 1, 0))
        below = jnp.where(plane_c == 0, 0.0, pltpu.roll(got, 2, 1))
        above = jnp.where(plane_c == planes - 1, 0.0, pltpu.roll(got, 126, 1))
        beside = (
            (pltpu.roll(got, inner, 1) + pltpu.roll(mine, inner, 1)) + (upper + lower) + (below + above)
        )
        volts = pltpu.roll(got, 64, 1)
        volts = jnp.where(lane_c < 2 * planes, volts, pltpu.roll(volts, 2 * planes, 1))
        coeff = step_dt * (volts + field_1 * height(plane_c) + 6.0 * kinetic)
        move = coeff * got - (step_dt * kinetic) * beside
        ghost[0, side] = got
        ghost[1, side] = (
            got
            + jnp.where(
                lane_c < 2 * planes, pltpu.roll(move, 128 - 2 * planes, 1), -pltpu.roll(move, 2 * planes, 1)
            )
        ) * keep

    first = lane8 == 0
    last = lane8 == 127

    def spread(src, p, r0, stage, b):
        rows_b = pl.ds(r0, 8)
        cur = [src[j, p, rows_b, :] for j in range(lane_blocks)]
        right = [pltpu.roll(c, 1, 1) for c in cur]
        left = [pltpu.roll(c, 127, 1) for c in cur]
        gr = pl.ds(pl.multiple_of(b * 8, 8), 8)
        edge_w = pltpu.roll(ghost[stage, 0, gr, :], (128 - (2 * p + 1)) % 128, 1)
        edge_e = pltpu.roll(ghost[stage, 1, gr, :], (127 - 2 * p) % 128, 1)
        out = []
        for j in range(lane_blocks):
            up = src[j, p, pl.ds(r0 - 1, 8), :]
            down = src[j, p, pl.ds(r0 + 1, 8), :]
            w = jnp.where(first, edge_w if j == 0 else right[j - 1], right[j])
            e = jnp.where(last, edge_e if j == lane_blocks - 1 else left[j + 1], left[j])
            out.append((up + down) + (w + e))
        return cur, out

    def stage_block(src, stage, b, finish):
        r0 = pl.multiple_of(b * 8 + top, 8)
        rows_b = pl.ds(r0, 8)
        dt = step_dt if stage == 0 else half_dt
        field = field_1 if stage == 0 else field_2
        for z in range(planes):
            found = [spread(src, part * planes + z, r0, stage, b) for part in range(2)]
            shift = dt * (field * spacing * (z - 0.5 * (planes - 1)) + 6.0 * kinetic)
            for j in range(lane_blocks):
                coeff = dt * pot_v[j, z, pl.ds(pl.multiple_of(b * 8, 8), 8), :] + shift
                moves = []
                for part in range(2):
                    cur, beside = found[part]
                    p = part * planes + z
                    total = beside[j]
                    if z > 0:
                        total = total + src[j, p - 1, rows_b, :]
                    if z < planes - 1:
                        total = total + src[j, p + 1, rows_b, :]
                    moves.append(coeff * cur[j] - (dt * kinetic) * total)
                finish(z, rows_b, j, found[0][0][j], found[1][0][j], moves)

    def finish_section(z, rows_b, j, real, imag, moves):
        sec_v[j, z, rows_b, :] = real + moves[1]
        sec_v[j, planes + z, rows_b, :] = imag - moves[0]

    def finish_next(z, rows_b, j, real, imag, moves):
        psi_v[j, z, rows_b, :] = 0.5 * (psi_v[j, z, rows_b, :] + real) + moves[1]
        psi_v[j, planes + z, rows_b, :] = 0.5 * (psi_v[j, planes + z, rows_b, :] + imag) - moves[0]

    def run_section(b, carry):
        stage_block(psi_v, 0, b, finish_section)
        return carry

    def run_next(b, carry):
        stage_block(sec_v, 1, b, finish_next)
        return carry

    lax.fori_loop(0, blocks, run_section, 0)
    x_wait(gather_0, 0)
    y_start(gather_0, 0)
    stores = []
    pieces = 4
    per = blocks // pieces
    for q in range(pieces):
        lax.fori_loop(q * per, (q + 1) * per, run_next, 0)
        for j in range(lane_blocks):
            stores.append(
                pltpu.make_async_copy(
                    psi_v.at[j, :, top + 8 * per * q : top + 8 * per * (q + 1), :],
                    next_hbm.at[:, 8 * per * q : 8 * per * (q + 1), 128 * j : 128 * j + 128],
                    store_sem.at[q, j],
                )
            )
            stores[-1].start()
    surface(gather_1, False)
    x_start(gather_1, 1)
    y_wait(gather_0, 0)

    def count_row(i, total):
        for k in range(x_count):
            total = jnp.where(
                lane8 == i * x_count + k, gather_0[i, k][:, 2 * parts + 2 : 2 * parts + 3], total
            )
        return total

    live_ref[...] = lax.fori_loop(0, y_count, count_row, jnp.zeros((8, 128), f32))
    x_wait(gather_1, 1)
    y_start(gather_1, 1)
    for copy in halo:
        copy.wait_send()
    for copy in stores:
        copy.wait()
    y_wait(gather_1, 1)
    sends_wait(gather_0, 0)
    sends_wait(gather_1, 1)


def turns(phase):
    quarter = jnp.floor(phase * 0.6366197723675814 + 0.5)
    rest = phase - quarter * 1.5703125
    rest = rest - quarter * 4.83751296997e-4
    rest = rest - quarter * 7.5497899548918821e-8
    square = rest * rest
    sine = rest + rest * square * (
        -1.6666654611e-1 + square * (8.3321608736e-3 + square * -1.9515295891e-4)
    )
    cosine = (
        1.0
        - 0.5 * square
        + square * square * (4.166664568298827e-2 + square * (-1.388731625493765e-3 + square * 2.443315711809948e-5))
    )
    which = quarter.astype(jnp.int32)
    swap = (which & 1) == 1
    sin_out = jnp.where(swap, cosine, sine)
    cos_out = jnp.where(swap, sine, cosine)
    sin_out = jnp.where((which & 2) == 2, -sin_out, sin_out)
    cos_out = jnp.where(((which + 1) & 2) == 2, -cos_out, cos_out)
    return cos_out, sin_out


def flux_kernel(
    x_count,
    y_count,
    live_ref,
    count_ref,
    order_ref,
    gather_0,
    gather_1,
    weight_ref,
    amp_ref,
    tmp_hbm,
    next_hbm,
    out_ref,
    comp_0,
    comp_1,
    total,
    copy_sem,
):
    copies = []
    parts = tmp_hbm.shape[0]
    quarter = parts // 4
    for q in range(4):
        sl = slice(q * quarter, (q + 1) * quarter)
        copies.append(pltpu.make_async_copy(tmp_hbm.at[sl], next_hbm.at[sl], copy_sem.at[q]))
        copies[-1].start()
    me = lax.axis_index("gx") * y_count + lax.axis_index("gy")
    groups = count_ref.shape[0]
    slots = amp_ref.shape[0]
    features = weight_ref.shape[1]

    def offset(i, at):
        return at + jnp.where(i < me, count_ref[i], 0)

    own_start = lax.fori_loop(0, groups, offset, 0, unroll=8)
    own_count = count_ref[me]
    waves = []
    for s in range(slots):
        plane = order_ref[jnp.minimum(own_start + s, groups - 1)]
        waves.append((plane.astype(f32) - 0.5 * (groups - 1)) * (k_span / groups))

    def gather_tile(t, n):
        c = live_ref[0, t]
        at = pl.ds(pl.multiple_of(t * 8, 8), 8)
        block_0, block_1 = gather_0[at, :], gather_1[at, :]
        to = pl.ds(pl.multiple_of(n * 8, 8), 8)
        comp_0[to, :] = block_0
        comp_1[to, :] = block_1
        n = n + jnp.where(c > 0.5, 1, 0)
        to = pl.ds(pl.multiple_of(n * 8, 8), 8)
        comp_0[to, :] = pltpu.roll(block_0, 64, 1)
        comp_1[to, :] = pltpu.roll(block_1, 64, 1)
        return n + jnp.where(c > 8.5, 1, 0)

    live = lax.fori_loop(0, x_count * y_count, gather_tile, 0, unroll=8)

    def clear(i, carry):
        to = pl.ds(pl.multiple_of((live + i) * 8, 8), 8)
        comp_0[to, :] = jnp.zeros((8, 128), f32)
        comp_1[to, :] = jnp.zeros((8, 128), f32)
        return carry

    lax.fori_loop(0, 16, clear, 0)
    total[...] = jnp.zeros_like(total)
    kx = (iota((128, 128), 0).astype(f32) - 63.5) * (k_span / 128)
    sub8 = iota((8, 128), 0)
    ky = jnp.zeros((8, 128), f32)
    for s in range(slots):
        ky = jnp.where(sub8 // 2 == s, waves[s], ky)
    moment8 = jnp.where(sub8 % 2 == 0, start_time, later_time).astype(f32)

    def chunk(c, carry):
        at = pl.ds(pl.multiple_of(c * 128, 128), 128)
        rows = (comp_0[at, :], comp_1[at, :])
        place = jnp.transpose(rows[0])
        px, py = place[features : features + 1, :], place[features + 1 : features + 2, :]
        col_x, col_y = rows[0][:, features : features + 1], rows[0][:, features + 1 : features + 2]
        square = col_x * col_x + col_y * col_y
        radius = jnp.sqrt(jnp.where(square > 0.0, square, 1.0))
        nx, ny = col_x / radius, col_y / radius
        right = []
        left = []
        for t, moment in enumerate((start_time, later_time)):
            modes = jnp.dot(
                rows[t][:, :features],
                weight_ref[t],
                precision=lax.Precision.HIGHEST,
                preferred_element_type=f32,
            )
            ur, ui, dr, di = (modes[:, 128 * i : 128 * i + 128] for i in range(4))
            right.append(
                jnp.concatenate([nx * ur, ny * ur, dr, nx * ui, ny * ui, di], axis=1).astype(jnp.bfloat16)
            )
            left.append(turns(0.5 * kx * kx * moment - kx * px))
        right = jnp.concatenate(right, axis=0)
        rot_cos, rot_sin = turns(0.5 * ky * ky * moment8 - ky * py)

        for s in range(slots):

            @pl.when(s < own_count)
            def _():
                real = []
                imag = []
                for t in range(2):
                    bc, bs = rot_cos[2 * s + t : 2 * s + t + 1], rot_sin[2 * s + t : 2 * s + t + 1]
                    ac, as_ = left[t]
                    real.append((ac * bc - as_ * bs).astype(jnp.bfloat16))
                    imag.append((ac * bs + as_ * bc).astype(jnp.bfloat16))
                q = jnp.concatenate(
                    [jnp.concatenate(real, axis=1), jnp.concatenate(imag, axis=1)], axis=0
                )
                prod = jnp.dot(q, right, preferred_element_type=f32)
                m = [prod[:128, 128 * i : 128 * i + 128] for i in range(6)]
                w = [prod[128:, 128 * i : 128 * i + 128] for i in range(6)]
                hy = waves[s]
                total[s, 0] += kx * (m[0] - w[3]) + hy * (m[1] - w[4]) + (m[5] + w[2])
                total[s, 1] += kx * (m[3] + w[0]) + hy * (m[4] + w[1]) - (m[2] - w[5])

        return carry

    lax.fori_loop(0, (live + 15) // 16, chunk, 0)
    for s in range(slots):
        for part in range(2):
            sl = pl.ds(part, 128, stride=2)
            inc = jnp.where(s < own_count, (0.5 * flux_weight) * total[s, part], 0.0)
            out_ref[s, sl, :] = amp_ref[s, sl, :] + inc
    for copy in copies:
        copy.wait()


def shards(psi_now, potential, surf_cells, surf_count, block_count, block_order, amplitude):
    x_count = lax.axis_size("gx")
    y_count = lax.axis_size("gy")
    planes, rows, cols = potential.shape
    parts = 2 * planes
    slots = surf_cells.shape[2]
    own, modes_x, _, modes_z = amplitude.shape
    any_spec = pl.BlockSpec(memory_space=pl.ANY)
    vmem = pl.BlockSpec(memory_space=pltpu.VMEM)
    smem = pl.BlockSpec(memory_space=pltpu.SMEM)
    dma = pltpu.SemaphoreType.DMA
    gathered = jax.ShapeDtypeStruct((y_count, x_count, 8, 128), f32)
    field = jax.ShapeDtypeStruct((parts, rows, cols), f32)
    staged, gather_0, gather_1, live = pl.pallas_call(
        functools.partial(step_kernel, x_count, y_count),
        out_shape=(field, gathered, gathered, jax.ShapeDtypeStruct((8, 128), f32)),
        in_specs=[smem, smem, any_spec, any_spec],
        out_specs=(any_spec, vmem, vmem, vmem),
        scratch_shapes=[
            pltpu.VMEM((cols // 128, parts, rows + 16, 128), f32),
            pltpu.VMEM((cols // 128, parts, rows + 16, 128), f32),
            pltpu.VMEM((cols // 128, planes, rows, 128), f32),
            pltpu.VMEM((2, 2 * parts + planes, cols), f32),
            pltpu.VMEM((2, 2 * parts + planes, cols), f32),
            pltpu.VMEM((2, rows, 128), f32),
            pltpu.VMEM((2, rows, 128), f32),
            pltpu.VMEM((4, parts, 128), f32),
            pltpu.VMEM((2, 2, rows, 128), f32),
            dma((2, cols // 128)),
            dma((4, cols // 128)),
            dma((2,)),
            dma((2,)),
            dma((2,)),
            dma((2,)),
            dma((4,)),
            dma((4,)),
            dma((2, x_count)),
            dma((2, x_count)),
            dma((2, y_count)),
            dma((2, y_count)),
        ],
        compiler_params=pltpu.CompilerParams(
            collective_id=0, has_side_effects=True, vmem_limit_bytes=40 * 1024 * 1024
        ),
        name="step",
    )(
        surf_cells.reshape(slots),
        surf_count.reshape(1),
        psi_now.reshape(parts, rows, cols),
        potential,
    )
    tiles = x_count * y_count
    psi_next, amplitude_next = pl.pallas_call(
        functools.partial(flux_kernel, x_count, y_count),
        out_shape=(field, jax.ShapeDtypeStruct((own, 2 * modes_x, modes_z), f32)),
        in_specs=[smem, smem, smem, vmem, vmem, vmem, vmem, any_spec],
        out_specs=(any_spec, vmem),
        scratch_shapes=[
            pltpu.VMEM((slots * tiles + 144, 128), f32),
            pltpu.VMEM((slots * tiles + 144, 128), f32),
            pltpu.VMEM((own, 2, modes_x, modes_z), f32),
            dma((4,)),
        ],
        compiler_params=pltpu.CompilerParams(vmem_limit_bytes=40 * 1024 * 1024),
        name="flux",
    )(
        live,
        block_count,
        block_order,
        gather_0.reshape(tiles * 8, 128),
        gather_1.reshape(tiles * 8, 128),
        jnp.asarray(mode_weights(planes, modes_z)),
        amplitude.reshape(own, 2 * modes_x, modes_z),
        staged,
    )
    return psi_next.reshape(psi_now.shape), amplitude_next.reshape(amplitude.shape)


def solution(mesh):
    return jax.shard_map(
        shards,
        mesh=mesh,
        in_specs=(
            P(None, None, "gy", "gx"),
            P(None, "gy", "gx"),
            P("gy", "gx", None),
            P("gy", "gx"),
            P(),
            P(),
            P(("gx", "gy"), None, None, None),
        ),
        out_specs=(P(None, None, "gy", "gx"), P(("gx", "gy"), None, None, None)),
        check_vma=False,
    )
```

```python
import functools
import math

import jax
import jax.numpy as jnp
import numpy as np
from jax import lax
from jax.experimental import pallas as pl
from jax.experimental.pallas import tpu as pltpu
from jax.sharding import PartitionSpec as P

spacing = 0.2
kinetic = 12.5
step_dt = 0.016
half_dt = 0.008
start_time = 100.0
later_time = start_time + step_dt
field_peak = 0.05
field_freq = 0.057
k_span = 4.0
flux_weight = 0.0078125
MESH = pl.DeviceIdType.MESH
f32 = jnp.float32


def field_at(moment):
    return field_peak * math.sin(field_freq * moment)


def drift_at(moment):
    return field_peak / (field_freq * field_freq) * math.sin(field_freq * moment)


def mode_weights(planes, modes):
    wave = ((np.arange(modes) - 0.5 * (modes - 1)) * (k_span / modes)).astype(np.float32)
    height = np.float32(spacing) * (np.arange(planes) - 0.5 * (planes - 1)).astype(np.float32)
    out = np.zeros((2, 4 * planes, 4 * modes), np.float32)
    for t, moment in enumerate((start_time, later_time)):
        phase = (
            np.float32(0.5) * wave * wave * np.float32(moment) + wave * np.float32(drift_at(moment))
        )[None, :] - wave[None, :] * height[:, None]
        cos = np.cos(phase.astype(np.float64)).astype(np.float32)
        sin = np.sin(phase.astype(np.float64)).astype(np.float32)
        block = np.block([[cos, sin], [-sin, cos]])
        out[t, : 2 * planes, : 2 * modes] = block
        out[t, 2 * planes :, 2 * modes :] = block
    return out


def iota(shape, dim):
    return lax.broadcasted_iota(jnp.int32, shape, dim)


def step_kernel(
    x_count,
    y_count,
    cells_ref,
    count_ref,
    psi_hbm,
    pot_hbm,
    next_hbm,
    gather_0,
    gather_1,
    live_ref,
    psi_v,
    sec_v,
    pot_v,
    row_msg,
    row_got,
    col_msg,
    col_got,
    corner_got,
    ghost,
    load_sem,
    store_sem,
    row_send,
    row_recv,
    col_send,
    col_recv,
    corner_send,
    corner_recv,
    x_send,
    x_recv,
    y_send,
    y_recv,
):
    gx = lax.axis_index("gx")
    gy = lax.axis_index("gy")
    parts, rows, cols = psi_hbm.shape
    planes = parts // 2
    blocks = rows // 8
    lane_blocks = cols // 128
    top = 8

    def wrap(value, count):
        return lax.rem(value + count, count)

    west, east = wrap(gx - 1, x_count), wrap(gx + 1, x_count)
    north, south = wrap(gy - 1, y_count), wrap(gy + 1, y_count)
    loads = []
    for j in range(lane_blocks):
        sl = slice(128 * j, 128 * j + 128)
        loads.append(
            pltpu.make_async_copy(
                psi_hbm.at[:, :, sl], psi_v.at[j, :, top : top + rows, :], load_sem.at[0, j]
            )
        )
        loads.append(pltpu.make_async_copy(pot_hbm.at[:, :, sl], pot_v.at[j], load_sem.at[1, j]))
    for copy in loads:
        copy.start()

    barrier = pltpu.get_barrier_semaphore()
    partner = gx + 1 - 2 * lax.rem(gx, 2)
    column = lax.rem(gx, 2)
    chip = gx // 2
    chips = x_count // 2
    signals = 0
    for k in range(1, chips):
        pl.semaphore_signal(
            barrier, inc=1, device_id=(wrap(gx + 2 * k, x_count), gy), device_id_type=MESH
        )
        signals += 1
    for k in range(1, y_count):
        pl.semaphore_signal(barrier, inc=1, device_id=(gx, wrap(gy + k, y_count)), device_id_type=MESH)
        signals += 1
    for sx in (west, east):
        for sy in (north, gy, south):
            pl.semaphore_signal(barrier, inc=1, device_id=(sx, sy), device_id_type=MESH)
            signals += 1

    for copy in loads:
        copy.wait()

    for side, (near, far) in enumerate(((top, top + 1), (top + rows - 1, top + rows - 2))):
        for j in range(lane_blocks):
            sl = slice(128 * j, 128 * j + 128)
            for p in range(parts):
                row_msg[side, p : p + 1, sl] = psi_v[j, p, near : near + 1, :]
                row_msg[side, parts + p : parts + p + 1, sl] = psi_v[j, p, far : far + 1, :]
            for z in range(planes):
                row_msg[side, 2 * parts + z : 2 * parts + z + 1, sl] = pot_v[
                    j, z, near - top : near - top + 1, :
                ]

    lane8 = iota((8, 128), 1)
    sub8 = iota((8, 128), 0)

    def pack(b, carry):
        r0 = pl.multiple_of(b * 8, 8)
        for side in range(2):
            j = 0 if side == 0 else lane_blocks - 1
            base = 0 if side == 0 else 2
            packed = jnp.zeros((8, 128), f32)
            for p in range(parts):
                block = psi_v[j, p, pl.ds(r0 + top, 8), :]
                packed = jnp.where(lane8 // 2 == p, pltpu.roll(block, (2 * p + base) % 128, 1), packed)
            for z in range(planes):
                block = pot_v[j, z, pl.ds(r0, 8), :]
                packed = jnp.where(
                    lane8 // 2 == 32 + z, pltpu.roll(block, (64 + 2 * z + base) % 128, 1), packed
                )
            col_msg[side, pl.ds(r0, 8), :] = packed
        return carry

    lax.fori_loop(0, blocks, pack, 0, unroll=2)

    pl.semaphore_wait(barrier, signals)

    halo = []
    for side, target in enumerate((north, south)):
        halo.append(
            pltpu.make_async_remote_copy(
                src_ref=row_msg.at[side],
                dst_ref=row_got.at[1 - side],
                send_sem=row_send.at[side],
                recv_sem=row_recv.at[1 - side],
                device_id=(gx, target),
                device_id_type=MESH,
            )
        )
    for side, target in enumerate((west, east)):
        halo.append(
            pltpu.make_async_remote_copy(
                src_ref=col_msg.at[side],
                dst_ref=col_got.at[1 - side],
                send_sem=col_send.at[side],
                recv_sem=col_recv.at[1 - side],
                device_id=(target, gy),
                device_id_type=MESH,
            )
        )
    for sy, ty in enumerate((north, south)):
        for sx, tx in enumerate((west, east)):
            lo = 0 if sx == 0 else cols - 128
            halo.append(
                pltpu.make_async_remote_copy(
                    src_ref=row_msg.at[sy, 0:parts, lo : lo + 128],
                    dst_ref=corner_got.at[2 * (1 - sy) + 1 - sx],
                    send_sem=corner_send.at[2 * sy + sx],
                    recv_sem=corner_recv.at[2 * (1 - sy) + 1 - sx],
                    device_id=(tx, ty),
                    device_id_type=MESH,
                )
            )
    for copy in halo:
        copy.start()

    lane_p = iota((parts, 128), 1)

    def take(slot, carry):
        out_u, out_d = carry
        cell = cells_ref[slot]
        y = cell // cols
        x = cell - y * cols
        alive = jnp.where(slot < count_ref[0], 1.0, 0.0).astype(f32)
        px = jnp.full((1, 128), spacing * ((gx * cols + x).astype(f32) - (0.5 * cols * x_count - 0.5)), f32)
        py = jnp.full((1, 128), spacing * ((gy * rows + y).astype(f32) - (0.5 * rows * y_count - 0.5)), f32)
        radius = jnp.sqrt(px * px + py * py)
        weight_x = px / radius / (2.0 * spacing) * alive
        weight_y = py / radius / (2.0 * spacing) * alive
        total_u = jnp.zeros((parts, 128), f32)
        total_d = jnp.zeros((parts, 128), f32)
        for j in range(lane_blocks):
            lane = iota((1, 128), 1) + 128 * j
            at = jnp.where(lane == x, alive, 0.0)
            along = jnp.where(lane == x + 1, weight_x, 0.0) - jnp.where(lane == x - 1, weight_x, 0.0)
            across = jnp.where(lane == x, weight_y, 0.0)
            flat = psi_v.at[j].reshape(parts * (rows + 16), 128)
            middle = flat[pl.ds(y + top, parts, stride=rows + 16), :]
            after = flat[pl.ds(y + top + 1, parts, stride=rows + 16), :]
            before = flat[pl.ds(y + top - 1, parts, stride=rows + 16), :]
            total_u = total_u + middle * at
            total_d = total_d + (middle * along + (after - before) * across)
        out_u = jnp.where(lane_p == slot, jnp.sum(total_u, axis=1, keepdims=True), out_u)
        out_d = jnp.where(lane_p == slot, jnp.sum(total_d, axis=1, keepdims=True), out_d)
        return out_u, out_d

    slots = cells_ref.shape[0]

    half_kin = half_dt * kinetic

    def swap_parts(value):
        return jnp.concatenate([value[planes:], -value[:planes]], axis=0)

    sub_p = lax.rem(iota((parts, 128), 0), planes)
    hit_w = lane_p == 2 * iota((parts, 128), 0) + 1
    hit_e = lane_p == 2 * iota((parts, 128), 0)

    def take_next(slot, carry):
        out_u, out_d = carry
        cell = cells_ref[slot]
        row = cell // cols
        x = cell - row * cols
        y = jnp.maximum(row, 1)
        alive = jnp.where(slot < count_ref[0], 1.0, 0.0).astype(f32)
        px = jnp.full((1, 128), spacing * ((gx * cols + x).astype(f32) - (0.5 * cols * x_count - 0.5)), f32)
        py = jnp.full((1, 128), spacing * ((gy * rows + y).astype(f32) - (0.5 * rows * y_count - 0.5)), f32)
        radius = jnp.sqrt(px * px + py * py)
        weight_x = px / radius / (2.0 * spacing) * alive
        weight_y = py / radius / (2.0 * spacing) * alive
        shift = half_dt * (
            field_2 * (spacing * (sub_p.astype(f32) - 0.5 * (planes - 1))) + 6.0 * kinetic
        )
        zero = jnp.zeros((parts, 128), f32)
        mean = [zero, zero]
        plain = [zero, zero]
        scaled = [zero, zero]
        around = [zero, zero]
        for j in range(lane_blocks):
            lane = iota((1, 128), 1) + 128 * j
            at = jnp.where(lane == x, alive, 0.0)
            at_side = jnp.where((lane == x + 1) | (lane == x - 1), alive, 0.0)
            along = jnp.where(lane == x + 1, weight_x, 0.0) - jnp.where(lane == x - 1, weight_x, 0.0)
            along_side = jnp.where(lane == x + 2, weight_x, 0.0) - jnp.where(
                lane == x - 2, weight_x, 0.0
            )
            across = jnp.where(lane == x, weight_y, 0.0)
            across_side = jnp.where((lane == x + 1) | (lane == x - 1), weight_y, 0.0)
            flat_s = sec_v.at[j].reshape(parts * (rows + 16), 128)
            flat_f = psi_v.at[j].reshape(parts * (rows + 16), 128)
            flat_p = pot_v.at[j].reshape(planes * rows, 128)
            sec = [flat_s[pl.ds(y + top + r, parts, stride=rows + 16), :] for r in range(-2, 3)]
            psi = [flat_f[pl.ds(y + top + r, parts, stride=rows + 16), :] for r in range(-1, 2)]
            pot = [flat_p[pl.ds(y + r, planes, stride=rows), :] for r in range(-1, 2)]
            coeff = [jnp.concatenate([v, v], axis=0) * half_dt + shift for v in pot]
            mean[0] = mean[0] + (0.5 * at) * (psi[1] + sec[2])
            plain[0] = plain[0] + at * sec[2]
            scaled[0] = scaled[0] + at * (coeff[1] * sec[2])
            around[0] = around[0] + (at * (sec[1] + sec[3]) + at_side * sec[2])
            mean[1] = mean[1] + 0.5 * (
                along * (psi[1] + sec[2]) + across * ((psi[2] + sec[3]) - (psi[0] + sec[1]))
            )
            plain[1] = plain[1] + (along * sec[2] + across * (sec[3] - sec[1]))
            scaled[1] = scaled[1] + (
                along * (coeff[1] * sec[2]) + across * (coeff[2] * sec[3] - coeff[0] * sec[1])
            )
            around[1] = around[1] + (
                (along * (sec[1] + sec[3]) + across * (sec[4] - sec[0]))
                + (along_side * sec[2] + across_side * (sec[3] - sec[1]))
            )
        row_w = ghost[1, 0, pl.ds(y, 1), :] * jnp.where(x == 1, -weight_x, 0.0)
        row_e = ghost[1, 1, pl.ds(y, 1), :] * jnp.where(x == cols - 2, weight_x, 0.0)
        around[1] = around[1] + (jnp.where(hit_w, row_w, 0.0) + jnp.where(hit_e, row_e, 0.0))
        sums = []
        for i in range(2):
            below = jnp.where(sub_p == 0, 0.0, pltpu.roll(plain[i], 1, 0))
            above = jnp.where(sub_p == planes - 1, 0.0, pltpu.roll(plain[i], parts - 1, 0))
            move = scaled[i] - half_kin * (around[i] + (below + above))
            sums.append(jnp.sum(mean[i] + swap_parts(move), axis=1, keepdims=True))
        return jnp.where(lane_p == slot, sums[0], out_u), jnp.where(lane_p == slot, sums[1], out_d)

    def surface(target, is_now):
        zero = jnp.zeros((parts, 128), f32)
        out_u, out_d = lax.fori_loop(
            0, slots, take if is_now else take_next, (zero, zero), unroll=4 if is_now else 2
        )
        turned = jnp.transpose(
            jnp.concatenate([out_u, out_d, jnp.zeros((128 - 2 * parts, 128), f32)], axis=0)
        )
        packed = jnp.where(lane8 < 64, turned[0:8], pltpu.roll(turned[8:16], 64, 1))
        if is_now:
            for slot in range(slots):
                cell = cells_ref[slot]
                y = cell // cols
                x = cell - y * cols
                px = spacing * ((gx * cols + x).astype(f32) - (0.5 * cols * x_count - 0.5))
                py = spacing * ((gy * rows + y).astype(f32) - (0.5 * rows * y_count - 0.5))
                base = 64 * (slot // 8) + 2 * parts
                row = sub8 == slot % 8
                packed = jnp.where(row & (lane8 == base), px, packed)
                packed = jnp.where(row & (lane8 == base + 1), py, packed)
            packed = jnp.where(lane8 == 2 * parts + 2, count_ref[0].astype(f32), packed)
        target[column, gy, chip] = packed

    def chip_copy(buf, phase, k, source):
        return pltpu.make_async_remote_copy(
            src_ref=buf.at[column, gy, source],
            dst_ref=buf.at[column, gy, source],
            send_sem=x_send.at[phase, k],
            recv_sem=x_recv.at[phase, k],
            device_id=(wrap(gx + 2 * k, x_count), gy),
            device_id_type=MESH,
        )

    def y_copy(buf, phase, k, source):
        return pltpu.make_async_remote_copy(
            src_ref=buf.at[column, source],
            dst_ref=buf.at[column, source],
            send_sem=y_send.at[phase, k],
            recv_sem=y_recv.at[phase, k],
            device_id=(gx, wrap(gy + k, y_count)),
            device_id_type=MESH,
        )

    def pair_copy(buf, phase, which):
        return pltpu.make_async_remote_copy(
            src_ref=buf.at[which],
            dst_ref=buf.at[which],
            send_sem=x_send.at[phase, 0],
            recv_sem=x_recv.at[phase, 0],
            device_id=(partner, gy),
            device_id_type=MESH,
        )

    def hop_1(buf, phase):
        for k in range(1, chips):
            chip_copy(buf, phase, k, chip).start()

    def hop_2(buf, phase):
        for k in range(1, chips):
            chip_copy(buf, phase, k, wrap(chip - k, chips)).wait_recv()
        for k in range(1, y_count):
            y_copy(buf, phase, k, gy).start()

    def hop_3(buf, phase):
        for k in range(1, y_count):
            y_copy(buf, phase, k, wrap(gy - k, y_count)).wait_recv()
        pair_copy(buf, phase, column).start()

    def hop_end(buf, phase):
        pair_copy(buf, phase, 1 - column).wait_recv()

    def sends_wait(buf, phase):
        for k in range(1, chips):
            chip_copy(buf, phase, k, chip).wait_send()
        for k in range(1, y_count):
            y_copy(buf, phase, k, gy).wait_send()
        pair_copy(buf, phase, column).wait_send()

    field_1 = field_at(start_time)
    field_2 = field_at(later_time)
    first = lane8 == 0
    last = lane8 == 127

    def edges(stage, p, b):
        at = pl.ds(pl.multiple_of(b * 8, 8), 8)
        edge_w = pltpu.roll(ghost[stage, 0, at, :], (128 - (2 * p + 1)) % 128, 1)
        edge_e = pltpu.roll(ghost[stage, 1, at, :], (127 - 2 * p) % 128, 1)
        return edge_w, edge_e

    def spread(src, p, r0, stage, b):
        rows_b = pl.ds(r0, 8)
        cur = [src[j, p, rows_b, :] for j in range(lane_blocks)]
        right = [pltpu.roll(c, 1, 1) for c in cur]
        left = [pltpu.roll(c, 127, 1) for c in cur]
        if stage == 0:
            edge_w = edge_e = 0.0
        else:
            edge_w, edge_e = edges(1, p, b)
        out = []
        for j in range(lane_blocks):
            up = src[j, p, pl.ds(r0 - 1, 8), :]
            down = src[j, p, pl.ds(r0 + 1, 8), :]
            w = jnp.where(first, edge_w if j == 0 else right[j - 1], right[j])
            e = jnp.where(last, edge_e if j == lane_blocks - 1 else left[j + 1], left[j])
            out.append((up + down) + (w + e))
        return cur, out

    def stage_block(src, stage, b, finish):
        r0 = pl.multiple_of(b * 8 + top, 8)
        rows_b = pl.ds(r0, 8)
        dt = step_dt if stage == 0 else half_dt
        field = field_1 if stage == 0 else field_2
        for z in range(planes):
            found = [spread(src, part * planes + z, r0, stage, b) for part in range(2)]
            shift = dt * (field * spacing * (z - 0.5 * (planes - 1)) + 6.0 * kinetic)
            for j in range(lane_blocks):
                coeff = dt * pot_v[j, z, pl.ds(pl.multiple_of(b * 8, 8), 8), :] + shift
                moves = []
                for part in range(2):
                    cur, beside = found[part]
                    p = part * planes + z
                    total = beside[j]
                    if z > 0:
                        total = total + src[j, p - 1, rows_b, :]
                    if z < planes - 1:
                        total = total + src[j, p + 1, rows_b, :]
                    moves.append(coeff * cur[j] - (dt * kinetic) * total)
                finish(z, rows_b, j, found[0][0][j], found[1][0][j], moves)

    def finish_section(z, rows_b, j, real, imag, moves):
        sec_v[j, z, rows_b, :] = real + moves[1]
        sec_v[j, planes + z, rows_b, :] = imag - moves[0]

    def finish_next(z, rows_b, j, real, imag, moves):
        psi_v[j, z, rows_b, :] = 0.5 * (psi_v[j, z, rows_b, :] + real) + moves[1]
        psi_v[j, planes + z, rows_b, :] = 0.5 * (psi_v[j, planes + z, rows_b, :] + imag) - moves[0]

    def run_section(b, carry):
        stage_block(psi_v, 0, b, finish_section)
        return carry

    def run_next(b, carry):
        stage_block(sec_v, 1, b, finish_next)
        return carry

    def fix_columns(b, carry):
        rows_b = pl.ds(pl.multiple_of(b * 8 + top, 8), 8)
        for p in range(parts):
            edge_w, edge_e = edges(0, p, b)
            other = (p + planes) % parts
            scale = step_dt * kinetic if p < planes else -step_dt * kinetic
            sec_v[0, other, rows_b, :] += jnp.where(first, scale * edge_w, 0.0)
            sec_v[lane_blocks - 1, other, rows_b, :] += jnp.where(last, scale * edge_e, 0.0)
        return carry

    surface(gather_0, True)
    hop_1(gather_0, 0)
    clear = jnp.zeros((1, 128), f32)
    for j in range(lane_blocks):
        for p in range(parts):
            psi_v[j, p, top - 1 : top, :] = clear
            psi_v[j, p, top + rows : top + rows + 1, :] = clear
    lax.fori_loop(0, blocks, run_section, 0)
    hop_2(gather_0, 0)

    for copy in halo:
        copy.wait_recv()

    keep_n = jnp.where(gy > 0, 1.0, 0.0).astype(f32)
    keep_s = jnp.where(gy < y_count - 1, 1.0, 0.0).astype(f32)
    keep_w = jnp.where(gx > 0, 1.0, 0.0).astype(f32)
    keep_e = jnp.where(gx < x_count - 1, 1.0, 0.0).astype(f32)

    def height(index):
        return spacing * (index.astype(f32) - 0.5 * (planes - 1))

    corner_cols = []
    for sy, keep_y in enumerate((keep_n, keep_s)):
        for sx, keep_x in enumerate((keep_w, keep_e)):
            lane = 127 if sx == 0 else 0
            corner_cols.append(corner_got[2 * sy + sx][:, lane : lane + 1] * (keep_y * keep_x))
    lane_row = iota((planes, cols), 1)
    sub_row = iota((planes, cols), 0)
    for side, keep in enumerate((keep_n, keep_s)):
        coeff = step_dt * (
            row_got[side, 2 * parts : 2 * parts + planes, :] + field_1 * height(sub_row) + 6.0 * kinetic
        )
        nears = []
        moves = []
        for part in range(2):
            sl = slice(part * planes, (part + 1) * planes)
            near = row_got[side, sl, :] * keep
            far = row_got[side, parts + part * planes : parts + (part + 1) * planes, :] * keep
            own = row_msg[side, sl, :]
            left = jnp.where(lane_row == 0, corner_cols[2 * side][sl], pltpu.roll(near, 1, 1))
            right = jnp.where(lane_row == cols - 1, corner_cols[2 * side + 1][sl], pltpu.roll(near, cols - 1, 1))
            below = jnp.where(sub_row == 0, 0.0, pltpu.roll(near, 1, 0))
            above = jnp.where(sub_row == planes - 1, 0.0, pltpu.roll(near, planes - 1, 0))
            beside = (far + own) + (left + right) + (below + above)
            nears.append(near)
            moves.append(coeff * near - (step_dt * kinetic) * beside)
        ghost_rows = (nears[0] + moves[1]) * keep, (nears[1] - moves[0]) * keep
        at = top - 1 if side == 0 else top + rows
        edge = top if side == 0 else top + rows - 1
        for part in range(2):
            for z in range(planes):
                for j in range(lane_blocks):
                    sl = slice(128 * j, 128 * j + 128)
                    p = part * planes + z
                    sec_v[j, p, at : at + 1, :] = ghost_rows[part][z : z + 1, sl]
                    share = (step_dt * kinetic) * nears[1 - part][z : z + 1, sl]
                    old = sec_v[j, p, edge : edge + 1, :]
                    sec_v[j, p, edge : edge + 1, :] = old - share if part == 0 else old + share

    lane_c = iota((rows, 128), 1)
    sub_c = iota((rows, 128), 0)
    diag_lane = iota((parts, 128), 1)
    diag_sub = iota((parts, 128), 0)
    plane_c = (lane_c % (2 * planes)) // 2
    for side, keep in enumerate((keep_w, keep_e)):
        got = col_got[side] * keep
        mine = col_msg[side]
        inner = 1 if side == 0 else 127
        odd = 1 if side == 0 else 0
        hit = diag_lane == 2 * diag_sub + odd
        ends = [
            jnp.sum(jnp.where(hit, corner_cols[2 * sy + side], 0.0), axis=0, keepdims=True)
            for sy in range(2)
        ]
        upper = jnp.where(sub_c == 0, ends[0], pltpu.roll(got, 1, 0))
        lower = jnp.where(sub_c == rows - 1, ends[1], pltpu.roll(got, rows - 1, 0))
        below = jnp.where(plane_c == 0, 0.0, pltpu.roll(got, 2, 1))
        above = jnp.where(plane_c == planes - 1, 0.0, pltpu.roll(got, 126, 1))
        beside = (
            (pltpu.roll(got, inner, 1) + pltpu.roll(mine, inner, 1)) + (upper + lower) + (below + above)
        )
        volts = pltpu.roll(got, 64, 1)
        volts = jnp.where(lane_c < 2 * planes, volts, pltpu.roll(volts, 2 * planes, 1))
        coeff = step_dt * (volts + field_1 * height(plane_c) + 6.0 * kinetic)
        move = coeff * got - (step_dt * kinetic) * beside
        ghost[0, side] = got
        ghost[1, side] = (
            got
            + jnp.where(
                lane_c < 2 * planes, pltpu.roll(move, 128 - 2 * planes, 1), -pltpu.roll(move, 2 * planes, 1)
            )
        ) * keep

    lax.fori_loop(0, blocks, fix_columns, 0, unroll=2)
    surface(gather_1, False)
    hop_1(gather_1, 1)
    stores = []
    pieces = 4
    per = blocks // pieces
    for q in range(pieces):
        lax.fori_loop(q * per, (q + 1) * per, run_next, 0)
        for j in range(lane_blocks):
            stores.append(
                pltpu.make_async_copy(
                    psi_v.at[j, :, top + 8 * per * q : top + 8 * per * (q + 1), :],
                    next_hbm.at[:, 8 * per * q : 8 * per * (q + 1), 128 * j : 128 * j + 128],
                    store_sem.at[q, j],
                )
            )
            stores[-1].start()
        if q == 0:
            hop_2(gather_1, 1)
            hop_3(gather_0, 0)
    hop_end(gather_0, 0)

    def count_row(i, total):
        for k in range(x_count):
            got = gather_0[i // (y_count // 2), lax.rem(i, y_count // 2) * 2 + k // chips, k % chips]
            total = jnp.where(lane8 == i * x_count + k, got[:, 2 * parts + 2 : 2 * parts + 3], total)
        return total

    live_ref[...] = lax.fori_loop(0, y_count, count_row, jnp.zeros((8, 128), f32))
    hop_3(gather_1, 1)
    for copy in halo:
        copy.wait_send()
    for copy in stores:
        copy.wait()
    hop_end(gather_1, 1)
    sends_wait(gather_0, 0)
    sends_wait(gather_1, 1)


def turns(phase):
    quarter = jnp.floor(phase * 0.6366197723675814 + 0.5)
    rest = phase - quarter * 1.5703125
    rest = rest - quarter * 4.83751296997e-4
    rest = rest - quarter * 7.5497899548918821e-8
    square = rest * rest
    sine = rest + rest * square * (
        -1.6666654611e-1 + square * (8.3321608736e-3 + square * -1.9515295891e-4)
    )
    cosine = (
        1.0
        - 0.5 * square
        + square * square * (4.166664568298827e-2 + square * (-1.388731625493765e-3 + square * 2.443315711809948e-5))
    )
    which = quarter.astype(jnp.int32)
    swap = (which & 1) == 1
    sin_out = jnp.where(swap, cosine, sine)
    cos_out = jnp.where(swap, sine, cosine)
    sin_out = jnp.where((which & 2) == 2, -sin_out, sin_out)
    cos_out = jnp.where(((which + 1) & 2) == 2, -cos_out, cos_out)
    return cos_out, sin_out


def flux_kernel(
    x_count,
    y_count,
    live_ref,
    count_ref,
    order_ref,
    gather_0,
    gather_1,
    weight_ref,
    amp_ref,
    tmp_hbm,
    next_hbm,
    out_ref,
    comp_0,
    comp_1,
    total,
    copy_sem,
):
    copies = []
    parts = tmp_hbm.shape[0]
    quarter = parts // 4
    for q in range(4):
        sl = slice(q * quarter, (q + 1) * quarter)
        copies.append(pltpu.make_async_copy(tmp_hbm.at[sl], next_hbm.at[sl], copy_sem.at[q]))
        copies[-1].start()
    me = lax.axis_index("gx") * y_count + lax.axis_index("gy")
    groups = count_ref.shape[0]
    slots = amp_ref.shape[0]
    features = weight_ref.shape[1]

    def offset(i, at):
        return at + jnp.where(i < me, count_ref[i], 0)

    own_start = lax.fori_loop(0, groups, offset, 0, unroll=8)
    own_count = count_ref[me]
    waves = []
    for s in range(slots):
        plane = order_ref[jnp.minimum(own_start + s, groups - 1)]
        waves.append((plane.astype(f32) - 0.5 * (groups - 1)) * (k_span / groups))

    def gather_tile(t, n):
        c = live_ref[0, t]
        at = pl.ds(pl.multiple_of(t * 8, 8), 8)
        block_0, block_1 = gather_0[at, :], gather_1[at, :]
        to = pl.ds(pl.multiple_of(n * 8, 8), 8)
        comp_0[to, :] = block_0
        comp_1[to, :] = block_1
        n = n + jnp.where(c > 0.5, 1, 0)
        to = pl.ds(pl.multiple_of(n * 8, 8), 8)
        comp_0[to, :] = pltpu.roll(block_0, 64, 1)
        comp_1[to, :] = pltpu.roll(block_1, 64, 1)
        return n + jnp.where(c > 8.5, 1, 0)

    live = lax.fori_loop(0, x_count * y_count, gather_tile, 0, unroll=8)

    def clear(i, carry):
        to = pl.ds(pl.multiple_of((live + i) * 8, 8), 8)
        comp_0[to, :] = jnp.zeros((8, 128), f32)
        comp_1[to, :] = jnp.zeros((8, 128), f32)
        return carry

    lax.fori_loop(0, 16, clear, 0)
    total[...] = jnp.zeros_like(total)
    kx = (iota((128, 128), 0).astype(f32) - 63.5) * (k_span / 128)
    sub8 = iota((8, 128), 0)
    ky = jnp.zeros((8, 128), f32)
    for s in range(slots):
        ky = jnp.where(sub8 // 2 == s, waves[s], ky)
    moment8 = jnp.where(sub8 % 2 == 0, start_time, later_time).astype(f32)

    def chunk(c, carry):
        at = pl.ds(pl.multiple_of(c * 128, 128), 128)
        rows = (comp_0[at, :], comp_1[at, :])
        place = jnp.transpose(rows[0])
        px, py = place[features : features + 1, :], place[features + 1 : features + 2, :]
        col_x, col_y = rows[0][:, features : features + 1], rows[0][:, features + 1 : features + 2]
        square = col_x * col_x + col_y * col_y
        radius = jnp.sqrt(jnp.where(square > 0.0, square, 1.0))
        nx, ny = col_x / radius, col_y / radius
        right = []
        left = []
        for t, moment in enumerate((start_time, later_time)):
            modes = jnp.dot(
                rows[t][:, :features],
                weight_ref[t],
                precision=lax.Precision.HIGHEST,
                preferred_element_type=f32,
            )
            ur, ui, dr, di = (modes[:, 128 * i : 128 * i + 128] for i in range(4))
            right.append(
                jnp.concatenate([nx * ur, ny * ur, dr, nx * ui, ny * ui, di], axis=1).astype(jnp.bfloat16)
            )
            left.append(turns(0.5 * kx * kx * moment - kx * px))
        right = jnp.concatenate(right, axis=0)
        rot_cos, rot_sin = turns(0.5 * ky * ky * moment8 - ky * py)

        for s in range(slots):

            @pl.when(s < own_count)
            def _():
                real = []
                imag = []
                for t in range(2):
                    bc, bs = rot_cos[2 * s + t : 2 * s + t + 1], rot_sin[2 * s + t : 2 * s + t + 1]
                    ac, as_ = left[t]
                    real.append((ac * bc - as_ * bs).astype(jnp.bfloat16))
                    imag.append((ac * bs + as_ * bc).astype(jnp.bfloat16))
                q = jnp.concatenate(
                    [jnp.concatenate(real, axis=1), jnp.concatenate(imag, axis=1)], axis=0
                )
                prod = jnp.dot(q, right, preferred_element_type=f32)
                m = [prod[:128, 128 * i : 128 * i + 128] for i in range(6)]
                w = [prod[128:, 128 * i : 128 * i + 128] for i in range(6)]
                hy = waves[s]
                total[s, 0] += kx * (m[0] - w[3]) + hy * (m[1] - w[4]) + (m[5] + w[2])
                total[s, 1] += kx * (m[3] + w[0]) + hy * (m[4] + w[1]) - (m[2] - w[5])

        return carry

    lax.fori_loop(0, (live + 15) // 16, chunk, 0)
    for s in range(slots):
        for part in range(2):
            sl = pl.ds(part, 128, stride=2)
            inc = jnp.where(s < own_count, (0.5 * flux_weight) * total[s, part], 0.0)
            out_ref[s, sl, :] = amp_ref[s, sl, :] + inc
    for copy in copies:
        copy.wait()


def shards(psi_now, potential, surf_cells, surf_count, block_count, block_order, amplitude):
    x_count = lax.axis_size("gx")
    y_count = lax.axis_size("gy")
    planes, rows, cols = potential.shape
    parts = 2 * planes
    slots = surf_cells.shape[2]
    own, modes_x, _, modes_z = amplitude.shape
    any_spec = pl.BlockSpec(memory_space=pl.ANY)
    vmem = pl.BlockSpec(memory_space=pltpu.VMEM)
    smem = pl.BlockSpec(memory_space=pltpu.SMEM)
    hbm = pl.BlockSpec(memory_space=pltpu.HBM)
    dma = pltpu.SemaphoreType.DMA
    gathered = jax.ShapeDtypeStruct((2, y_count, x_count // 2, 8, 128), f32)
    field = jax.ShapeDtypeStruct((parts, rows, cols), f32)
    staged, gather_0, gather_1, live = pl.pallas_call(
        functools.partial(step_kernel, x_count, y_count),
        out_shape=(field, gathered, gathered, jax.ShapeDtypeStruct((8, 128), f32)),
        in_specs=[smem, smem, hbm, hbm],
        out_specs=(any_spec, vmem, vmem, vmem),
        scratch_shapes=[
            pltpu.VMEM((cols // 128, parts, rows + 16, 128), f32),
            pltpu.VMEM((cols // 128, parts, rows + 16, 128), f32),
            pltpu.VMEM((cols // 128, planes, rows, 128), f32),
            pltpu.VMEM((2, 2 * parts + planes, cols), f32),
            pltpu.VMEM((2, 2 * parts + planes, cols), f32),
            pltpu.VMEM((2, rows, 128), f32),
            pltpu.VMEM((2, rows, 128), f32),
            pltpu.VMEM((4, parts, 128), f32),
            pltpu.VMEM((2, 2, rows, 128), f32),
            dma((2, cols // 128)),
            dma((4, cols // 128)),
            dma((2,)),
            dma((2,)),
            dma((2,)),
            dma((2,)),
            dma((4,)),
            dma((4,)),
            dma((2, x_count)),
            dma((2, x_count)),
            dma((2, y_count)),
            dma((2, y_count)),
        ],
        compiler_params=pltpu.CompilerParams(
            collective_id=0, has_side_effects=True, vmem_limit_bytes=52 * 1024 * 1024
        ),
        name="step",
    )(
        surf_cells.reshape(slots),
        surf_count.reshape(1),
        psi_now.reshape(parts, rows, cols),
        potential,
    )
    tiles = x_count * y_count
    psi_next, amplitude_next = pl.pallas_call(
        functools.partial(flux_kernel, x_count, y_count),
        out_shape=(field, jax.ShapeDtypeStruct((own, 2 * modes_x, modes_z), f32)),
        in_specs=[smem, smem, smem, vmem, vmem, vmem, vmem, any_spec],
        out_specs=(any_spec, vmem),
        scratch_shapes=[
            pltpu.VMEM((slots * tiles + 144, 128), f32),
            pltpu.VMEM((slots * tiles + 144, 128), f32),
            pltpu.VMEM((own, 2, modes_x, modes_z), f32),
            dma((4,)),
        ],
        compiler_params=pltpu.CompilerParams(vmem_limit_bytes=52 * 1024 * 1024),
        name="flux",
    )(
        live,
        block_count,
        block_order,
        gather_0.reshape(tiles * 8, 128),
        gather_1.reshape(tiles * 8, 128),
        jnp.asarray(mode_weights(planes, modes_z)),
        amplitude.reshape(own, 2 * modes_x, modes_z),
        staged,
    )
    return psi_next.reshape(psi_now.shape), amplitude_next.reshape(amplitude.shape)


def solution(mesh):
    return jax.shard_map(
        shards,
        mesh=mesh,
        in_specs=(
            P(None, None, "gy", "gx"),
            P(None, "gy", "gx"),
            P("gy", "gx", None),
            P("gy", "gx"),
            P(),
            P(),
            P(("gx", "gy"), None, None, None),
        ),
        out_specs=(P(None, None, "gy", "gx"), P(("gx", "gy"), None, None, None)),
        check_vma=False,
    )
```

```python
import functools
import math

import jax
import jax.numpy as jnp
import numpy as np
from jax import lax
from jax.experimental import pallas as pl
from jax.experimental.pallas import tpu as pltpu
from jax.sharding import PartitionSpec as P

spacing = 0.2
kinetic = 12.5
step_dt = 0.016
half_dt = 0.008
start_time = 100.0
later_time = start_time + step_dt
field_peak = 0.05
field_freq = 0.057
k_span = 4.0
flux_weight = 0.0078125
MESH = pl.DeviceIdType.MESH
f32 = jnp.float32


def field_at(moment):
    return field_peak * math.sin(field_freq * moment)


def drift_at(moment):
    return field_peak / (field_freq * field_freq) * math.sin(field_freq * moment)


def mode_weights(planes, modes):
    wave = ((np.arange(modes) - 0.5 * (modes - 1)) * (k_span / modes)).astype(np.float32)
    height = np.float32(spacing) * (np.arange(planes) - 0.5 * (planes - 1)).astype(np.float32)
    out = np.zeros((2, 4 * planes, 4 * modes), np.float32)
    for t, moment in enumerate((start_time, later_time)):
        phase = (
            np.float32(0.5) * wave * wave * np.float32(moment) + wave * np.float32(drift_at(moment))
        )[None, :] - wave[None, :] * height[:, None]
        cos = np.cos(phase.astype(np.float64)).astype(np.float32)
        sin = np.sin(phase.astype(np.float64)).astype(np.float32)
        block = np.block([[cos, sin], [-sin, cos]])
        out[t, : 2 * planes, : 2 * modes] = block
        out[t, 2 * planes :, 2 * modes :] = block
    return out


def iota(shape, dim):
    return lax.broadcasted_iota(jnp.int32, shape, dim)


def step_kernel(
    x_count,
    y_count,
    cells_ref,
    count_ref,
    psi_hbm,
    pot_hbm,
    next_hbm,
    gather_0,
    gather_1,
    live_ref,
    psi_v,
    sec_v,
    pot_v,
    row_msg,
    row_got,
    col_msg,
    col_got,
    corner_got,
    ghost,
    load_sem,
    store_sem,
    row_send,
    row_recv,
    col_send,
    col_recv,
    corner_send,
    corner_recv,
    x_send,
    x_recv,
    y_send,
    y_recv,
):
    gx = lax.axis_index("gx")
    gy = lax.axis_index("gy")
    parts, rows, cols = psi_hbm.shape
    planes = parts // 2
    blocks = rows // 8
    lane_blocks = cols // 128
    top = 8

    def wrap(value, count):
        return lax.rem(value + count, count)

    west, east = wrap(gx - 1, x_count), wrap(gx + 1, x_count)
    north, south = wrap(gy - 1, y_count), wrap(gy + 1, y_count)
    loads = []
    for j in range(lane_blocks):
        sl = slice(128 * j, 128 * j + 128)
        loads.append(
            pltpu.make_async_copy(
                psi_hbm.at[:, :, sl], psi_v.at[j, :, top : top + rows, :], load_sem.at[0, j]
            )
        )
        loads.append(pltpu.make_async_copy(pot_hbm.at[:, :, sl], pot_v.at[j], load_sem.at[1, j]))
    for copy in loads:
        copy.start()

    barrier = pltpu.get_barrier_semaphore()
    partner = gx + 1 - 2 * lax.rem(gx, 2)
    column = lax.rem(gx, 2)
    chip = gx // 2
    chips = x_count // 2
    signals = 0
    for k in range(1, chips):
        pl.semaphore_signal(
            barrier, inc=1, device_id=(wrap(gx + 2 * k, x_count), gy), device_id_type=MESH
        )
        signals += 1
    for k in range(1, y_count):
        pl.semaphore_signal(barrier, inc=1, device_id=(gx, wrap(gy + k, y_count)), device_id_type=MESH)
        signals += 1
    for sx in (west, east):
        for sy in (north, gy, south):
            pl.semaphore_signal(barrier, inc=1, device_id=(sx, sy), device_id_type=MESH)
            signals += 1

    for copy in loads:
        copy.wait()

    for side, (near, far) in enumerate(((top, top + 1), (top + rows - 1, top + rows - 2))):
        for j in range(lane_blocks):
            sl = slice(128 * j, 128 * j + 128)
            for p in range(parts):
                row_msg[side, p : p + 1, sl] = psi_v[j, p, near : near + 1, :]
                row_msg[side, parts + p : parts + p + 1, sl] = psi_v[j, p, far : far + 1, :]
            for z in range(planes):
                row_msg[side, 2 * parts + z : 2 * parts + z + 1, sl] = pot_v[
                    j, z, near - top : near - top + 1, :
                ]

    lane8 = iota((8, 128), 1)
    sub8 = iota((8, 128), 0)

    def pack(b, carry):
        r0 = pl.multiple_of(b * 8, 8)
        for side in range(2):
            j = 0 if side == 0 else lane_blocks - 1
            base = 0 if side == 0 else 2
            packed = jnp.zeros((8, 128), f32)
            for p in range(parts):
                block = psi_v[j, p, pl.ds(r0 + top, 8), :]
                packed = jnp.where(lane8 // 2 == p, pltpu.roll(block, (2 * p + base) % 128, 1), packed)
            for z in range(planes):
                block = pot_v[j, z, pl.ds(r0, 8), :]
                packed = jnp.where(
                    lane8 // 2 == 32 + z, pltpu.roll(block, (64 + 2 * z + base) % 128, 1), packed
                )
            col_msg[side, pl.ds(r0, 8), :] = packed
        return carry

    lax.fori_loop(0, blocks, pack, 0, unroll=2)

    pl.semaphore_wait(barrier, signals)

    halo = []
    for side, target in enumerate((north, south)):
        halo.append(
            pltpu.make_async_remote_copy(
                src_ref=row_msg.at[side],
                dst_ref=row_got.at[1 - side],
                send_sem=row_send.at[side],
                recv_sem=row_recv.at[1 - side],
                device_id=(gx, target),
                device_id_type=MESH,
            )
        )
    for side, target in enumerate((west, east)):
        halo.append(
            pltpu.make_async_remote_copy(
                src_ref=col_msg.at[side],
                dst_ref=col_got.at[1 - side],
                send_sem=col_send.at[side],
                recv_sem=col_recv.at[1 - side],
                device_id=(target, gy),
                device_id_type=MESH,
            )
        )
    for sy, ty in enumerate((north, south)):
        for sx, tx in enumerate((west, east)):
            lo = 0 if sx == 0 else cols - 128
            halo.append(
                pltpu.make_async_remote_copy(
                    src_ref=row_msg.at[sy, 0:parts, lo : lo + 128],
                    dst_ref=corner_got.at[2 * (1 - sy) + 1 - sx],
                    send_sem=corner_send.at[2 * sy + sx],
                    recv_sem=corner_recv.at[2 * (1 - sy) + 1 - sx],
                    device_id=(tx, ty),
                    device_id_type=MESH,
                )
            )
    for copy in halo:
        copy.start()

    lane_p = iota((parts, 128), 1)

    def take(slot, carry):
        out_u, out_d = carry
        cell = cells_ref[slot]
        y = cell // cols
        x = cell - y * cols
        alive = jnp.where(slot < count_ref[0], 1.0, 0.0).astype(f32)
        px = jnp.full((1, 128), spacing * ((gx * cols + x).astype(f32) - (0.5 * cols * x_count - 0.5)), f32)
        py = jnp.full((1, 128), spacing * ((gy * rows + y).astype(f32) - (0.5 * rows * y_count - 0.5)), f32)
        radius = jnp.sqrt(px * px + py * py)
        weight_x = px / radius / (2.0 * spacing) * alive
        weight_y = py / radius / (2.0 * spacing) * alive
        total_u = jnp.zeros((parts, 128), f32)
        total_d = jnp.zeros((parts, 128), f32)
        for j in range(lane_blocks):
            lane = iota((1, 128), 1) + 128 * j
            at = jnp.where(lane == x, alive, 0.0)
            along = jnp.where(lane == x + 1, weight_x, 0.0) - jnp.where(lane == x - 1, weight_x, 0.0)
            across = jnp.where(lane == x, weight_y, 0.0)
            flat = psi_v.at[j].reshape(parts * (rows + 16), 128)
            middle = flat[pl.ds(y + top, parts, stride=rows + 16), :]
            after = flat[pl.ds(y + top + 1, parts, stride=rows + 16), :]
            before = flat[pl.ds(y + top - 1, parts, stride=rows + 16), :]
            total_u = total_u + middle * at
            total_d = total_d + (middle * along + (after - before) * across)
        out_u = jnp.where(lane_p == slot, jnp.sum(total_u, axis=1, keepdims=True), out_u)
        out_d = jnp.where(lane_p == slot, jnp.sum(total_d, axis=1, keepdims=True), out_d)
        return out_u, out_d

    slots = cells_ref.shape[0]

    half_kin = half_dt * kinetic

    def swap_parts(value):
        return jnp.concatenate([value[planes:], -value[:planes]], axis=0)

    sub_p = lax.rem(iota((parts, 128), 0), planes)
    hit_w = lane_p == 2 * iota((parts, 128), 0) + 1
    hit_e = lane_p == 2 * iota((parts, 128), 0)

    def take_next(slot, carry):
        out_u, out_d = carry
        cell = cells_ref[slot]
        row = cell // cols
        x = cell - row * cols
        y = jnp.maximum(row, 1)
        alive = jnp.where(slot < count_ref[0], 1.0, 0.0).astype(f32)
        px = jnp.full((1, 128), spacing * ((gx * cols + x).astype(f32) - (0.5 * cols * x_count - 0.5)), f32)
        py = jnp.full((1, 128), spacing * ((gy * rows + y).astype(f32) - (0.5 * rows * y_count - 0.5)), f32)
        radius = jnp.sqrt(px * px + py * py)
        weight_x = px / radius / (2.0 * spacing) * alive
        weight_y = py / radius / (2.0 * spacing) * alive
        shift = half_dt * (
            field_2 * (spacing * (sub_p.astype(f32) - 0.5 * (planes - 1))) + 6.0 * kinetic
        )
        zero = jnp.zeros((parts, 128), f32)
        mean = [zero, zero]
        plain = [zero, zero]
        scaled = [zero, zero]
        around = [zero, zero]
        for j in range(lane_blocks):
            lane = iota((1, 128), 1) + 128 * j
            at = jnp.where(lane == x, alive, 0.0)
            at_side = jnp.where((lane == x + 1) | (lane == x - 1), alive, 0.0)
            along = jnp.where(lane == x + 1, weight_x, 0.0) - jnp.where(lane == x - 1, weight_x, 0.0)
            along_side = jnp.where(lane == x + 2, weight_x, 0.0) - jnp.where(
                lane == x - 2, weight_x, 0.0
            )
            across = jnp.where(lane == x, weight_y, 0.0)
            across_side = jnp.where((lane == x + 1) | (lane == x - 1), weight_y, 0.0)
            flat_s = sec_v.at[j].reshape(parts * (rows + 16), 128)
            flat_f = psi_v.at[j].reshape(parts * (rows + 16), 128)
            flat_p = pot_v.at[j].reshape(planes * rows, 128)
            sec = [flat_s[pl.ds(y + top + r, parts, stride=rows + 16), :] for r in range(-2, 3)]
            psi = [flat_f[pl.ds(y + top + r, parts, stride=rows + 16), :] for r in range(-1, 2)]
            pot = [flat_p[pl.ds(y + r, planes, stride=rows), :] for r in range(-1, 2)]
            coeff = [jnp.concatenate([v, v], axis=0) * half_dt + shift for v in pot]
            mean[0] = mean[0] + (0.5 * at) * (psi[1] + sec[2])
            plain[0] = plain[0] + at * sec[2]
            scaled[0] = scaled[0] + at * (coeff[1] * sec[2])
            around[0] = around[0] + (at * (sec[1] + sec[3]) + at_side * sec[2])
            mean[1] = mean[1] + 0.5 * (
                along * (psi[1] + sec[2]) + across * ((psi[2] + sec[3]) - (psi[0] + sec[1]))
            )
            plain[1] = plain[1] + (along * sec[2] + across * (sec[3] - sec[1]))
            scaled[1] = scaled[1] + (
                along * (coeff[1] * sec[2]) + across * (coeff[2] * sec[3] - coeff[0] * sec[1])
            )
            around[1] = around[1] + (
                (along * (sec[1] + sec[3]) + across * (sec[4] - sec[0]))
                + (along_side * sec[2] + across_side * (sec[3] - sec[1]))
            )
        row_w = ghost[1, 0, pl.ds(y, 1), :] * jnp.where(x == 1, -weight_x, 0.0)
        row_e = ghost[1, 1, pl.ds(y, 1), :] * jnp.where(x == cols - 2, weight_x, 0.0)
        around[1] = around[1] + (jnp.where(hit_w, row_w, 0.0) + jnp.where(hit_e, row_e, 0.0))
        sums = []
        for i in range(2):
            below = jnp.where(sub_p == 0, 0.0, pltpu.roll(plain[i], 1, 0))
            above = jnp.where(sub_p == planes - 1, 0.0, pltpu.roll(plain[i], parts - 1, 0))
            move = scaled[i] - half_kin * (around[i] + (below + above))
            sums.append(jnp.sum(mean[i] + swap_parts(move), axis=1, keepdims=True))
        return jnp.where(lane_p == slot, sums[0], out_u), jnp.where(lane_p == slot, sums[1], out_d)

    def surface(target, is_now):
        zero = jnp.zeros((parts, 128), f32)
        out_u, out_d = lax.fori_loop(
            0, slots, take if is_now else take_next, (zero, zero), unroll=4 if is_now else 2
        )
        turned = jnp.transpose(
            jnp.concatenate([out_u, out_d, jnp.zeros((128 - 2 * parts, 128), f32)], axis=0)
        )
        packed = jnp.where(lane8 < 64, turned[0:8], pltpu.roll(turned[8:16], 64, 1))
        if is_now:
            for slot in range(slots):
                cell = cells_ref[slot]
                y = cell // cols
                x = cell - y * cols
                px = spacing * ((gx * cols + x).astype(f32) - (0.5 * cols * x_count - 0.5))
                py = spacing * ((gy * rows + y).astype(f32) - (0.5 * rows * y_count - 0.5))
                base = 64 * (slot // 8) + 2 * parts
                row = sub8 == slot % 8
                packed = jnp.where(row & (lane8 == base), px, packed)
                packed = jnp.where(row & (lane8 == base + 1), py, packed)
            packed = jnp.where(lane8 == 2 * parts + 2, count_ref[0].astype(f32), packed)
        target[column, gy, chip] = packed

    def chip_copy(buf, phase, k, source):
        return pltpu.make_async_remote_copy(
            src_ref=buf.at[column, gy, source],
            dst_ref=buf.at[column, gy, source],
            send_sem=x_send.at[phase, k],
            recv_sem=x_recv.at[phase, k],
            device_id=(wrap(gx + 2 * k, x_count), gy),
            device_id_type=MESH,
        )

    def y_copy(buf, phase, k, source):
        return pltpu.make_async_remote_copy(
            src_ref=buf.at[column, source],
            dst_ref=buf.at[column, source],
            send_sem=y_send.at[phase, k],
            recv_sem=y_recv.at[phase, k],
            device_id=(gx, wrap(gy + k, y_count)),
            device_id_type=MESH,
        )

    def pair_copy(buf, phase, which):
        return pltpu.make_async_remote_copy(
            src_ref=buf.at[which],
            dst_ref=buf.at[which],
            send_sem=x_send.at[phase, 0],
            recv_sem=x_recv.at[phase, 0],
            device_id=(partner, gy),
            device_id_type=MESH,
        )

    def hop_1(buf, phase):
        for k in range(1, chips):
            chip_copy(buf, phase, k, chip).start()

    def hop_2(buf, phase):
        for k in range(1, chips):
            chip_copy(buf, phase, k, wrap(chip - k, chips)).wait_recv()
        for k in range(1, y_count):
            y_copy(buf, phase, k, gy).start()

    def hop_3(buf, phase):
        for k in range(1, y_count):
            y_copy(buf, phase, k, wrap(gy - k, y_count)).wait_recv()
        pair_copy(buf, phase, column).start()

    def hop_end(buf, phase):
        pair_copy(buf, phase, 1 - column).wait_recv()

    def sends_wait(buf, phase):
        for k in range(1, chips):
            chip_copy(buf, phase, k, chip).wait_send()
        for k in range(1, y_count):
            y_copy(buf, phase, k, gy).wait_send()
        pair_copy(buf, phase, column).wait_send()

    field_1 = field_at(start_time)
    field_2 = field_at(later_time)
    first = lane8 == 0
    last = lane8 == 127

    def edges(stage, p, b):
        at = pl.ds(pl.multiple_of(b * 8, 8), 8)
        edge_w = pltpu.roll(ghost[stage, 0, at, :], (128 - (2 * p + 1)) % 128, 1)
        edge_e = pltpu.roll(ghost[stage, 1, at, :], (127 - 2 * p) % 128, 1)
        return edge_w, edge_e

    def spread(src, p, r0, stage, b):
        rows_b = pl.ds(r0, 8)
        cur = [src[j, p, rows_b, :] for j in range(lane_blocks)]
        right = [pltpu.roll(c, 1, 1) for c in cur]
        left = [pltpu.roll(c, 127, 1) for c in cur]
        if stage == 0:
            edge_w = edge_e = 0.0
        else:
            edge_w, edge_e = edges(1, p, b)
        out = []
        for j in range(lane_blocks):
            up = src[j, p, pl.ds(r0 - 1, 8), :]
            down = src[j, p, pl.ds(r0 + 1, 8), :]
            w = jnp.where(first, edge_w if j == 0 else right[j - 1], right[j])
            e = jnp.where(last, edge_e if j == lane_blocks - 1 else left[j + 1], left[j])
            out.append((up + down) + (w + e))
        return cur, out

    def stage_block(src, stage, b, finish):
        r0 = pl.multiple_of(b * 8 + top, 8)
        rows_b = pl.ds(r0, 8)
        dt = step_dt if stage == 0 else half_dt
        field = field_1 if stage == 0 else field_2
        for z in range(planes):
            found = [spread(src, part * planes + z, r0, stage, b) for part in range(2)]
            shift = dt * (field * spacing * (z - 0.5 * (planes - 1)) + 6.0 * kinetic)
            for j in range(lane_blocks):
                coeff = dt * pot_v[j, z, pl.ds(pl.multiple_of(b * 8, 8), 8), :] + shift
                moves = []
                for part in range(2):
                    cur, beside = found[part]
                    p = part * planes + z
                    total = beside[j]
                    if z > 0:
                        total = total + src[j, p - 1, rows_b, :]
                    if z < planes - 1:
                        total = total + src[j, p + 1, rows_b, :]
                    moves.append(coeff * cur[j] - (dt * kinetic) * total)
                finish(z, rows_b, j, found[0][0][j], found[1][0][j], moves)

    def finish_section(z, rows_b, j, real, imag, moves):
        sec_v[j, z, rows_b, :] = real + moves[1]
        sec_v[j, planes + z, rows_b, :] = imag - moves[0]

    def finish_next(z, rows_b, j, real, imag, moves):
        psi_v[j, z, rows_b, :] = 0.5 * (psi_v[j, z, rows_b, :] + real) + moves[1]
        psi_v[j, planes + z, rows_b, :] = 0.5 * (psi_v[j, planes + z, rows_b, :] + imag) - moves[0]

    def run_section(b, carry):
        stage_block(psi_v, 0, b, finish_section)
        return carry

    def run_next(b, carry):
        stage_block(sec_v, 1, b, finish_next)
        return carry

    def fix_columns(b, carry):
        rows_b = pl.ds(pl.multiple_of(b * 8 + top, 8), 8)
        for p in range(parts):
            edge_w, edge_e = edges(0, p, b)
            other = (p + planes) % parts
            scale = step_dt * kinetic if p < planes else -step_dt * kinetic
            sec_v[0, other, rows_b, :] += jnp.where(first, scale * edge_w, 0.0)
            sec_v[lane_blocks - 1, other, rows_b, :] += jnp.where(last, scale * edge_e, 0.0)
        return carry

    surface(gather_0, True)
    hop_1(gather_0, 0)
    clear = jnp.zeros((1, 128), f32)
    for j in range(lane_blocks):
        for p in range(parts):
            psi_v[j, p, top - 1 : top, :] = clear
            psi_v[j, p, top + rows : top + rows + 1, :] = clear
    lax.fori_loop(0, blocks, run_section, 0)
    hop_2(gather_0, 0)

    for copy in halo:
        copy.wait_recv()

    keep_n = jnp.where(gy > 0, 1.0, 0.0).astype(f32)
    keep_s = jnp.where(gy < y_count - 1, 1.0, 0.0).astype(f32)
    keep_w = jnp.where(gx > 0, 1.0, 0.0).astype(f32)
    keep_e = jnp.where(gx < x_count - 1, 1.0, 0.0).astype(f32)

    def height(index):
        return spacing * (index.astype(f32) - 0.5 * (planes - 1))

    corner_cols = []
    for sy, keep_y in enumerate((keep_n, keep_s)):
        for sx, keep_x in enumerate((keep_w, keep_e)):
            lane = 127 if sx == 0 else 0
            corner_cols.append(corner_got[2 * sy + sx][:, lane : lane + 1] * (keep_y * keep_x))
    lane_row = iota((planes, cols), 1)
    sub_row = iota((planes, cols), 0)
    for side, keep in enumerate((keep_n, keep_s)):
        coeff = step_dt * (
            row_got[side, 2 * parts : 2 * parts + planes, :] + field_1 * height(sub_row) + 6.0 * kinetic
        )
        nears = []
        moves = []
        for part in range(2):
            sl = slice(part * planes, (part + 1) * planes)
            near = row_got[side, sl, :] * keep
            far = row_got[side, parts + part * planes : parts + (part + 1) * planes, :] * keep
            own = row_msg[side, sl, :]
            left = jnp.where(lane_row == 0, corner_cols[2 * side][sl], pltpu.roll(near, 1, 1))
            right = jnp.where(lane_row == cols - 1, corner_cols[2 * side + 1][sl], pltpu.roll(near, cols - 1, 1))
            below = jnp.where(sub_row == 0, 0.0, pltpu.roll(near, 1, 0))
            above = jnp.where(sub_row == planes - 1, 0.0, pltpu.roll(near, planes - 1, 0))
            beside = (far + own) + (left + right) + (below + above)
            nears.append(near)
            moves.append(coeff * near - (step_dt * kinetic) * beside)
        ghost_rows = (nears[0] + moves[1]) * keep, (nears[1] - moves[0]) * keep
        at = top - 1 if side == 0 else top + rows
        edge = top if side == 0 else top + rows - 1
        for part in range(2):
            for z in range(planes):
                for j in range(lane_blocks):
                    sl = slice(128 * j, 128 * j + 128)
                    p = part * planes + z
                    sec_v[j, p, at : at + 1, :] = ghost_rows[part][z : z + 1, sl]
                    share = (step_dt * kinetic) * nears[1 - part][z : z + 1, sl]
                    old = sec_v[j, p, edge : edge + 1, :]
                    sec_v[j, p, edge : edge + 1, :] = old - share if part == 0 else old + share

    lane_c = iota((rows, 128), 1)
    sub_c = iota((rows, 128), 0)
    diag_lane = iota((parts, 128), 1)
    diag_sub = iota((parts, 128), 0)
    plane_c = (lane_c % (2 * planes)) // 2
    for side, keep in enumerate((keep_w, keep_e)):
        got = col_got[side] * keep
        mine = col_msg[side]
        inner = 1 if side == 0 else 127
        odd = 1 if side == 0 else 0
        hit = diag_lane == 2 * diag_sub + odd
        ends = [
            jnp.sum(jnp.where(hit, corner_cols[2 * sy + side], 0.0), axis=0, keepdims=True)
            for sy in range(2)
        ]
        upper = jnp.where(sub_c == 0, ends[0], pltpu.roll(got, 1, 0))
        lower = jnp.where(sub_c == rows - 1, ends[1], pltpu.roll(got, rows - 1, 0))
        below = jnp.where(plane_c == 0, 0.0, pltpu.roll(got, 2, 1))
        above = jnp.where(plane_c == planes - 1, 0.0, pltpu.roll(got, 126, 1))
        beside = (
            (pltpu.roll(got, inner, 1) + pltpu.roll(mine, inner, 1)) + (upper + lower) + (below + above)
        )
        volts = pltpu.roll(got, 64, 1)
        volts = jnp.where(lane_c < 2 * planes, volts, pltpu.roll(volts, 2 * planes, 1))
        coeff = step_dt * (volts + field_1 * height(plane_c) + 6.0 * kinetic)
        move = coeff * got - (step_dt * kinetic) * beside
        ghost[0, side] = got
        ghost[1, side] = (
            got
            + jnp.where(
                lane_c < 2 * planes, pltpu.roll(move, 128 - 2 * planes, 1), -pltpu.roll(move, 2 * planes, 1)
            )
        ) * keep

    lax.fori_loop(0, blocks, fix_columns, 0, unroll=2)
    surface(gather_1, False)
    hop_1(gather_1, 1)
    stores = []
    pieces = 4
    per = blocks // pieces
    for q in range(pieces):
        lax.fori_loop(q * per, (q + 1) * per, run_next, 0)
        for j in range(lane_blocks):
            stores.append(
                pltpu.make_async_copy(
                    psi_v.at[j, :, top + 8 * per * q : top + 8 * per * (q + 1), :],
                    next_hbm.at[:, 8 * per * q : 8 * per * (q + 1), 128 * j : 128 * j + 128],
                    store_sem.at[q, j],
                )
            )
            stores[-1].start()
        if q == 0:
            hop_2(gather_1, 1)
            hop_3(gather_0, 0)
    hop_end(gather_0, 0)

    def count_row(i, total):
        for k in range(x_count):
            got = gather_0[i // (y_count // 2), lax.rem(i, y_count // 2) * 2 + k // chips, k % chips]
            total = jnp.where(lane8 == i * x_count + k, got[:, 2 * parts + 2 : 2 * parts + 3], total)
        return total

    live_ref[...] = lax.fori_loop(0, y_count, count_row, jnp.zeros((8, 128), f32))
    hop_3(gather_1, 1)
    for copy in halo:
        copy.wait_send()
    for copy in stores:
        copy.wait()
    hop_end(gather_1, 1)
    sends_wait(gather_0, 0)
    sends_wait(gather_1, 1)


def turns(phase):
    quarter = jnp.floor(phase * 0.6366197723675814 + 0.5)
    rest = phase - quarter * 1.5703125
    rest = rest - quarter * 4.83751296997e-4
    rest = rest - quarter * 7.5497899548918821e-8
    square = rest * rest
    sine = rest + rest * square * (
        -1.6666654611e-1 + square * (8.3321608736e-3 + square * -1.9515295891e-4)
    )
    cosine = (
        1.0
        - 0.5 * square
        + square * square * (4.166664568298827e-2 + square * (-1.388731625493765e-3 + square * 2.443315711809948e-5))
    )
    which = quarter.astype(jnp.int32)
    swap = (which & 1) == 1
    sin_out = jnp.where(swap, cosine, sine)
    cos_out = jnp.where(swap, sine, cosine)
    sin_out = jnp.where((which & 2) == 2, -sin_out, sin_out)
    cos_out = jnp.where(((which + 1) & 2) == 2, -cos_out, cos_out)
    return cos_out, sin_out


def flux_kernel(
    x_count,
    y_count,
    live_ref,
    count_ref,
    order_ref,
    gather_0,
    gather_1,
    weight_ref,
    amp_ref,
    tmp_hbm,
    next_hbm,
    out_ref,
    comp_0,
    comp_1,
    total,
    held,
    fetch_sem,
    copy_sem,
):
    copies = []
    parts = tmp_hbm.shape[0]
    quarter = parts // 4
    for q in range(4):
        sl = slice(q * quarter, (q + 1) * quarter)
        fetch = pltpu.make_async_copy(tmp_hbm.at[sl], held.at[sl], fetch_sem.at[q])
        fetch.start()
        copies.append((fetch, pltpu.make_async_copy(held.at[sl], next_hbm.at[sl], copy_sem.at[q])))
    me = lax.axis_index("gx") * y_count + lax.axis_index("gy")
    groups = count_ref.shape[0]
    slots = amp_ref.shape[0]
    features = weight_ref.shape[1]

    def offset(i, at):
        return at + jnp.where(i < me, count_ref[i], 0)

    own_start = lax.fori_loop(0, groups, offset, 0, unroll=8)
    own_count = count_ref[me]
    waves = []
    for s in range(slots):
        plane = order_ref[jnp.minimum(own_start + s, groups - 1)]
        waves.append((plane.astype(f32) - 0.5 * (groups - 1)) * (k_span / groups))

    def gather_tile(t, n):
        c = live_ref[0, t]
        at = pl.ds(pl.multiple_of(t * 8, 8), 8)
        block_0, block_1 = gather_0[at, :], gather_1[at, :]
        to = pl.ds(pl.multiple_of(n * 8, 8), 8)
        comp_0[to, :] = block_0
        comp_1[to, :] = block_1
        n = n + jnp.where(c > 0.5, 1, 0)
        to = pl.ds(pl.multiple_of(n * 8, 8), 8)
        comp_0[to, :] = pltpu.roll(block_0, 64, 1)
        comp_1[to, :] = pltpu.roll(block_1, 64, 1)
        return n + jnp.where(c > 8.5, 1, 0)

    live = lax.fori_loop(0, x_count * y_count, gather_tile, 0, unroll=8)

    def clear(i, carry):
        to = pl.ds(pl.multiple_of((live + i) * 8, 8), 8)
        comp_0[to, :] = jnp.zeros((8, 128), f32)
        comp_1[to, :] = jnp.zeros((8, 128), f32)
        return carry

    lax.fori_loop(0, 16, clear, 0)
    for fetch, copy in copies:
        fetch.wait()
        copy.start()
    total[...] = jnp.zeros_like(total)
    kx = (iota((128, 128), 0).astype(f32) - 63.5) * (k_span / 128)
    sub8 = iota((8, 128), 0)
    ky = jnp.zeros((8, 128), f32)
    for s in range(slots):
        ky = jnp.where(sub8 // 2 == s, waves[s], ky)
    moment8 = jnp.where(sub8 % 2 == 0, start_time, later_time).astype(f32)

    def chunk(c, carry):
        at = pl.ds(pl.multiple_of(c * 128, 128), 128)
        rows = (comp_0[at, :], comp_1[at, :])
        place = jnp.transpose(rows[0])
        px, py = place[features : features + 1, :], place[features + 1 : features + 2, :]
        col_x, col_y = rows[0][:, features : features + 1], rows[0][:, features + 1 : features + 2]
        square = col_x * col_x + col_y * col_y
        radius = jnp.sqrt(jnp.where(square > 0.0, square, 1.0))
        nx, ny = col_x / radius, col_y / radius
        right = []
        left = []
        for t, moment in enumerate((start_time, later_time)):
            modes = jnp.dot(
                rows[t][:, :features],
                weight_ref[t],
                precision=lax.Precision.HIGHEST,
                preferred_element_type=f32,
            )
            ur, ui, dr, di = (modes[:, 128 * i : 128 * i + 128] for i in range(4))
            right.append(
                jnp.concatenate([nx * ur, ny * ur, dr, nx * ui, ny * ui, di], axis=1).astype(jnp.bfloat16)
            )
            left.append(turns(0.5 * kx * kx * moment - kx * px))
        right = jnp.concatenate(right, axis=0)
        rot_cos, rot_sin = turns(0.5 * ky * ky * moment8 - ky * py)

        for s in range(slots):

            @pl.when(s < own_count)
            def _():
                real = []
                imag = []
                for t in range(2):
                    bc, bs = rot_cos[2 * s + t : 2 * s + t + 1], rot_sin[2 * s + t : 2 * s + t + 1]
                    ac, as_ = left[t]
                    real.append((ac * bc - as_ * bs).astype(jnp.bfloat16))
                    imag.append((ac * bs + as_ * bc).astype(jnp.bfloat16))
                q = jnp.concatenate(
                    [jnp.concatenate(real, axis=1), jnp.concatenate(imag, axis=1)], axis=0
                )
                prod = jnp.dot(q, right, preferred_element_type=f32)
                m = [prod[:128, 128 * i : 128 * i + 128] for i in range(6)]
                w = [prod[128:, 128 * i : 128 * i + 128] for i in range(6)]
                hy = waves[s]
                total[s, 0] += kx * (m[0] - w[3]) + hy * (m[1] - w[4]) + (m[5] + w[2])
                total[s, 1] += kx * (m[3] + w[0]) + hy * (m[4] + w[1]) - (m[2] - w[5])

        return carry

    lax.fori_loop(0, (live + 15) // 16, chunk, 0)
    for s in range(slots):
        for part in range(2):
            sl = pl.ds(part, 128, stride=2)
            inc = jnp.where(s < own_count, (0.5 * flux_weight) * total[s, part], 0.0)
            out_ref[s, sl, :] = amp_ref[s, sl, :] + inc
    for fetch, copy in copies:
        copy.wait()


def shards(psi_now, potential, surf_cells, surf_count, block_count, block_order, amplitude):
    x_count = lax.axis_size("gx")
    y_count = lax.axis_size("gy")
    planes, rows, cols = potential.shape
    parts = 2 * planes
    slots = surf_cells.shape[2]
    own, modes_x, _, modes_z = amplitude.shape
    any_spec = pl.BlockSpec(memory_space=pl.ANY)
    vmem = pl.BlockSpec(memory_space=pltpu.VMEM)
    smem = pl.BlockSpec(memory_space=pltpu.SMEM)
    hbm = pl.BlockSpec(memory_space=pltpu.HBM)
    dma = pltpu.SemaphoreType.DMA
    gathered = jax.ShapeDtypeStruct((2, y_count, x_count // 2, 8, 128), f32)
    field = jax.ShapeDtypeStruct((parts, rows, cols), f32)
    staged, gather_0, gather_1, live = pl.pallas_call(
        functools.partial(step_kernel, x_count, y_count),
        out_shape=(field, gathered, gathered, jax.ShapeDtypeStruct((8, 128), f32)),
        in_specs=[smem, smem, hbm, hbm],
        out_specs=(any_spec, vmem, vmem, vmem),
        scratch_shapes=[
            pltpu.VMEM((cols // 128, parts, rows + 16, 128), f32),
            pltpu.VMEM((cols // 128, parts, rows + 16, 128), f32),
            pltpu.VMEM((cols // 128, planes, rows, 128), f32),
            pltpu.VMEM((2, 2 * parts + planes, cols), f32),
            pltpu.VMEM((2, 2 * parts + planes, cols), f32),
            pltpu.VMEM((2, rows, 128), f32),
            pltpu.VMEM((2, rows, 128), f32),
            pltpu.VMEM((4, parts, 128), f32),
            pltpu.VMEM((2, 2, rows, 128), f32),
            dma((2, cols // 128)),
            dma((4, cols // 128)),
            dma((2,)),
            dma((2,)),
            dma((2,)),
            dma((2,)),
            dma((4,)),
            dma((4,)),
            dma((2, x_count)),
            dma((2, x_count)),
            dma((2, y_count)),
            dma((2, y_count)),
        ],
        compiler_params=pltpu.CompilerParams(
            collective_id=0, has_side_effects=True, vmem_limit_bytes=52 * 1024 * 1024
        ),
        name="step",
    )(
        surf_cells.reshape(slots),
        surf_count.reshape(1),
        psi_now.reshape(parts, rows, cols),
        potential,
    )
    tiles = x_count * y_count
    psi_next, amplitude_next = pl.pallas_call(
        functools.partial(flux_kernel, x_count, y_count),
        out_shape=(field, jax.ShapeDtypeStruct((own, 2 * modes_x, modes_z), f32)),
        in_specs=[smem, smem, smem, vmem, vmem, vmem, vmem, any_spec],
        out_specs=(any_spec, vmem),
        scratch_shapes=[
            pltpu.VMEM((slots * tiles + 144, 128), f32),
            pltpu.VMEM((slots * tiles + 144, 128), f32),
            pltpu.VMEM((own, 2, modes_x, modes_z), f32),
            pltpu.VMEM((parts, rows, cols), f32),
            dma((4,)),
            dma((4,)),
        ],
        compiler_params=pltpu.CompilerParams(vmem_limit_bytes=52 * 1024 * 1024),
        name="flux",
    )(
        live,
        block_count,
        block_order,
        gather_0.reshape(tiles * 8, 128),
        gather_1.reshape(tiles * 8, 128),
        jnp.asarray(mode_weights(planes, modes_z)),
        amplitude.reshape(own, 2 * modes_x, modes_z),
        staged,
    )
    return psi_next.reshape(psi_now.shape), amplitude_next.reshape(amplitude.shape)


def solution(mesh):
    return jax.shard_map(
        shards,
        mesh=mesh,
        in_specs=(
            P(None, None, "gy", "gx"),
            P(None, "gy", "gx"),
            P("gy", "gx", None),
            P("gy", "gx"),
            P(),
            P(),
            P(("gx", "gy"), None, None, None),
        ),
        out_specs=(P(None, None, "gy", "gx"), P(("gx", "gy"), None, None, None)),
        check_vma=False,
    )
```

```python
import functools
import math

import jax
import jax.numpy as jnp
import numpy as np
from jax import lax
from jax.experimental import pallas as pl
from jax.experimental.pallas import tpu as pltpu
from jax.sharding import PartitionSpec as P

spacing = 0.2
kinetic = 12.5
step_dt = 0.016
half_dt = 0.008
start_time = 100.0
later_time = start_time + step_dt
field_peak = 0.05
field_freq = 0.057
k_span = 4.0
flux_weight = 0.0078125
MESH = pl.DeviceIdType.MESH
f32 = jnp.float32


def field_at(moment):
    return field_peak * math.sin(field_freq * moment)


def drift_at(moment):
    return field_peak / (field_freq * field_freq) * math.sin(field_freq * moment)


def mode_weights(planes, modes):
    wave = ((np.arange(modes) - 0.5 * (modes - 1)) * (k_span / modes)).astype(np.float32)
    height = np.float32(spacing) * (np.arange(planes) - 0.5 * (planes - 1)).astype(np.float32)
    out = np.zeros((2, 4 * planes, 4 * modes), np.float32)
    for t, moment in enumerate((start_time, later_time)):
        phase = (
            np.float32(0.5) * wave * wave * np.float32(moment) + wave * np.float32(drift_at(moment))
        )[None, :] - wave[None, :] * height[:, None]
        cos = np.cos(phase.astype(np.float64)).astype(np.float32)
        sin = np.sin(phase.astype(np.float64)).astype(np.float32)
        block = np.block([[cos, sin], [-sin, cos]])
        out[t, : 2 * planes, : 2 * modes] = block
        out[t, 2 * planes :, 2 * modes :] = block
    high = out.astype(jnp.bfloat16).astype(np.float32)
    mid = (out - high).astype(jnp.bfloat16).astype(np.float32)
    low = out - high - mid
    none = np.zeros_like(out)
    return np.concatenate([high, high, high, mid, low, mid, none, none], axis=1).astype(jnp.bfloat16)


def iota(shape, dim):
    return lax.broadcasted_iota(jnp.int32, shape, dim)


def step_kernel(
    x_count,
    y_count,
    cells_ref,
    count_ref,
    psi_hbm,
    pot_hbm,
    next_hbm,
    gather_0,
    gather_1,
    live_ref,
    psi_v,
    sec_v,
    pot_v,
    row_msg,
    row_got,
    col_msg,
    col_got,
    corner_got,
    ghost,
    load_sem,
    store_sem,
    row_send,
    row_recv,
    col_send,
    col_recv,
    corner_send,
    corner_recv,
    x_send,
    x_recv,
    y_send,
    y_recv,
):
    gx = lax.axis_index("gx")
    gy = lax.axis_index("gy")
    parts, rows, cols = psi_hbm.shape
    planes = parts // 2
    blocks = rows // 8
    lane_blocks = cols // 128
    top = 8

    def wrap(value, count):
        return lax.rem(value + count, count)

    west, east = wrap(gx - 1, x_count), wrap(gx + 1, x_count)
    north, south = wrap(gy - 1, y_count), wrap(gy + 1, y_count)
    loads = []
    for j in range(lane_blocks):
        sl = slice(128 * j, 128 * j + 128)
        loads.append(
            pltpu.make_async_copy(
                psi_hbm.at[:, :, sl], psi_v.at[j, :, top : top + rows, :], load_sem.at[0, j]
            )
        )
        loads.append(pltpu.make_async_copy(pot_hbm.at[:, :, sl], pot_v.at[j], load_sem.at[1, j]))
    for copy in loads:
        copy.start()

    barrier = pltpu.get_barrier_semaphore()
    partner = gx + 1 - 2 * lax.rem(gx, 2)
    column = lax.rem(gx, 2)
    chip = gx // 2
    chips = x_count // 2
    signals = 0
    for k in range(1, chips):
        pl.semaphore_signal(
            barrier, inc=1, device_id=(wrap(gx + 2 * k, x_count), gy), device_id_type=MESH
        )
        signals += 1
    for k in range(1, y_count):
        pl.semaphore_signal(barrier, inc=1, device_id=(gx, wrap(gy + k, y_count)), device_id_type=MESH)
        signals += 1
    for sx in (west, east):
        for sy in (north, gy, south):
            pl.semaphore_signal(barrier, inc=1, device_id=(sx, sy), device_id_type=MESH)
            signals += 1

    for copy in loads:
        copy.wait()

    for side, (near, far) in enumerate(((top, top + 1), (top + rows - 1, top + rows - 2))):
        for j in range(lane_blocks):
            sl = slice(128 * j, 128 * j + 128)
            for p in range(parts):
                row_msg[side, p : p + 1, sl] = psi_v[j, p, near : near + 1, :]
                row_msg[side, parts + p : parts + p + 1, sl] = psi_v[j, p, far : far + 1, :]
            for z in range(planes):
                row_msg[side, 2 * parts + z : 2 * parts + z + 1, sl] = pot_v[
                    j, z, near - top : near - top + 1, :
                ]

    lane8 = iota((8, 128), 1)
    sub8 = iota((8, 128), 0)

    def pack(b, carry):
        r0 = pl.multiple_of(b * 8, 8)
        for side in range(2):
            j = 0 if side == 0 else lane_blocks - 1
            base = 0 if side == 0 else 2
            moved = [
                (p, pltpu.roll(psi_v[j, p, pl.ds(r0 + top, 8), :], (2 * p + base) % 128, 1))
                for p in range(parts)
            ] + [
                (32 + z, pltpu.roll(pot_v[j, z, pl.ds(r0, 8), :], (64 + 2 * z + base) % 128, 1))
                for z in range(planes)
            ]
            while len(moved) > 1:
                joined = []
                for i in range(0, len(moved) - 1, 2):
                    (at_a, part_a), (at_b, part_b) = moved[i], moved[i + 1]
                    joined.append((at_a, jnp.where(lane8 < 2 * at_b, part_a, part_b)))
                if len(moved) % 2:
                    joined.append(moved[-1])
                moved = joined
            packed = moved[0][1]
            col_msg[side, pl.ds(r0, 8), :] = packed
        return carry

    lax.fori_loop(0, blocks, pack, 0, unroll=4)

    pl.semaphore_wait(barrier, signals)

    halo = []
    for side, target in enumerate((north, south)):
        halo.append(
            pltpu.make_async_remote_copy(
                src_ref=row_msg.at[side],
                dst_ref=row_got.at[1 - side],
                send_sem=row_send.at[side],
                recv_sem=row_recv.at[1 - side],
                device_id=(gx, target),
                device_id_type=MESH,
            )
        )
    for side, target in enumerate((west, east)):
        halo.append(
            pltpu.make_async_remote_copy(
                src_ref=col_msg.at[side],
                dst_ref=col_got.at[1 - side],
                send_sem=col_send.at[side],
                recv_sem=col_recv.at[1 - side],
                device_id=(target, gy),
                device_id_type=MESH,
            )
        )
    for sy, ty in enumerate((north, south)):
        for sx, tx in enumerate((west, east)):
            lo = 0 if sx == 0 else cols - 128
            halo.append(
                pltpu.make_async_remote_copy(
                    src_ref=row_msg.at[sy, 0:parts, lo : lo + 128],
                    dst_ref=corner_got.at[2 * (1 - sy) + 1 - sx],
                    send_sem=corner_send.at[2 * sy + sx],
                    recv_sem=corner_recv.at[2 * (1 - sy) + 1 - sx],
                    device_id=(tx, ty),
                    device_id_type=MESH,
                )
            )
    for copy in halo:
        copy.start()

    lane_p = iota((parts, 128), 1)

    def take(slot, carry):
        out_u, out_d = carry
        cell = cells_ref[0, 0, slot]
        y = cell // cols
        x = cell - y * cols
        alive = jnp.where(slot < count_ref[0, 0], 1.0, 0.0).astype(f32)
        px = jnp.full((1, 128), spacing * ((gx * cols + x).astype(f32) - (0.5 * cols * x_count - 0.5)), f32)
        py = jnp.full((1, 128), spacing * ((gy * rows + y).astype(f32) - (0.5 * rows * y_count - 0.5)), f32)
        radius = jnp.sqrt(px * px + py * py)
        weight_x = px / radius / (2.0 * spacing) * alive
        weight_y = py / radius / (2.0 * spacing) * alive
        total_u = jnp.zeros((parts, 128), f32)
        total_d = jnp.zeros((parts, 128), f32)
        low = jnp.minimum(jnp.maximum(x - 1, 0) // 128, max(lane_blocks - 2, 0))
        for j in [low + i for i in range(min(lane_blocks, 2))]:
            lane = iota((1, 128), 1) + 128 * j
            at = jnp.where(lane == x, alive, 0.0)
            along = jnp.where(lane == x + 1, weight_x, 0.0) - jnp.where(lane == x - 1, weight_x, 0.0)
            across = jnp.where(lane == x, weight_y, 0.0)
            flat = psi_v.at[j].reshape(parts * (rows + 16), 128)
            middle = flat[pl.ds(y + top, parts, stride=rows + 16), :]
            after = flat[pl.ds(y + top + 1, parts, stride=rows + 16), :]
            before = flat[pl.ds(y + top - 1, parts, stride=rows + 16), :]
            total_u = total_u + middle * at
            total_d = total_d + (middle * along + (after - before) * across)
        out_u = jnp.where(lane_p == slot, jnp.sum(total_u, axis=1, keepdims=True), out_u)
        out_d = jnp.where(lane_p == slot, jnp.sum(total_d, axis=1, keepdims=True), out_d)
        return out_u, out_d

    slots = cells_ref.shape[2]

    half_kin = half_dt * kinetic

    def swap_parts(value):
        return jnp.concatenate([value[planes:], -value[:planes]], axis=0)

    sub_p = lax.rem(iota((parts, 128), 0), planes)
    hit_w = lane_p == 2 * iota((parts, 128), 0) + 1
    hit_e = lane_p == 2 * iota((parts, 128), 0)

    def take_next(slot, carry):
        out_u, out_d = carry
        cell = cells_ref[0, 0, slot]
        row = cell // cols
        x = cell - row * cols
        y = jnp.maximum(row, 1)
        alive = jnp.where(slot < count_ref[0, 0], 1.0, 0.0).astype(f32)
        px = jnp.full((1, 128), spacing * ((gx * cols + x).astype(f32) - (0.5 * cols * x_count - 0.5)), f32)
        py = jnp.full((1, 128), spacing * ((gy * rows + y).astype(f32) - (0.5 * rows * y_count - 0.5)), f32)
        radius = jnp.sqrt(px * px + py * py)
        weight_x = px / radius / (2.0 * spacing) * alive
        weight_y = py / radius / (2.0 * spacing) * alive
        shift = half_dt * (
            field_2 * (spacing * (sub_p.astype(f32) - 0.5 * (planes - 1))) + 6.0 * kinetic
        )
        zero = jnp.zeros((parts, 128), f32)
        mean = [zero, zero]
        plain = [zero, zero]
        scaled = [zero, zero]
        around = [zero, zero]
        low = jnp.minimum(jnp.maximum(x - 2, 0) // 128, max(lane_blocks - 2, 0))
        for j in [low + i for i in range(min(lane_blocks, 2))]:
            lane = iota((1, 128), 1) + 128 * j
            at = jnp.where(lane == x, alive, 0.0)
            at_side = jnp.where((lane == x + 1) | (lane == x - 1), alive, 0.0)
            along = jnp.where(lane == x + 1, weight_x, 0.0) - jnp.where(lane == x - 1, weight_x, 0.0)
            along_side = jnp.where(lane == x + 2, weight_x, 0.0) - jnp.where(
                lane == x - 2, weight_x, 0.0
            )
            across = jnp.where(lane == x, weight_y, 0.0)
            across_side = jnp.where((lane == x + 1) | (lane == x - 1), weight_y, 0.0)
            flat_s = sec_v.at[j].reshape(parts * (rows + 16), 128)
            flat_f = psi_v.at[j].reshape(parts * (rows + 16), 128)
            flat_p = pot_v.at[j].reshape(planes * rows, 128)
            sec = [flat_s[pl.ds(y + top + r, parts, stride=rows + 16), :] for r in range(-2, 3)]
            psi = [flat_f[pl.ds(y + top + r, parts, stride=rows + 16), :] for r in range(-1, 2)]
            pot = [flat_p[pl.ds(y + r, planes, stride=rows), :] for r in range(-1, 2)]
            coeff = [jnp.concatenate([v, v], axis=0) * half_dt + shift for v in pot]
            mean[0] = mean[0] + (0.5 * at) * (psi[1] + sec[2])
            plain[0] = plain[0] + at * sec[2]
            scaled[0] = scaled[0] + at * (coeff[1] * sec[2])
            around[0] = around[0] + (at * (sec[1] + sec[3]) + at_side * sec[2])
            mean[1] = mean[1] + 0.5 * (
                along * (psi[1] + sec[2]) + across * ((psi[2] + sec[3]) - (psi[0] + sec[1]))
            )
            plain[1] = plain[1] + (along * sec[2] + across * (sec[3] - sec[1]))
            scaled[1] = scaled[1] + (
                along * (coeff[1] * sec[2]) + across * (coeff[2] * sec[3] - coeff[0] * sec[1])
            )
            around[1] = around[1] + (
                (along * (sec[1] + sec[3]) + across * (sec[4] - sec[0]))
                + (along_side * sec[2] + across_side * (sec[3] - sec[1]))
            )
        row_w = ghost[1, 0, pl.ds(y, 1), :] * jnp.where(x == 1, -weight_x, 0.0)
        row_e = ghost[1, 1, pl.ds(y, 1), :] * jnp.where(x == cols - 2, weight_x, 0.0)
        around[1] = around[1] + (jnp.where(hit_w, row_w, 0.0) + jnp.where(hit_e, row_e, 0.0))
        sums = []
        for i in range(2):
            below = jnp.where(sub_p == 0, 0.0, pltpu.roll(plain[i], 1, 0))
            above = jnp.where(sub_p == planes - 1, 0.0, pltpu.roll(plain[i], parts - 1, 0))
            move = scaled[i] - half_kin * (around[i] + (below + above))
            sums.append(jnp.sum(mean[i] + swap_parts(move), axis=1, keepdims=True))
        return jnp.where(lane_p == slot, sums[0], out_u), jnp.where(lane_p == slot, sums[1], out_d)

    def surface(target, is_now):
        zero = jnp.zeros((parts, 128), f32)
        out_u, out_d = lax.fori_loop(
            0, slots, take if is_now else take_next, (zero, zero), unroll=4 if is_now else 2
        )
        turned = jnp.transpose(
            jnp.concatenate([out_u, out_d, jnp.zeros((128 - 2 * parts, 128), f32)], axis=0)
        )
        packed = jnp.where(lane8 < 64, turned[0:8], pltpu.roll(turned[8:16], 64, 1))
        if is_now:
            for slot in range(slots):
                cell = cells_ref[0, 0, slot]
                y = cell // cols
                x = cell - y * cols
                px = spacing * ((gx * cols + x).astype(f32) - (0.5 * cols * x_count - 0.5))
                py = spacing * ((gy * rows + y).astype(f32) - (0.5 * rows * y_count - 0.5))
                base = 64 * (slot // 8) + 2 * parts
                row = sub8 == slot % 8
                packed = jnp.where(row & (lane8 == base), px, packed)
                packed = jnp.where(row & (lane8 == base + 1), py, packed)
            packed = jnp.where(lane8 == 2 * parts + 2, count_ref[0, 0].astype(f32), packed)
        target[column, gy, chip] = packed

    def chip_copy(buf, phase, k, source):
        return pltpu.make_async_remote_copy(
            src_ref=buf.at[column, gy, source],
            dst_ref=buf.at[column, gy, source],
            send_sem=x_send.at[phase, k],
            recv_sem=x_recv.at[phase, k],
            device_id=(wrap(gx + 2 * k, x_count), gy),
            device_id_type=MESH,
        )

    def y_copy(buf, phase, k, source):
        return pltpu.make_async_remote_copy(
            src_ref=buf.at[column, source],
            dst_ref=buf.at[column, source],
            send_sem=y_send.at[phase, k],
            recv_sem=y_recv.at[phase, k],
            device_id=(gx, wrap(gy + k, y_count)),
            device_id_type=MESH,
        )

    def pair_copy(buf, phase, which):
        return pltpu.make_async_remote_copy(
            src_ref=buf.at[which],
            dst_ref=buf.at[which],
            send_sem=x_send.at[phase, 0],
            recv_sem=x_recv.at[phase, 0],
            device_id=(partner, gy),
            device_id_type=MESH,
        )

    def hop_1(buf, phase):
        for k in range(1, chips):
            chip_copy(buf, phase, k, chip).start()

    def hop_2(buf, phase):
        for k in range(1, chips):
            chip_copy(buf, phase, k, wrap(chip - k, chips)).wait_recv()
        for k in range(1, y_count):
            y_copy(buf, phase, k, gy).start()

    def hop_3(buf, phase):
        for k in range(1, y_count):
            y_copy(buf, phase, k, wrap(gy - k, y_count)).wait_recv()
        pair_copy(buf, phase, column).start()

    def hop_end(buf, phase):
        pair_copy(buf, phase, 1 - column).wait_recv()

    def sends_wait(buf, phase):
        for k in range(1, chips):
            chip_copy(buf, phase, k, chip).wait_send()
        for k in range(1, y_count):
            y_copy(buf, phase, k, gy).wait_send()
        pair_copy(buf, phase, column).wait_send()

    field_1 = field_at(start_time)
    field_2 = field_at(later_time)
    first = lane8 == 0
    last = lane8 == 127

    def edges(stage, p, b):
        at = pl.ds(pl.multiple_of(b * 8, 8), 8)
        edge_w = pltpu.roll(ghost[stage, 0, at, :], (128 - (2 * p + 1)) % 128, 1)
        edge_e = pltpu.roll(ghost[stage, 1, at, :], (127 - 2 * p) % 128, 1)
        return edge_w, edge_e

    def spread(src, p, r0, stage, b):
        rows_b = pl.ds(r0, 8)
        cur = [src[j, p, rows_b, :] for j in range(lane_blocks)]
        right = [pltpu.roll(c, 1, 1) for c in cur]
        left = [pltpu.roll(c, 127, 1) for c in cur]
        if stage == 0:
            edge_w = edge_e = 0.0
        else:
            edge_w, edge_e = edges(1, p, b)
        out = []
        for j in range(lane_blocks):
            up = src[j, p, pl.ds(r0 - 1, 8), :]
            down = src[j, p, pl.ds(r0 + 1, 8), :]
            w = jnp.where(first, edge_w if j == 0 else right[j - 1], right[j])
            e = jnp.where(last, edge_e if j == lane_blocks - 1 else left[j + 1], left[j])
            out.append((up + down) + (w + e))
        return cur, out

    def stage_block(src, stage, b, finish):
        r0 = pl.multiple_of(b * 8 + top, 8)
        rows_b = pl.ds(r0, 8)
        dt = step_dt if stage == 0 else half_dt
        field = field_1 if stage == 0 else field_2
        for z in range(planes):
            found = [spread(src, part * planes + z, r0, stage, b) for part in range(2)]
            shift = dt * (field * spacing * (z - 0.5 * (planes - 1)) + 6.0 * kinetic)
            for j in range(lane_blocks):
                coeff = dt * pot_v[j, z, pl.ds(pl.multiple_of(b * 8, 8), 8), :] + shift
                moves = []
                for part in range(2):
                    cur, beside = found[part]
                    p = part * planes + z
                    total = beside[j]
                    if z > 0:
                        total = total + src[j, p - 1, rows_b, :]
                    if z < planes - 1:
                        total = total + src[j, p + 1, rows_b, :]
                    moves.append(coeff * cur[j] - (dt * kinetic) * total)
                finish(z, rows_b, j, found[0][0][j], found[1][0][j], moves)

    def finish_section(z, rows_b, j, real, imag, moves):
        sec_v[j, z, rows_b, :] = real + moves[1]
        sec_v[j, planes + z, rows_b, :] = imag - moves[0]

    def finish_next(z, rows_b, j, real, imag, moves):
        psi_v[j, z, rows_b, :] = 0.5 * (psi_v[j, z, rows_b, :] + real) + moves[1]
        psi_v[j, planes + z, rows_b, :] = 0.5 * (psi_v[j, planes + z, rows_b, :] + imag) - moves[0]

    def run_section(b, carry):
        stage_block(psi_v, 0, b, finish_section)
        return carry

    def run_next(b, carry):
        stage_block(sec_v, 1, b, finish_next)
        return carry

    def fix_columns(b, carry):
        rows_b = pl.ds(pl.multiple_of(b * 8 + top, 8), 8)
        sides = []
        for p in range(parts):
            other = (p + planes) % parts
            edge_w, edge_e = edges(0, p, b)
            scale = step_dt * kinetic if p < planes else -step_dt * kinetic
            sides.append(
                (
                    other,
                    sec_v[0, other, rows_b, :] + jnp.where(first, scale * edge_w, 0.0),
                    sec_v[lane_blocks - 1, other, rows_b, :] + jnp.where(last, scale * edge_e, 0.0),
                )
            )
        for other, low, high in sides:
            sec_v[0, other, rows_b, :] = low
            sec_v[lane_blocks - 1, other, rows_b, :] = high
        return carry

    surface(gather_0, True)
    hop_1(gather_0, 0)
    clear = jnp.zeros((1, 128), f32)
    for j in range(lane_blocks):
        for p in range(parts):
            psi_v[j, p, top - 1 : top, :] = clear
            psi_v[j, p, top + rows : top + rows + 1, :] = clear
    lax.fori_loop(0, blocks, run_section, 0)
    hop_2(gather_0, 0)

    for copy in halo:
        copy.wait_recv()

    keep_n = jnp.where(gy > 0, 1.0, 0.0).astype(f32)
    keep_s = jnp.where(gy < y_count - 1, 1.0, 0.0).astype(f32)
    keep_w = jnp.where(gx > 0, 1.0, 0.0).astype(f32)
    keep_e = jnp.where(gx < x_count - 1, 1.0, 0.0).astype(f32)

    def height(index):
        return spacing * (index.astype(f32) - 0.5 * (planes - 1))

    corner_cols = []
    for sy, keep_y in enumerate((keep_n, keep_s)):
        for sx, keep_x in enumerate((keep_w, keep_e)):
            lane = 127 if sx == 0 else 0
            corner_cols.append(corner_got[2 * sy + sx][:, lane : lane + 1] * (keep_y * keep_x))
    lane_row = iota((planes, cols), 1)
    sub_row = iota((planes, cols), 0)
    for side, keep in enumerate((keep_n, keep_s)):
        coeff = step_dt * (
            row_got[side, 2 * parts : 2 * parts + planes, :] + field_1 * height(sub_row) + 6.0 * kinetic
        )
        nears = []
        moves = []
        for part in range(2):
            sl = slice(part * planes, (part + 1) * planes)
            near = row_got[side, sl, :] * keep
            far = row_got[side, parts + part * planes : parts + (part + 1) * planes, :] * keep
            own = row_msg[side, sl, :]
            left = jnp.where(lane_row == 0, corner_cols[2 * side][sl], pltpu.roll(near, 1, 1))
            right = jnp.where(lane_row == cols - 1, corner_cols[2 * side + 1][sl], pltpu.roll(near, cols - 1, 1))
            below = jnp.where(sub_row == 0, 0.0, pltpu.roll(near, 1, 0))
            above = jnp.where(sub_row == planes - 1, 0.0, pltpu.roll(near, planes - 1, 0))
            beside = (far + own) + (left + right) + (below + above)
            nears.append(near)
            moves.append(coeff * near - (step_dt * kinetic) * beside)
        ghost_rows = (nears[0] + moves[1]) * keep, (nears[1] - moves[0]) * keep
        at = top - 1 if side == 0 else top + rows
        edge = top if side == 0 else top + rows - 1
        for part in range(2):
            for z in range(planes):
                for j in range(lane_blocks):
                    sl = slice(128 * j, 128 * j + 128)
                    p = part * planes + z
                    sec_v[j, p, at : at + 1, :] = ghost_rows[part][z : z + 1, sl]
                    share = (step_dt * kinetic) * nears[1 - part][z : z + 1, sl]
                    old = sec_v[j, p, edge : edge + 1, :]
                    sec_v[j, p, edge : edge + 1, :] = old - share if part == 0 else old + share

    lane_c = iota((rows, 128), 1)
    sub_c = iota((rows, 128), 0)
    diag_lane = iota((parts, 128), 1)
    diag_sub = iota((parts, 128), 0)
    plane_c = (lane_c % (2 * planes)) // 2
    for side, keep in enumerate((keep_w, keep_e)):
        got = col_got[side] * keep
        mine = col_msg[side]
        inner = 1 if side == 0 else 127
        odd = 1 if side == 0 else 0
        hit = diag_lane == 2 * diag_sub + odd
        ends = [
            jnp.sum(jnp.where(hit, corner_cols[2 * sy + side], 0.0), axis=0, keepdims=True)
            for sy in range(2)
        ]
        upper = jnp.where(sub_c == 0, ends[0], pltpu.roll(got, 1, 0))
        lower = jnp.where(sub_c == rows - 1, ends[1], pltpu.roll(got, rows - 1, 0))
        below = jnp.where(plane_c == 0, 0.0, pltpu.roll(got, 2, 1))
        above = jnp.where(plane_c == planes - 1, 0.0, pltpu.roll(got, 126, 1))
        beside = (
            (pltpu.roll(got, inner, 1) + pltpu.roll(mine, inner, 1)) + (upper + lower) + (below + above)
        )
        volts = pltpu.roll(got, 64, 1)
        volts = jnp.where(lane_c < 2 * planes, volts, pltpu.roll(volts, 2 * planes, 1))
        coeff = step_dt * (volts + field_1 * height(plane_c) + 6.0 * kinetic)
        move = coeff * got - (step_dt * kinetic) * beside
        ghost[0, side] = got
        ghost[1, side] = (
            got
            + jnp.where(
                lane_c < 2 * planes, pltpu.roll(move, 128 - 2 * planes, 1), -pltpu.roll(move, 2 * planes, 1)
            )
        ) * keep

    lax.fori_loop(0, blocks, fix_columns, 0, unroll=2)
    surface(gather_1, False)
    hop_1(gather_1, 1)
    stores = []
    pieces = 4
    per = blocks // pieces
    for q in range(pieces):
        lax.fori_loop(q * per, (q + 1) * per, run_next, 0)
        for j in range(lane_blocks):
            stores.append(
                pltpu.make_async_copy(
                    psi_v.at[j, :, top + 8 * per * q : top + 8 * per * (q + 1), :],
                    next_hbm.at[:, 8 * per * q : 8 * per * (q + 1), 128 * j : 128 * j + 128],
                    store_sem.at[q, j],
                )
            )
            stores[-1].start()
        if q == 0:
            hop_2(gather_1, 1)
            hop_3(gather_0, 0)
    hop_end(gather_0, 0)

    def count_row(i, total):
        for k in range(x_count):
            got = gather_0[i // (y_count // 2), lax.rem(i, y_count // 2) * 2 + k // chips, k % chips]
            total = jnp.where(lane8 == i * x_count + k, got[:, 2 * parts + 2 : 2 * parts + 3], total)
        return total

    live_ref[...] = lax.fori_loop(0, y_count, count_row, jnp.zeros((8, 128), f32))
    hop_3(gather_1, 1)
    for copy in halo:
        copy.wait_send()
    for copy in stores:
        copy.wait()
    hop_end(gather_1, 1)
    sends_wait(gather_0, 0)
    sends_wait(gather_1, 1)


def turns(phase):
    quarter = jnp.floor(phase * 0.6366197723675814 + 0.5)
    rest = phase - quarter * 1.5703125
    rest = rest - quarter * 4.83751296997e-4
    rest = rest - quarter * 7.5497899548918821e-8
    square = rest * rest
    sine = rest + rest * square * (
        -1.6666654611e-1 + square * (8.3321608736e-3 + square * -1.9515295891e-4)
    )
    cosine = (
        1.0
        - 0.5 * square
        + square * square * (4.166664568298827e-2 + square * (-1.388731625493765e-3 + square * 2.443315711809948e-5))
    )
    which = quarter.astype(jnp.int32)
    swap = (which & 1) == 1
    sin_out = jnp.where(swap, cosine, sine)
    cos_out = jnp.where(swap, sine, cosine)
    sin_out = jnp.where((which & 2) == 2, -sin_out, sin_out)
    cos_out = jnp.where(((which + 1) & 2) == 2, -cos_out, cos_out)
    return cos_out, sin_out


def flux_kernel(
    x_count,
    y_count,
    live_ref,
    count_ref,
    order_ref,
    gather_0,
    gather_1,
    weight_ref,
    amp_ref,
    tmp_hbm,
    next_hbm,
    out_ref,
    comp_0,
    comp_1,
    total,
    held,
    fetch_sem,
    copy_sem,
):
    copies = []
    parts = tmp_hbm.shape[0]
    quarter = parts // 4
    for q in range(4):
        sl = slice(q * quarter, (q + 1) * quarter)
        fetch = pltpu.make_async_copy(tmp_hbm.at[sl], held.at[sl], fetch_sem.at[q])
        fetch.start()
        copies.append((fetch, pltpu.make_async_copy(held.at[sl], next_hbm.at[sl], copy_sem.at[q])))
    me = lax.axis_index("gx") * y_count + lax.axis_index("gy")
    groups = count_ref.shape[0]
    slots = amp_ref.shape[0]
    features = weight_ref.shape[1] // 8
    feature = iota((128, 128), 1) < features

    def offset(i, at):
        return at + jnp.where(i < me, count_ref[i], 0)

    own_start = lax.fori_loop(0, groups, offset, 0, unroll=8)
    own_count = count_ref[me]
    waves = []
    for s in range(slots):
        plane = order_ref[jnp.minimum(own_start + s, groups - 1)]
        waves.append((plane.astype(f32) - 0.5 * (groups - 1)) * (k_span / groups))

    def gather_tile(t, n):
        c = live_ref[0, t].astype(jnp.int32)
        at = pl.ds(pl.multiple_of(t * 8, 8), 8)
        block_0, block_1 = gather_0[at, :], gather_1[at, :]
        comp_0[pl.ds(n, 8), :] = block_0
        comp_1[pl.ds(n, 8), :] = block_1
        n = n + jnp.minimum(c, 8)
        comp_0[pl.ds(n, 8), :] = pltpu.roll(block_0, 64, 1)
        comp_1[pl.ds(n, 8), :] = pltpu.roll(block_1, 64, 1)
        return n + jnp.maximum(c - 8, 0)

    live = lax.fori_loop(0, x_count * y_count, gather_tile, 0, unroll=8)

    def clear(i, carry):
        to = pl.ds(live + i * 8, 8)
        comp_0[to, :] = jnp.zeros((8, 128), f32)
        comp_1[to, :] = jnp.zeros((8, 128), f32)
        return carry

    lax.fori_loop(0, 16, clear, 0)
    total[...] = jnp.zeros_like(total)
    kx = (iota((128, 128), 0).astype(f32) - 63.5) * (k_span / 128)
    sub8 = iota((8, 128), 0)
    ky = jnp.zeros((8, 128), f32)
    for s in range(slots):
        ky = jnp.where(sub8 // 2 == s, waves[s], ky)
    moment8 = jnp.where(sub8 % 2 == 0, start_time, later_time).astype(f32)

    def chunk(c, carry):
        at = pl.ds(pl.multiple_of(c * 128, 128), 128)
        rows = (comp_0[at, :], comp_1[at, :])
        place = jnp.transpose(rows[0])
        px, py = place[features : features + 1, :], place[features + 1 : features + 2, :]
        col_x, col_y = rows[0][:, features : features + 1], rows[0][:, features + 1 : features + 2]
        square = col_x * col_x + col_y * col_y
        radius = jnp.sqrt(jnp.where(square > 0.0, square, 1.0))
        nx, ny = col_x / radius, col_y / radius
        right = []
        left = []
        for t, moment in enumerate((start_time, later_time)):
            raw = jnp.where(feature, rows[t], 0.0)
            high = raw.astype(jnp.bfloat16).astype(f32)
            mid = (raw - high).astype(jnp.bfloat16).astype(f32)
            low = (raw - high) - mid
            side = (
                (high + pltpu.roll(mid, features, 1))
                + (pltpu.roll(low, 2 * features, 1) + pltpu.roll(high, 3 * features, 1))
            ).astype(jnp.bfloat16)
            modes = jnp.dot(
                jnp.concatenate([side, side], axis=1), weight_ref[t], preferred_element_type=f32
            )
            ur, ui, dr, di = (modes[:, 128 * i : 128 * i + 128] for i in range(4))
            right.append(
                jnp.concatenate([nx * ur, ny * ur, dr, nx * ui, ny * ui, di], axis=1).astype(jnp.bfloat16)
            )
            left.append(turns(0.5 * kx * kx * moment - kx * px))
        right = jnp.concatenate(right, axis=0)
        rot_cos, rot_sin = turns(0.5 * ky * ky * moment8 - ky * py)

        for first in range(0, slots, 2):

            @pl.when(first < own_count)
            def _():
                sides = []
                pair = range(first, min(first + 2, slots))
                for s in pair:
                    real = []
                    imag = []
                    for t in range(2):
                        bc, bs = rot_cos[2 * s + t : 2 * s + t + 1], rot_sin[2 * s + t : 2 * s + t + 1]
                        ac, as_ = left[t]
                        real.append((ac * bc - as_ * bs).astype(jnp.bfloat16))
                        imag.append((ac * bs + as_ * bc).astype(jnp.bfloat16))
                    sides.append(jnp.concatenate(real, axis=1))
                    sides.append(jnp.concatenate(imag, axis=1))
                prod = jnp.dot(jnp.concatenate(sides, axis=0), right, preferred_element_type=f32)
                for i, s in enumerate(pair):
                    m = [prod[256 * i : 256 * i + 128, 128 * k : 128 * k + 128] for k in range(6)]
                    w = [prod[256 * i + 128 : 256 * i + 256, 128 * k : 128 * k + 128] for k in range(6)]
                    hy = waves[s]
                    total[s, 0] += kx * (m[0] - w[3]) + hy * (m[1] - w[4]) + (m[5] + w[2])
                    total[s, 1] += kx * (m[3] + w[0]) + hy * (m[4] + w[1]) - (m[2] - w[5])

        return carry

    chunks = (live + 127) // 128
    lax.fori_loop(0, jnp.minimum(chunks, 1), chunk, 0)
    for fetch, copy in copies:
        fetch.wait()
        copy.start()
    lax.fori_loop(1, chunks, chunk, 0)
    for s in range(slots):
        for part in range(2):
            sl = pl.ds(part, 128, stride=2)
            inc = jnp.where(s < own_count, (0.5 * flux_weight) * total[s, part], 0.0)
            out_ref[s, sl, :] = amp_ref[s, sl, :] + inc
    for fetch, copy in copies:
        copy.wait()


def shards(psi_now, potential, surf_cells, surf_count, block_count, block_order, amplitude):
    x_count = lax.axis_size("gx")
    y_count = lax.axis_size("gy")
    planes, rows, cols = potential.shape
    parts = 2 * planes
    slots = surf_cells.shape[2]
    own, modes_x, _, modes_z = amplitude.shape
    any_spec = pl.BlockSpec(memory_space=pl.ANY)
    vmem = pl.BlockSpec(memory_space=pltpu.VMEM)
    smem = pl.BlockSpec(memory_space=pltpu.SMEM)
    hbm = pl.BlockSpec(memory_space=pltpu.HBM)
    dma = pltpu.SemaphoreType.DMA
    gathered = jax.ShapeDtypeStruct((2, y_count, x_count // 2, 8, 128), f32)
    field = jax.ShapeDtypeStruct((parts, rows, cols), f32)
    staged, gather_0, gather_1, live = pl.pallas_call(
        functools.partial(step_kernel, x_count, y_count),
        out_shape=(field, gathered, gathered, jax.ShapeDtypeStruct((8, 128), f32)),
        in_specs=[smem, smem, hbm, hbm],
        out_specs=(any_spec, vmem, vmem, vmem),
        scratch_shapes=[
            pltpu.VMEM((cols // 128, parts, rows + 16, 128), f32),
            pltpu.VMEM((cols // 128, parts, rows + 16, 128), f32),
            pltpu.VMEM((cols // 128, planes, rows, 128), f32),
            pltpu.VMEM((2, 2 * parts + planes, cols), f32),
            pltpu.VMEM((2, 2 * parts + planes, cols), f32),
            pltpu.VMEM((2, rows, 128), f32),
            pltpu.VMEM((2, rows, 128), f32),
            pltpu.VMEM((4, parts, 128), f32),
            pltpu.VMEM((2, 2, rows, 128), f32),
            dma((2, cols // 128)),
            dma((4, cols // 128)),
            dma((2,)),
            dma((2,)),
            dma((2,)),
            dma((2,)),
            dma((4,)),
            dma((4,)),
            dma((2, x_count)),
            dma((2, x_count)),
            dma((2, y_count)),
            dma((2, y_count)),
        ],
        compiler_params=pltpu.CompilerParams(
            collective_id=0, has_side_effects=True, vmem_limit_bytes=52 * 1024 * 1024
        ),
        name="step",
    )(
        surf_cells,
        surf_count,
        psi_now.reshape(parts, rows, cols),
        potential,
    )
    tiles = x_count * y_count
    psi_next, amplitude_next = pl.pallas_call(
        functools.partial(flux_kernel, x_count, y_count),
        out_shape=(field, jax.ShapeDtypeStruct((own, 2 * modes_x, modes_z), f32)),
        in_specs=[smem, smem, smem, vmem, vmem, vmem, vmem, any_spec],
        out_specs=(any_spec, vmem),
        scratch_shapes=[
            pltpu.VMEM((slots * tiles + 144, 128), f32),
            pltpu.VMEM((slots * tiles + 144, 128), f32),
            pltpu.VMEM((own, 2, modes_x, modes_z), f32),
            pltpu.VMEM((parts, rows, cols), f32),
            dma((4,)),
            dma((4,)),
        ],
        compiler_params=pltpu.CompilerParams(vmem_limit_bytes=52 * 1024 * 1024),
        name="flux",
    )(
        live,
        block_count,
        block_order,
        gather_0.reshape(tiles * 8, 128),
        gather_1.reshape(tiles * 8, 128),
        jnp.asarray(mode_weights(planes, modes_z)),
        amplitude.reshape(own, 2 * modes_x, modes_z),
        staged,
    )
    return psi_next.reshape(psi_now.shape), amplitude_next.reshape(amplitude.shape)


def solution(mesh):
    return jax.shard_map(
        shards,
        mesh=mesh,
        in_specs=(
            P(None, None, "gy", "gx"),
            P(None, "gy", "gx"),
            P("gy", "gx", None),
            P("gy", "gx"),
            P(),
            P(),
            P(("gx", "gy"), None, None, None),
        ),
        out_specs=(P(None, None, "gy", "gx"), P(("gx", "gy"), None, None, None)),
        check_vma=False,
    )
```

```python
import functools
import math

import jax
import jax.numpy as jnp
import numpy as np
from jax import lax
from jax.experimental import pallas as pl
from jax.experimental.pallas import tpu as pltpu
from jax.sharding import PartitionSpec as P

spacing = 0.2
kinetic = 12.5
step_dt = 0.016
half_dt = 0.008
start_time = 100.0
later_time = start_time + step_dt
field_peak = 0.05
field_freq = 0.057
k_span = 4.0
flux_weight = 0.0078125
MESH = pl.DeviceIdType.MESH
f32 = jnp.float32


def field_at(moment):
    return field_peak * math.sin(field_freq * moment)


def drift_at(moment):
    return field_peak / (field_freq * field_freq) * math.sin(field_freq * moment)


def mode_weights(planes, modes):
    wave = ((np.arange(modes) - 0.5 * (modes - 1)) * (k_span / modes)).astype(np.float32)
    height = np.float32(spacing) * (np.arange(planes) - 0.5 * (planes - 1)).astype(np.float32)
    out = np.zeros((2, 4 * planes, 4 * modes), np.float32)
    for t, moment in enumerate((start_time, later_time)):
        phase = (
            np.float32(0.5) * wave * wave * np.float32(moment) + wave * np.float32(drift_at(moment))
        )[None, :] - wave[None, :] * height[:, None]
        cos = np.cos(phase.astype(np.float64)).astype(np.float32)
        sin = np.sin(phase.astype(np.float64)).astype(np.float32)
        block = np.block([[cos, sin], [-sin, cos]])
        out[t, : 2 * planes, : 2 * modes] = block
        out[t, 2 * planes :, 2 * modes :] = block
    high = out.astype(jnp.bfloat16).astype(np.float32)
    mid = (out - high).astype(jnp.bfloat16).astype(np.float32)
    low = out - high - mid
    none = np.zeros_like(out)
    return np.concatenate([high, high, high, mid, low, mid, none, none], axis=1).astype(jnp.bfloat16)


def iota(shape, dim):
    return lax.broadcasted_iota(jnp.int32, shape, dim)


def step_kernel(
    x_count,
    y_count,
    cells_ref,
    count_ref,
    psi_hbm,
    pot_hbm,
    next_hbm,
    gather_0,
    gather_1,
    live_ref,
    psi_v,
    sec_v,
    pot_v,
    row_msg,
    row_got,
    col_msg,
    col_got,
    corner_got,
    ghost,
    load_sem,
    store_sem,
    row_send,
    row_recv,
    col_send,
    col_recv,
    corner_send,
    corner_recv,
    x_send,
    x_recv,
    y_send,
    y_recv,
):
    gx = lax.axis_index("gx")
    gy = lax.axis_index("gy")
    parts, rows, cols = psi_hbm.shape
    planes = parts // 2
    blocks = rows // 8
    lane_blocks = cols // 128
    top = 8

    def wrap(value, count):
        return lax.rem(value + count, count)

    west, east = wrap(gx - 1, x_count), wrap(gx + 1, x_count)
    north, south = wrap(gy - 1, y_count), wrap(gy + 1, y_count)
    loads = []
    load_order = [0, lane_blocks - 1] + list(range(1, lane_blocks - 1))
    for j in load_order:
        sl = slice(128 * j, 128 * j + 128)
        loads.append(
            pltpu.make_async_copy(
                psi_hbm.at[:, :, sl], psi_v.at[j, :, top : top + rows, :], load_sem.at[0, j]
            )
        )
        loads.append(pltpu.make_async_copy(pot_hbm.at[:, :, sl], pot_v.at[j], load_sem.at[1, j]))
    for copy in loads:
        copy.start()

    barrier = pltpu.get_barrier_semaphore()
    partner = gx + 1 - 2 * lax.rem(gx, 2)
    column = lax.rem(gx, 2)
    chip = gx // 2
    chips = x_count // 2
    signals = 0
    for k in range(1, x_count):
        pl.semaphore_signal(barrier, inc=1, device_id=(wrap(gx + k, x_count), gy), device_id_type=MESH)
        signals += 1
    for k in range(1, y_count):
        pl.semaphore_signal(barrier, inc=1, device_id=(gx, wrap(gy + k, y_count)), device_id_type=MESH)
        signals += 1
    for sx in (west, east):
        for sy in (north, south):
            pl.semaphore_signal(barrier, inc=1, device_id=(sx, sy), device_id_type=MESH)
            signals += 1

    for copy in loads[:4]:
        copy.wait()

    lane8 = iota((8, 128), 1)
    sub8 = iota((8, 128), 0)

    def pack(b, carry):
        r0 = pl.multiple_of(b * 8, 8)
        for side in range(2):
            j = 0 if side == 0 else lane_blocks - 1
            base = 0 if side == 0 else 2
            moved = [
                (p, pltpu.roll(psi_v[j, p, pl.ds(r0 + top, 8), :], (2 * p + base) % 128, 1))
                for p in range(parts)
            ] + [
                (32 + z, pltpu.roll(pot_v[j, z, pl.ds(r0, 8), :], (64 + 2 * z + base) % 128, 1))
                for z in range(planes)
            ]
            while len(moved) > 1:
                joined = []
                for i in range(0, len(moved) - 1, 2):
                    (at_a, part_a), (at_b, part_b) = moved[i], moved[i + 1]
                    joined.append((at_a, jnp.where(lane8 < 2 * at_b, part_a, part_b)))
                if len(moved) % 2:
                    joined.append(moved[-1])
                moved = joined
            packed = moved[0][1]
            col_msg[side, pl.ds(r0, 8), :] = packed
        return carry

    lax.fori_loop(0, blocks, pack, 0, unroll=4)

    pl.semaphore_wait(barrier, signals)

    halo = []
    for side, target in enumerate((west, east)):
        halo.append(
            pltpu.make_async_remote_copy(
                src_ref=col_msg.at[side],
                dst_ref=col_got.at[1 - side],
                send_sem=col_send.at[side],
                recv_sem=col_recv.at[1 - side],
                device_id=(target, gy),
                device_id_type=MESH,
            )
        )
    for copy in halo:
        copy.start()
    for copy in loads[4:]:
        copy.wait()
    for side, (near, far) in enumerate(((top, top + 1), (top + rows - 1, top + rows - 2))):
        for j in range(lane_blocks):
            sl = slice(128 * j, 128 * j + 128)
            for p in range(parts):
                row_msg[side, p : p + 1, sl] = psi_v[j, p, near : near + 1, :]
                row_msg[side, parts + p : parts + p + 1, sl] = psi_v[j, p, far : far + 1, :]
            for z in range(planes):
                row_msg[side, 2 * parts + z : 2 * parts + z + 1, sl] = pot_v[
                    j, z, near - top : near - top + 1, :
                ]

    for side, target in enumerate((north, south)):
        halo.append(
            pltpu.make_async_remote_copy(
                src_ref=row_msg.at[side],
                dst_ref=row_got.at[1 - side],
                send_sem=row_send.at[side],
                recv_sem=row_recv.at[1 - side],
                device_id=(gx, target),
                device_id_type=MESH,
            )
        )
    for sy, ty in enumerate((north, south)):
        for sx, tx in enumerate((west, east)):
            lo = 0 if sx == 0 else cols - 128
            halo.append(
                pltpu.make_async_remote_copy(
                    src_ref=row_msg.at[sy, 0:parts, lo : lo + 128],
                    dst_ref=corner_got.at[2 * (1 - sy) + 1 - sx],
                    send_sem=corner_send.at[2 * sy + sx],
                    recv_sem=corner_recv.at[2 * (1 - sy) + 1 - sx],
                    device_id=(tx, ty),
                    device_id_type=MESH,
                )
            )
    for copy in halo[2:]:
        copy.start()

    lane_p = iota((parts, 128), 1)

    def take(slot, carry):
        out_u, out_d = carry
        cell = cells_ref[0, 0, slot]
        y = cell // cols
        x = cell - y * cols
        alive = jnp.where(slot < count_ref[0, 0], 1.0, 0.0).astype(f32)
        px = jnp.full((1, 128), spacing * ((gx * cols + x).astype(f32) - (0.5 * cols * x_count - 0.5)), f32)
        py = jnp.full((1, 128), spacing * ((gy * rows + y).astype(f32) - (0.5 * rows * y_count - 0.5)), f32)
        radius = jnp.sqrt(px * px + py * py)
        weight_x = px / radius / (2.0 * spacing) * alive
        weight_y = py / radius / (2.0 * spacing) * alive
        total_u = jnp.zeros((parts, 128), f32)
        total_d = jnp.zeros((parts, 128), f32)
        low = jnp.minimum(jnp.maximum(x - 1, 0) // 128, max(lane_blocks - 2, 0))
        for j in [low + i for i in range(min(lane_blocks, 2))]:
            lane = iota((1, 128), 1) + 128 * j
            at = jnp.where(lane == x, alive, 0.0)
            along = jnp.where(lane == x + 1, weight_x, 0.0) - jnp.where(lane == x - 1, weight_x, 0.0)
            across = jnp.where(lane == x, weight_y, 0.0)
            flat = psi_v.at[j].reshape(parts * (rows + 16), 128)
            middle = flat[pl.ds(y + top, parts, stride=rows + 16), :]
            after = flat[pl.ds(y + top + 1, parts, stride=rows + 16), :]
            before = flat[pl.ds(y + top - 1, parts, stride=rows + 16), :]
            total_u = total_u + middle * at
            total_d = total_d + (middle * along + (after - before) * across)
        out_u = jnp.where(lane_p == slot, jnp.sum(total_u, axis=1, keepdims=True), out_u)
        out_d = jnp.where(lane_p == slot, jnp.sum(total_d, axis=1, keepdims=True), out_d)
        return out_u, out_d

    slots = cells_ref.shape[2]

    half_kin = half_dt * kinetic

    def swap_parts(value):
        return jnp.concatenate([value[planes:], -value[:planes]], axis=0)

    sub_p = lax.rem(iota((parts, 128), 0), planes)
    hit_w = lane_p == 2 * iota((parts, 128), 0) + 1
    hit_e = lane_p == 2 * iota((parts, 128), 0)

    def take_next(slot, carry):
        out_u, out_d = carry
        cell = cells_ref[0, 0, slot]
        row = cell // cols
        x = cell - row * cols
        y = jnp.maximum(row, 1)
        alive = jnp.where(slot < count_ref[0, 0], 1.0, 0.0).astype(f32)
        px = jnp.full((1, 128), spacing * ((gx * cols + x).astype(f32) - (0.5 * cols * x_count - 0.5)), f32)
        py = jnp.full((1, 128), spacing * ((gy * rows + y).astype(f32) - (0.5 * rows * y_count - 0.5)), f32)
        radius = jnp.sqrt(px * px + py * py)
        weight_x = px / radius / (2.0 * spacing) * alive
        weight_y = py / radius / (2.0 * spacing) * alive
        shift = half_dt * (
            field_2 * (spacing * (sub_p.astype(f32) - 0.5 * (planes - 1))) + 6.0 * kinetic
        )
        zero = jnp.zeros((parts, 128), f32)
        mean = [zero, zero]
        plain = [zero, zero]
        scaled = [zero, zero]
        around = [zero, zero]
        low = jnp.minimum(jnp.maximum(x - 2, 0) // 128, max(lane_blocks - 2, 0))
        for j in [low + i for i in range(min(lane_blocks, 2))]:
            lane = iota((1, 128), 1) + 128 * j
            at = jnp.where(lane == x, alive, 0.0)
            at_side = jnp.where((lane == x + 1) | (lane == x - 1), alive, 0.0)
            along = jnp.where(lane == x + 1, weight_x, 0.0) - jnp.where(lane == x - 1, weight_x, 0.0)
            along_side = jnp.where(lane == x + 2, weight_x, 0.0) - jnp.where(
                lane == x - 2, weight_x, 0.0
            )
            across = jnp.where(lane == x, weight_y, 0.0)
            across_side = jnp.where((lane == x + 1) | (lane == x - 1), weight_y, 0.0)
            flat_s = sec_v.at[j].reshape(parts * (rows + 16), 128)
            flat_f = psi_v.at[j].reshape(parts * (rows + 16), 128)
            flat_p = pot_v.at[j].reshape(planes * rows, 128)
            sec = [flat_s[pl.ds(y + top + r, parts, stride=rows + 16), :] for r in range(-2, 3)]
            psi = [flat_f[pl.ds(y + top + r, parts, stride=rows + 16), :] for r in range(-1, 2)]
            pot = [flat_p[pl.ds(y + r, planes, stride=rows), :] for r in range(-1, 2)]
            coeff = [jnp.concatenate([v, v], axis=0) * half_dt + shift for v in pot]
            mean[0] = mean[0] + (0.5 * at) * (psi[1] + sec[2])
            plain[0] = plain[0] + at * sec[2]
            scaled[0] = scaled[0] + at * (coeff[1] * sec[2])
            around[0] = around[0] + (at * (sec[1] + sec[3]) + at_side * sec[2])
            mean[1] = mean[1] + 0.5 * (
                along * (psi[1] + sec[2]) + across * ((psi[2] + sec[3]) - (psi[0] + sec[1]))
            )
            plain[1] = plain[1] + (along * sec[2] + across * (sec[3] - sec[1]))
            scaled[1] = scaled[1] + (
                along * (coeff[1] * sec[2]) + across * (coeff[2] * sec[3] - coeff[0] * sec[1])
            )
            around[1] = around[1] + (
                (along * (sec[1] + sec[3]) + across * (sec[4] - sec[0]))
                + (along_side * sec[2] + across_side * (sec[3] - sec[1]))
            )
        row_w = ghost[1, 0, pl.ds(y, 1), :] * jnp.where(x == 1, -weight_x, 0.0)
        row_e = ghost[1, 1, pl.ds(y, 1), :] * jnp.where(x == cols - 2, weight_x, 0.0)
        around[1] = around[1] + (jnp.where(hit_w, row_w, 0.0) + jnp.where(hit_e, row_e, 0.0))
        sums = []
        for i in range(2):
            below = jnp.where(sub_p == 0, 0.0, pltpu.roll(plain[i], 1, 0))
            above = jnp.where(sub_p == planes - 1, 0.0, pltpu.roll(plain[i], parts - 1, 0))
            move = scaled[i] - half_kin * (around[i] + (below + above))
            sums.append(jnp.sum(mean[i] + swap_parts(move), axis=1, keepdims=True))
        return jnp.where(lane_p == slot, sums[0], out_u), jnp.where(lane_p == slot, sums[1], out_d)

    def surface(target, is_now):
        zero = jnp.zeros((parts, 128), f32)
        out_u, out_d = lax.fori_loop(
            0, slots, take if is_now else take_next, (zero, zero), unroll=8
        )
        turned = jnp.transpose(
            jnp.concatenate([out_u, out_d, jnp.zeros((128 - 2 * parts, 128), f32)], axis=0)
        )
        if not is_now:
            target[gy, gx] = (turned[0:4] + pltpu.roll(turned[4:8], 32, 1)) + (
                pltpu.roll(turned[8:12], 64, 1) + pltpu.roll(turned[12:16], 96, 1)
            )
        if is_now:
            packed = jnp.where(lane8 < 64, turned[0:8], pltpu.roll(turned[8:16], 64, 1))
            for slot in range(slots):
                cell = cells_ref[0, 0, slot]
                y = cell // cols
                x = cell - y * cols
                px = spacing * ((gx * cols + x).astype(f32) - (0.5 * cols * x_count - 0.5))
                py = spacing * ((gy * rows + y).astype(f32) - (0.5 * rows * y_count - 0.5))
                base = 64 * (slot // 8) + 2 * parts
                row = sub8 == slot % 8
                packed = jnp.where(row & (lane8 == base), px, packed)
                packed = jnp.where(row & (lane8 == base + 1), py, packed)
            packed = jnp.where(lane8 == 2 * parts + 2, count_ref[0, 0].astype(f32), packed)
            target[column, gy, chip] = packed

    def chip_copy(buf, phase, k, source):
        return pltpu.make_async_remote_copy(
            src_ref=buf.at[column, gy, source],
            dst_ref=buf.at[column, gy, source],
            send_sem=x_send.at[phase, k],
            recv_sem=x_recv.at[phase, k],
            device_id=(wrap(gx + 2 * k, x_count), gy),
            device_id_type=MESH,
        )

    def y_copy(buf, phase, k, source):
        return pltpu.make_async_remote_copy(
            src_ref=buf.at[column, source],
            dst_ref=buf.at[column, source],
            send_sem=y_send.at[phase, k],
            recv_sem=y_recv.at[phase, k],
            device_id=(gx, wrap(gy + k, y_count)),
            device_id_type=MESH,
        )

    def pair_copy(buf, phase, which):
        return pltpu.make_async_remote_copy(
            src_ref=buf.at[which],
            dst_ref=buf.at[which],
            send_sem=x_send.at[phase, 0],
            recv_sem=x_recv.at[phase, 0],
            device_id=(partner, gy),
            device_id_type=MESH,
        )

    def hop_1(buf, phase):
        for k in range(1, chips):
            chip_copy(buf, phase, k, chip).start()

    def hop_2(buf, phase):
        for k in range(1, chips):
            chip_copy(buf, phase, k, wrap(chip - k, chips)).wait_recv()
        for k in range(1, y_count):
            y_copy(buf, phase, k, gy).start()

    def hop_3(buf, phase):
        for k in range(1, y_count):
            y_copy(buf, phase, k, wrap(gy - k, y_count)).wait_recv()
        pair_copy(buf, phase, column).start()

    def hop_end(buf, phase):
        pair_copy(buf, phase, 1 - column).wait_recv()

    def line_copy(k, source):
        return pltpu.make_async_remote_copy(
            src_ref=gather_1.at[gy, source],
            dst_ref=gather_1.at[gy, source],
            send_sem=x_send.at[1, k],
            recv_sem=x_recv.at[1, k],
            device_id=(wrap(gx + k, x_count), gy),
            device_id_type=MESH,
        )

    def sheet_copy(k, source):
        return pltpu.make_async_remote_copy(
            src_ref=gather_1.at[source],
            dst_ref=gather_1.at[source],
            send_sem=y_send.at[1, k],
            recv_sem=y_recv.at[1, k],
            device_id=(gx, wrap(gy + k, y_count)),
            device_id_type=MESH,
        )

    def sends_wait(buf, phase):
        for k in range(1, chips):
            chip_copy(buf, phase, k, chip).wait_send()
        for k in range(1, y_count):
            y_copy(buf, phase, k, gy).wait_send()
        pair_copy(buf, phase, column).wait_send()

    field_1 = field_at(start_time)
    field_2 = field_at(later_time)
    first = lane8 == 0
    last = lane8 == 127

    def edges(stage, p, b):
        at = pl.ds(pl.multiple_of(b * 8, 8), 8)
        edge_w = pltpu.roll(ghost[stage, 0, at, :], (128 - (2 * p + 1)) % 128, 1)
        edge_e = pltpu.roll(ghost[stage, 1, at, :], (127 - 2 * p) % 128, 1)
        return edge_w, edge_e

    def spread(src, p, r0, stage, b):
        rows_b = pl.ds(r0, 8)
        cur = [src[j, p, rows_b, :] for j in range(lane_blocks)]
        right = [pltpu.roll(c, 1, 1) for c in cur]
        left = [pltpu.roll(c, 127, 1) for c in cur]
        if stage == 0:
            edge_w = edge_e = 0.0
        else:
            edge_w, edge_e = edges(1, p, b)
        out = []
        for j in range(lane_blocks):
            up = src[j, p, pl.ds(r0 - 1, 8), :]
            down = src[j, p, pl.ds(r0 + 1, 8), :]
            w = jnp.where(first, edge_w if j == 0 else right[j - 1], right[j])
            e = jnp.where(last, edge_e if j == lane_blocks - 1 else left[j + 1], left[j])
            out.append((up + down) + (w + e))
        return cur, out

    def stage_block(src, stage, b, finish):
        r0 = pl.multiple_of(b * 8 + top, 8)
        rows_b = pl.ds(r0, 8)
        dt = step_dt if stage == 0 else half_dt
        field = field_1 if stage == 0 else field_2
        for z in range(planes):
            found = [spread(src, part * planes + z, r0, stage, b) for part in range(2)]
            shift = dt * (field * spacing * (z - 0.5 * (planes - 1)) + 6.0 * kinetic)
            for j in range(lane_blocks):
                coeff = dt * pot_v[j, z, pl.ds(pl.multiple_of(b * 8, 8), 8), :] + shift
                moves = []
                for part in range(2):
                    cur, beside = found[part]
                    p = part * planes + z
                    total = beside[j]
                    if z > 0:
                        total = total + src[j, p - 1, rows_b, :]
                    if z < planes - 1:
                        total = total + src[j, p + 1, rows_b, :]
                    moves.append(coeff * cur[j] - (dt * kinetic) * total)
                finish(z, rows_b, j, found[0][0][j], found[1][0][j], moves)

    def finish_section(z, rows_b, j, real, imag, moves):
        sec_v[j, z, rows_b, :] = real + moves[1]
        sec_v[j, planes + z, rows_b, :] = imag - moves[0]

    def finish_next(z, rows_b, j, real, imag, moves):
        psi_v[j, z, rows_b, :] = 0.5 * (psi_v[j, z, rows_b, :] + real) + moves[1]
        psi_v[j, planes + z, rows_b, :] = 0.5 * (psi_v[j, planes + z, rows_b, :] + imag) - moves[0]

    def run_section(b, carry):
        stage_block(psi_v, 0, b, finish_section)
        return carry

    def run_next(b, carry):
        stage_block(sec_v, 1, b, finish_next)
        return carry

    def fix_columns(b, carry):
        rows_b = pl.ds(pl.multiple_of(b * 8 + top, 8), 8)
        sides = []
        for p in range(parts):
            other = (p + planes) % parts
            edge_w, edge_e = edges(0, p, b)
            scale = step_dt * kinetic if p < planes else -step_dt * kinetic
            sides.append(
                (
                    other,
                    sec_v[0, other, rows_b, :] + jnp.where(first, scale * edge_w, 0.0),
                    sec_v[lane_blocks - 1, other, rows_b, :] + jnp.where(last, scale * edge_e, 0.0),
                )
            )
        for other, low, high in sides:
            sec_v[0, other, rows_b, :] = low
            sec_v[lane_blocks - 1, other, rows_b, :] = high
        return carry

    surface(gather_0, True)
    hop_1(gather_0, 0)
    clear = jnp.zeros((1, 128), f32)
    for j in range(lane_blocks):
        for p in range(parts):
            psi_v[j, p, top - 1 : top, :] = clear
            psi_v[j, p, top + rows : top + rows + 1, :] = clear
    lax.fori_loop(0, blocks, run_section, 0)
    hop_2(gather_0, 0)

    for copy in halo:
        copy.wait_recv()

    keep_n = jnp.where(gy > 0, 1.0, 0.0).astype(f32)
    keep_s = jnp.where(gy < y_count - 1, 1.0, 0.0).astype(f32)
    keep_w = jnp.where(gx > 0, 1.0, 0.0).astype(f32)
    keep_e = jnp.where(gx < x_count - 1, 1.0, 0.0).astype(f32)

    def height(index):
        return spacing * (index.astype(f32) - 0.5 * (planes - 1))

    corner_cols = []
    for sy, keep_y in enumerate((keep_n, keep_s)):
        for sx, keep_x in enumerate((keep_w, keep_e)):
            lane = 127 if sx == 0 else 0
            corner_cols.append(corner_got[2 * sy + sx][:, lane : lane + 1] * (keep_y * keep_x))
    lane_row = iota((planes, cols), 1)
    sub_row = iota((planes, cols), 0)
    for side, keep in enumerate((keep_n, keep_s)):
        coeff = step_dt * (
            row_got[side, 2 * parts : 2 * parts + planes, :] + field_1 * height(sub_row) + 6.0 * kinetic
        )
        nears = []
        moves = []
        for part in range(2):
            sl = slice(part * planes, (part + 1) * planes)
            near = row_got[side, sl, :] * keep
            far = row_got[side, parts + part * planes : parts + (part + 1) * planes, :] * keep
            own = row_msg[side, sl, :]
            left = jnp.where(lane_row == 0, corner_cols[2 * side][sl], pltpu.roll(near, 1, 1))
            right = jnp.where(lane_row == cols - 1, corner_cols[2 * side + 1][sl], pltpu.roll(near, cols - 1, 1))
            below = jnp.where(sub_row == 0, 0.0, pltpu.roll(near, 1, 0))
            above = jnp.where(sub_row == planes - 1, 0.0, pltpu.roll(near, planes - 1, 0))
            beside = (far + own) + (left + right) + (below + above)
            nears.append(near)
            moves.append(coeff * near - (step_dt * kinetic) * beside)
        ghost_rows = (nears[0] + moves[1]) * keep, (nears[1] - moves[0]) * keep
        at = top - 1 if side == 0 else top + rows
        edge = top if side == 0 else top + rows - 1
        for part in range(2):
            for z in range(planes):
                for j in range(lane_blocks):
                    sl = slice(128 * j, 128 * j + 128)
                    p = part * planes + z
                    sec_v[j, p, at : at + 1, :] = ghost_rows[part][z : z + 1, sl]
                    share = (step_dt * kinetic) * nears[1 - part][z : z + 1, sl]
                    old = sec_v[j, p, edge : edge + 1, :]
                    sec_v[j, p, edge : edge + 1, :] = old - share if part == 0 else old + share

    lane_c = iota((rows, 128), 1)
    sub_c = iota((rows, 128), 0)
    diag_lane = iota((parts, 128), 1)
    diag_sub = iota((parts, 128), 0)
    plane_c = (lane_c % (2 * planes)) // 2
    for side, keep in enumerate((keep_w, keep_e)):
        got = col_got[side] * keep
        mine = col_msg[side]
        inner = 1 if side == 0 else 127
        odd = 1 if side == 0 else 0
        hit = diag_lane == 2 * diag_sub + odd
        ends = [
            jnp.sum(jnp.where(hit, corner_cols[2 * sy + side], 0.0), axis=0, keepdims=True)
            for sy in range(2)
        ]
        upper = jnp.where(sub_c == 0, ends[0], pltpu.roll(got, 1, 0))
        lower = jnp.where(sub_c == rows - 1, ends[1], pltpu.roll(got, rows - 1, 0))
        below = jnp.where(plane_c == 0, 0.0, pltpu.roll(got, 2, 1))
        above = jnp.where(plane_c == planes - 1, 0.0, pltpu.roll(got, 126, 1))
        beside = (
            (pltpu.roll(got, inner, 1) + pltpu.roll(mine, inner, 1)) + (upper + lower) + (below + above)
        )
        volts = pltpu.roll(got, 64, 1)
        volts = jnp.where(lane_c < 2 * planes, volts, pltpu.roll(volts, 2 * planes, 1))
        coeff = step_dt * (volts + field_1 * height(plane_c) + 6.0 * kinetic)
        move = coeff * got - (step_dt * kinetic) * beside
        ghost[0, side] = got
        ghost[1, side] = (
            got
            + jnp.where(
                lane_c < 2 * planes, pltpu.roll(move, 128 - 2 * planes, 1), -pltpu.roll(move, 2 * planes, 1)
            )
        ) * keep

    lax.fori_loop(0, blocks, fix_columns, 0, unroll=2)
    surface(gather_1, False)
    for k in range(1, x_count):
        line_copy(k, gx).start()
    stores = []
    pieces = 4
    per = blocks // pieces
    for q in range(pieces):
        lax.fori_loop(q * per, (q + 1) * per, run_next, 0)
        for j in range(lane_blocks):
            stores.append(
                pltpu.make_async_copy(
                    psi_v.at[j, :, top + 8 * per * q : top + 8 * per * (q + 1), :],
                    next_hbm.at[:, 8 * per * q : 8 * per * (q + 1), 128 * j : 128 * j + 128],
                    store_sem.at[q, j],
                )
            )
            stores[-1].start()
        if q == 0:
            for k in range(1, x_count):
                line_copy(k, wrap(gx - k, x_count)).wait_recv()
            for k in range(1, y_count):
                sheet_copy(k, gy).start()
            hop_3(gather_0, 0)
    hop_end(gather_0, 0)

    def count_row(i, total):
        for k in range(x_count):
            got = gather_0[i // (y_count // 2), lax.rem(i, y_count // 2) * 2 + k // chips, k % chips]
            total = jnp.where(lane8 == i * x_count + k, got[:, 2 * parts + 2 : 2 * parts + 3], total)
        return total

    live_ref[...] = lax.fori_loop(0, y_count, count_row, jnp.zeros((8, 128), f32))
    for copy in halo:
        copy.wait_send()
    for copy in stores:
        copy.wait()
    for k in range(1, y_count):
        sheet_copy(k, wrap(gy - k, y_count)).wait_recv()
    sends_wait(gather_0, 0)
    for k in range(1, x_count):
        line_copy(k, gx).wait_send()
    for k in range(1, y_count):
        sheet_copy(k, gy).wait_send()


def turns(phase):
    quarter = jnp.floor(phase * 0.6366197723675814 + 0.5)
    rest = phase - quarter * 1.5703125
    rest = rest - quarter * 4.83751296997e-4
    rest = rest - quarter * 7.5497899548918821e-8
    square = rest * rest
    sine = rest + rest * square * (
        -1.6666654611e-1 + square * (8.3321608736e-3 + square * -1.9515295891e-4)
    )
    cosine = (
        1.0
        - 0.5 * square
        + square * square * (4.166664568298827e-2 + square * (-1.388731625493765e-3 + square * 2.443315711809948e-5))
    )
    which = quarter.astype(jnp.int32)
    swap = (which & 1) == 1
    sin_out = jnp.where(swap, cosine, sine)
    cos_out = jnp.where(swap, sine, cosine)
    sin_out = jnp.where((which & 2) == 2, -sin_out, sin_out)
    cos_out = jnp.where(((which + 1) & 2) == 2, -cos_out, cos_out)
    return cos_out, sin_out


def flux_kernel(
    x_count,
    y_count,
    live_ref,
    count_ref,
    order_ref,
    gather_0,
    gather_1,
    weight_ref,
    amp_ref,
    tmp_hbm,
    next_hbm,
    out_ref,
    comp_0,
    comp_1,
    total,
    held,
    fetch_sem,
    copy_sem,
):
    copies = []
    parts = tmp_hbm.shape[0]
    quarter = parts // 4
    for q in range(4):
        sl = slice(q * quarter, (q + 1) * quarter)
        fetch = pltpu.make_async_copy(tmp_hbm.at[sl], held.at[sl], fetch_sem.at[q])
        fetch.start()
        copies.append((fetch, pltpu.make_async_copy(held.at[sl], next_hbm.at[sl], copy_sem.at[q])))
    me = lax.axis_index("gx") * y_count + lax.axis_index("gy")
    groups = count_ref.shape[0]
    slots = amp_ref.shape[0]
    features = weight_ref.shape[1] // 8
    feature = iota((128, 128), 1) < features

    def offset(i, at):
        return at + jnp.where(i < me, count_ref[i], 0)

    own_start = lax.fori_loop(0, groups, offset, 0, unroll=8)
    own_count = count_ref[me]
    waves = []
    for s in range(slots):
        plane = order_ref[jnp.minimum(own_start + s, groups - 1)]
        waves.append((plane.astype(f32) - 0.5 * (groups - 1)) * (k_span / groups))

    tiles = x_count * y_count
    chips = x_count // 2

    def gather_tile(t, n):
        c = live_ref[0, t].astype(jnp.int32)
        at = pl.ds(pl.multiple_of(t * 8, 8), 8)
        block_0 = gather_0[at, :]
        half, row, chip = t // (tiles // 2), (t // chips) % y_count, t % chips
        block_1 = gather_1[row * x_count + 2 * chip + half]
        comp_0[pl.ds(n, 8), :] = block_0
        comp_1[pl.ds(n, 4), :] = block_1
        comp_1[pl.ds(n + 4, 4), :] = pltpu.roll(block_1, 96, 1)
        n = n + jnp.minimum(c, 8)
        comp_0[pl.ds(n, 8), :] = pltpu.roll(block_0, 64, 1)
        comp_1[pl.ds(n, 4), :] = pltpu.roll(block_1, 64, 1)
        comp_1[pl.ds(n + 4, 4), :] = pltpu.roll(block_1, 32, 1)
        return n + jnp.maximum(c - 8, 0)

    live = lax.fori_loop(0, x_count * y_count, gather_tile, 0, unroll=8)

    def clear(i, carry):
        to = pl.ds(live + i * 8, 8)
        comp_0[to, :] = jnp.zeros((8, 128), f32)
        comp_1[to, :] = jnp.zeros((8, 128), f32)
        return carry

    lax.fori_loop(0, 16, clear, 0)
    total[...] = jnp.zeros_like(total)
    kx = (iota((128, 128), 0).astype(f32) - 63.5) * (k_span / 128)
    sub8 = iota((8, 128), 0)
    ky = jnp.zeros((8, 128), f32)
    for s in range(slots):
        ky = jnp.where(sub8 // 2 == s, waves[s], ky)
    moment8 = jnp.where(sub8 % 2 == 0, start_time, later_time).astype(f32)

    def chunk(c, carry):
        at = pl.ds(pl.multiple_of(c * 128, 128), 128)
        rows = (comp_0[at, :], comp_1[at, :])
        place = jnp.transpose(rows[0])
        px, py = place[features : features + 1, :], place[features + 1 : features + 2, :]
        col_x, col_y = rows[0][:, features : features + 1], rows[0][:, features + 1 : features + 2]
        square = col_x * col_x + col_y * col_y
        radius = jnp.sqrt(jnp.where(square > 0.0, square, 1.0))
        nx, ny = col_x / radius, col_y / radius
        right = []
        left = []
        for t, moment in enumerate((start_time, later_time)):
            raw = jnp.where(feature, rows[t], 0.0)
            high = raw.astype(jnp.bfloat16).astype(f32)
            mid = (raw - high).astype(jnp.bfloat16).astype(f32)
            low = (raw - high) - mid
            side = (
                (high + pltpu.roll(mid, features, 1))
                + (pltpu.roll(low, 2 * features, 1) + pltpu.roll(high, 3 * features, 1))
            ).astype(jnp.bfloat16)
            modes = jnp.dot(
                jnp.concatenate([side, side], axis=1), weight_ref[t], preferred_element_type=f32
            )
            ur, ui, dr, di = (modes[:, 128 * i : 128 * i + 128] for i in range(4))
            right.append(
                jnp.concatenate([nx * ur, ny * ur, dr, nx * ui, ny * ui, di], axis=1).astype(jnp.bfloat16)
            )
            left.append(turns(0.5 * kx * kx * moment - kx * px))
        right = jnp.concatenate(right, axis=0)
        rot_cos, rot_sin = turns(0.5 * ky * ky * moment8 - ky * py)

        for first in range(0, slots, 2):

            @pl.when(first < own_count)
            def _():
                sides = []
                pair = range(first, min(first + 2, slots))
                for s in pair:
                    real = []
                    imag = []
                    for t in range(2):
                        bc, bs = rot_cos[2 * s + t : 2 * s + t + 1], rot_sin[2 * s + t : 2 * s + t + 1]
                        ac, as_ = left[t]
                        real.append((ac * bc - as_ * bs).astype(jnp.bfloat16))
                        imag.append((ac * bs + as_ * bc).astype(jnp.bfloat16))
                    sides.append(jnp.concatenate(real, axis=1))
                    sides.append(jnp.concatenate(imag, axis=1))
                prod = jnp.dot(jnp.concatenate(sides, axis=0), right, preferred_element_type=f32)
                for i, s in enumerate(pair):
                    m = [prod[256 * i : 256 * i + 128, 128 * k : 128 * k + 128] for k in range(6)]
                    w = [prod[256 * i + 128 : 256 * i + 256, 128 * k : 128 * k + 128] for k in range(6)]
                    hy = waves[s]
                    total[s, 0] += kx * (m[0] - w[3]) + hy * (m[1] - w[4]) + (m[5] + w[2])
                    total[s, 1] += kx * (m[3] + w[0]) + hy * (m[4] + w[1]) - (m[2] - w[5])

        return carry

    chunks = (live + 127) // 128
    lax.fori_loop(0, jnp.minimum(chunks, 1), chunk, 0)
    for fetch, copy in copies:
        fetch.wait()
        copy.start()
    lax.fori_loop(1, chunks, chunk, 0)
    for s in range(slots):
        for part in range(2):
            sl = pl.ds(part, 128, stride=2)
            inc = jnp.where(s < own_count, (0.5 * flux_weight) * total[s, part], 0.0)
            out_ref[s, sl, :] = amp_ref[s, sl, :] + inc
    for fetch, copy in copies:
        copy.wait()


def shards(psi_now, potential, surf_cells, surf_count, block_count, block_order, amplitude):
    x_count = lax.axis_size("gx")
    y_count = lax.axis_size("gy")
    planes, rows, cols = potential.shape
    parts = 2 * planes
    slots = surf_cells.shape[2]
    own, modes_x, _, modes_z = amplitude.shape
    any_spec = pl.BlockSpec(memory_space=pl.ANY)
    vmem = pl.BlockSpec(memory_space=pltpu.VMEM)
    smem = pl.BlockSpec(memory_space=pltpu.SMEM)
    hbm = pl.BlockSpec(memory_space=pltpu.HBM)
    dma = pltpu.SemaphoreType.DMA
    gathered = jax.ShapeDtypeStruct((2, y_count, x_count // 2, 8, 128), f32)
    sheet = jax.ShapeDtypeStruct((y_count, x_count, 4, 128), f32)
    field = jax.ShapeDtypeStruct((parts, rows, cols), f32)
    staged, gather_0, gather_1, live = pl.pallas_call(
        functools.partial(step_kernel, x_count, y_count),
        out_shape=(field, gathered, sheet, jax.ShapeDtypeStruct((8, 128), f32)),
        in_specs=[smem, smem, hbm, hbm],
        out_specs=(any_spec, vmem, vmem, vmem),
        scratch_shapes=[
            pltpu.VMEM((cols // 128, parts, rows + 16, 128), f32),
            pltpu.VMEM((cols // 128, parts, rows + 16, 128), f32),
            pltpu.VMEM((cols // 128, planes, rows, 128), f32),
            pltpu.VMEM((2, 2 * parts + planes, cols), f32),
            pltpu.VMEM((2, 2 * parts + planes, cols), f32),
            pltpu.VMEM((2, rows, 128), f32),
            pltpu.VMEM((2, rows, 128), f32),
            pltpu.VMEM((4, parts, 128), f32),
            pltpu.VMEM((2, 2, rows, 128), f32),
            dma((2, cols // 128)),
            dma((4, cols // 128)),
            dma((2,)),
            dma((2,)),
            dma((2,)),
            dma((2,)),
            dma((4,)),
            dma((4,)),
            dma((2, x_count)),
            dma((2, x_count)),
            dma((2, y_count)),
            dma((2, y_count)),
        ],
        compiler_params=pltpu.CompilerParams(
            collective_id=0, has_side_effects=True, vmem_limit_bytes=52 * 1024 * 1024
        ),
        name="step",
    )(
        surf_cells,
        surf_count,
        psi_now.reshape(parts, rows, cols),
        potential,
    )
    tiles = x_count * y_count
    psi_next, amplitude_next = pl.pallas_call(
        functools.partial(flux_kernel, x_count, y_count),
        out_shape=(field, jax.ShapeDtypeStruct((own, 2 * modes_x, modes_z), f32)),
        in_specs=[smem, smem, smem, vmem, vmem, vmem, vmem, any_spec],
        out_specs=(any_spec, vmem),
        scratch_shapes=[
            pltpu.VMEM((slots * tiles + 144, 128), f32),
            pltpu.VMEM((slots * tiles + 144, 128), f32),
            pltpu.VMEM((own, 2, modes_x, modes_z), f32),
            pltpu.VMEM((parts, rows, cols), f32),
            dma((4,)),
            dma((4,)),
        ],
        compiler_params=pltpu.CompilerParams(vmem_limit_bytes=52 * 1024 * 1024),
        name="flux",
    )(
        live,
        block_count,
        block_order,
        gather_0.reshape(tiles * 8, 128),
        gather_1.reshape(tiles, 4, 128),
        jnp.asarray(mode_weights(planes, modes_z)),
        amplitude.reshape(own, 2 * modes_x, modes_z),
        staged,
    )
    return psi_next.reshape(psi_now.shape), amplitude_next.reshape(amplitude.shape)


def solution(mesh):
    return jax.shard_map(
        shards,
        mesh=mesh,
        in_specs=(
            P(None, None, "gy", "gx"),
            P(None, "gy", "gx"),
            P("gy", "gx", None),
            P("gy", "gx"),
            P(),
            P(),
            P(("gx", "gy"), None, None, None),
        ),
        out_specs=(P(None, None, "gy", "gx"), P(("gx", "gy"), None, None, None)),
        check_vma=False,
    )
```

```python
import functools
import math

import jax
import jax.numpy as jnp
import numpy as np
from jax import lax
from jax.experimental import pallas as pl
from jax.experimental.pallas import tpu as pltpu
from jax.sharding import PartitionSpec as P

spacing = 0.2
kinetic = 12.5
step_dt = 0.016
half_dt = 0.008
start_time = 100.0
later_time = start_time + step_dt
field_peak = 0.05
field_freq = 0.057
k_span = 4.0
flux_weight = 0.0078125
MESH = pl.DeviceIdType.MESH
f32 = jnp.float32


def field_at(moment):
    return field_peak * math.sin(field_freq * moment)


def drift_at(moment):
    return field_peak / (field_freq * field_freq) * math.sin(field_freq * moment)


def mode_weights(planes, modes):
    wave = ((np.arange(modes) - 0.5 * (modes - 1)) * (k_span / modes)).astype(np.float32)
    height = np.float32(spacing) * (np.arange(planes) - 0.5 * (planes - 1)).astype(np.float32)
    out = np.zeros((2, 4 * planes, 4 * modes), np.float32)
    for t, moment in enumerate((start_time, later_time)):
        phase = (
            np.float32(0.5) * wave * wave * np.float32(moment) + wave * np.float32(drift_at(moment))
        )[None, :] - wave[None, :] * height[:, None]
        cos = np.cos(phase.astype(np.float64)).astype(np.float32)
        sin = np.sin(phase.astype(np.float64)).astype(np.float32)
        block = np.block([[cos, sin], [-sin, cos]])
        out[t, : 2 * planes, : 2 * modes] = block
        out[t, 2 * planes :, 2 * modes :] = block
    high = out.astype(jnp.bfloat16).astype(np.float32)
    mid = (out - high).astype(jnp.bfloat16).astype(np.float32)
    low = out - high - mid
    none = np.zeros_like(out)
    return np.concatenate([high, high, high, mid, low, mid, none, none], axis=1).astype(jnp.bfloat16)


def iota(shape, dim):
    return lax.broadcasted_iota(jnp.int32, shape, dim)


def step_kernel(
    x_count,
    y_count,
    cells_ref,
    count_ref,
    psi_hbm,
    pot_hbm,
    next_hbm,
    gather_0,
    gather_1,
    live_ref,
    psi_v,
    sec_v,
    pot_v,
    row_msg,
    row_got,
    col_msg,
    col_got,
    corner_got,
    ghost,
    load_sem,
    store_sem,
    row_send,
    row_recv,
    col_send,
    col_recv,
    corner_send,
    corner_recv,
    x_send,
    x_recv,
    y_send,
    y_recv,
):
    gx = lax.axis_index("gx")
    gy = lax.axis_index("gy")
    parts, rows, cols = psi_hbm.shape
    planes = parts // 2
    blocks = rows // 8
    lane_blocks = cols // 128
    top = 8

    def wrap(value, count):
        return lax.rem(value + count, count)

    west, east = wrap(gx - 1, x_count), wrap(gx + 1, x_count)
    north, south = wrap(gy - 1, y_count), wrap(gy + 1, y_count)
    loads = []
    halves = 2
    part_rows = rows // halves
    load_parts = [(j, h) for h in range(halves) for j in (0, lane_blocks - 1)]
    load_parts += [(j, h) for j in range(1, lane_blocks - 1) for h in range(halves)]
    for j, h in load_parts:
        sl = slice(128 * j, 128 * j + 128)
        lo, hi = h * part_rows, (h + 1) * part_rows
        loads.append(
            pltpu.make_async_copy(
                psi_hbm.at[:, lo:hi, sl], psi_v.at[j, :, top + lo : top + hi, :], load_sem.at[0, h, j]
            )
        )
        loads.append(
            pltpu.make_async_copy(pot_hbm.at[:, lo:hi, sl], pot_v.at[j, :, lo:hi, :], load_sem.at[1, h, j])
        )
    for copy in loads:
        copy.start()

    barrier = pltpu.get_barrier_semaphore()
    partner = gx + 1 - 2 * lax.rem(gx, 2)
    column = lax.rem(gx, 2)
    chip = gx // 2
    chips = x_count // 2
    signals = 0
    for k in range(1, x_count):
        pl.semaphore_signal(barrier, inc=1, device_id=(wrap(gx + k, x_count), gy), device_id_type=MESH)
        signals += 1
    for k in range(1, y_count):
        pl.semaphore_signal(barrier, inc=1, device_id=(gx, wrap(gy + k, y_count)), device_id_type=MESH)
        signals += 1
    for sx in (west, east):
        for sy in (north, south):
            pl.semaphore_signal(barrier, inc=1, device_id=(sx, sy), device_id_type=MESH)
            signals += 1


    lane8 = iota((8, 128), 1)
    sub8 = iota((8, 128), 0)

    def pack(b, carry):
        r0 = pl.multiple_of(b * 8, 8)
        for side in range(2):
            j = 0 if side == 0 else lane_blocks - 1
            base = 0 if side == 0 else 2
            moved = [
                (p, pltpu.roll(psi_v[j, p, pl.ds(r0 + top, 8), :], (2 * p + base) % 128, 1))
                for p in range(parts)
            ] + [
                (32 + z, pltpu.roll(pot_v[j, z, pl.ds(r0, 8), :], (64 + 2 * z + base) % 128, 1))
                for z in range(planes)
            ]
            while len(moved) > 1:
                joined = []
                for i in range(0, len(moved) - 1, 2):
                    (at_a, part_a), (at_b, part_b) = moved[i], moved[i + 1]
                    joined.append((at_a, jnp.where(lane8 < 2 * at_b, part_a, part_b)))
                if len(moved) % 2:
                    joined.append(moved[-1])
                moved = joined
            packed = moved[0][1]
            col_msg[side, pl.ds(r0, 8), :] = packed
        return carry

    for h in range(halves):
        for copy in loads[4 * h : 4 * h + 4]:
            copy.wait()
        lax.fori_loop(h * (blocks // halves), (h + 1) * (blocks // halves), pack, 0, unroll=4)

    pl.semaphore_wait(barrier, signals)

    halo = []
    for side, target in enumerate((west, east)):
        halo.append(
            pltpu.make_async_remote_copy(
                src_ref=col_msg.at[side],
                dst_ref=col_got.at[1 - side],
                send_sem=col_send.at[side],
                recv_sem=col_recv.at[1 - side],
                device_id=(target, gy),
                device_id_type=MESH,
            )
        )
    for copy in halo:
        copy.start()
    for copy in loads[4 * halves :]:
        copy.wait()
    for side, (near, far) in enumerate(((top, top + 1), (top + rows - 1, top + rows - 2))):
        for j in range(lane_blocks):
            sl = slice(128 * j, 128 * j + 128)
            for p in range(parts):
                row_msg[side, p : p + 1, sl] = psi_v[j, p, near : near + 1, :]
                row_msg[side, parts + p : parts + p + 1, sl] = psi_v[j, p, far : far + 1, :]
            for z in range(planes):
                row_msg[side, 2 * parts + z : 2 * parts + z + 1, sl] = pot_v[
                    j, z, near - top : near - top + 1, :
                ]

    for side, target in enumerate((north, south)):
        halo.append(
            pltpu.make_async_remote_copy(
                src_ref=row_msg.at[side],
                dst_ref=row_got.at[1 - side],
                send_sem=row_send.at[side],
                recv_sem=row_recv.at[1 - side],
                device_id=(gx, target),
                device_id_type=MESH,
            )
        )
    for sy, ty in enumerate((north, south)):
        for sx, tx in enumerate((west, east)):
            lo = 0 if sx == 0 else cols - 128
            halo.append(
                pltpu.make_async_remote_copy(
                    src_ref=row_msg.at[sy, 0:parts, lo : lo + 128],
                    dst_ref=corner_got.at[2 * (1 - sy) + 1 - sx],
                    send_sem=corner_send.at[2 * sy + sx],
                    recv_sem=corner_recv.at[2 * (1 - sy) + 1 - sx],
                    device_id=(tx, ty),
                    device_id_type=MESH,
                )
            )
    for copy in halo[2:]:
        copy.start()

    lane_p = iota((parts, 128), 1)

    def take(slot, carry):
        out_u, out_d = carry
        cell = cells_ref[0, 0, slot]
        y = cell // cols
        x = cell - y * cols
        alive = jnp.where(slot < count_ref[0, 0], 1.0, 0.0).astype(f32)
        px = jnp.full((1, 128), spacing * ((gx * cols + x).astype(f32) - (0.5 * cols * x_count - 0.5)), f32)
        py = jnp.full((1, 128), spacing * ((gy * rows + y).astype(f32) - (0.5 * rows * y_count - 0.5)), f32)
        radius = jnp.sqrt(px * px + py * py)
        weight_x = px / radius / (2.0 * spacing) * alive
        weight_y = py / radius / (2.0 * spacing) * alive
        total_u = jnp.zeros((parts, 128), f32)
        total_d = jnp.zeros((parts, 128), f32)
        low = jnp.minimum(jnp.maximum(x - 1, 0) // 128, max(lane_blocks - 2, 0))
        for j in [low + i for i in range(min(lane_blocks, 2))]:
            lane = iota((1, 128), 1) + 128 * j
            at = jnp.where(lane == x, alive, 0.0)
            along = jnp.where(lane == x + 1, weight_x, 0.0) - jnp.where(lane == x - 1, weight_x, 0.0)
            across = jnp.where(lane == x, weight_y, 0.0)
            flat = psi_v.at[j].reshape(parts * (rows + 16), 128)
            middle = flat[pl.ds(y + top, parts, stride=rows + 16), :]
            after = flat[pl.ds(y + top + 1, parts, stride=rows + 16), :]
            before = flat[pl.ds(y + top - 1, parts, stride=rows + 16), :]
            total_u = total_u + middle * at
            total_d = total_d + (middle * along + (after - before) * across)
        out_u = jnp.where(lane_p == slot, jnp.sum(total_u, axis=1, keepdims=True), out_u)
        out_d = jnp.where(lane_p == slot, jnp.sum(total_d, axis=1, keepdims=True), out_d)
        return out_u, out_d

    slots = cells_ref.shape[2]

    half_kin = half_dt * kinetic

    def swap_parts(value):
        return jnp.concatenate([value[planes:], -value[:planes]], axis=0)

    sub_p = lax.rem(iota((parts, 128), 0), planes)
    hit_w = lane_p == 2 * iota((parts, 128), 0) + 1
    hit_e = lane_p == 2 * iota((parts, 128), 0)

    def take_next(slot, carry):
        out_u, out_d = carry
        cell = cells_ref[0, 0, slot]
        row = cell // cols
        x = cell - row * cols
        y = jnp.maximum(row, 1)
        alive = jnp.where(slot < count_ref[0, 0], 1.0, 0.0).astype(f32)
        px = jnp.full((1, 128), spacing * ((gx * cols + x).astype(f32) - (0.5 * cols * x_count - 0.5)), f32)
        py = jnp.full((1, 128), spacing * ((gy * rows + y).astype(f32) - (0.5 * rows * y_count - 0.5)), f32)
        radius = jnp.sqrt(px * px + py * py)
        weight_x = px / radius / (2.0 * spacing) * alive
        weight_y = py / radius / (2.0 * spacing) * alive
        shift = half_dt * (
            field_2 * (spacing * (sub_p.astype(f32) - 0.5 * (planes - 1))) + 6.0 * kinetic
        )
        zero = jnp.zeros((parts, 128), f32)
        mean = [zero, zero]
        plain = [zero, zero]
        scaled = [zero, zero]
        around = [zero, zero]
        low = jnp.minimum(jnp.maximum(x - 2, 0) // 128, max(lane_blocks - 2, 0))
        for j in [low + i for i in range(min(lane_blocks, 2))]:
            lane = iota((1, 128), 1) + 128 * j
            at = jnp.where(lane == x, alive, 0.0)
            at_side = jnp.where((lane == x + 1) | (lane == x - 1), alive, 0.0)
            along = jnp.where(lane == x + 1, weight_x, 0.0) - jnp.where(lane == x - 1, weight_x, 0.0)
            along_side = jnp.where(lane == x + 2, weight_x, 0.0) - jnp.where(
                lane == x - 2, weight_x, 0.0
            )
            across = jnp.where(lane == x, weight_y, 0.0)
            across_side = jnp.where((lane == x + 1) | (lane == x - 1), weight_y, 0.0)
            flat_s = sec_v.at[j].reshape(parts * (rows + 16), 128)
            flat_f = psi_v.at[j].reshape(parts * (rows + 16), 128)
            flat_p = pot_v.at[j].reshape(planes * rows, 128)
            sec = [flat_s[pl.ds(y + top + r, parts, stride=rows + 16), :] for r in range(-2, 3)]
            psi = [flat_f[pl.ds(y + top + r, parts, stride=rows + 16), :] for r in range(-1, 2)]
            pot = [flat_p[pl.ds(y + r, planes, stride=rows), :] for r in range(-1, 2)]
            coeff = [jnp.concatenate([v, v], axis=0) * half_dt + shift for v in pot]
            mean[0] = mean[0] + (0.5 * at) * (psi[1] + sec[2])
            plain[0] = plain[0] + at * sec[2]
            scaled[0] = scaled[0] + at * (coeff[1] * sec[2])
            around[0] = around[0] + (at * (sec[1] + sec[3]) + at_side * sec[2])
            mean[1] = mean[1] + 0.5 * (
                along * (psi[1] + sec[2]) + across * ((psi[2] + sec[3]) - (psi[0] + sec[1]))
            )
            plain[1] = plain[1] + (along * sec[2] + across * (sec[3] - sec[1]))
            scaled[1] = scaled[1] + (
                along * (coeff[1] * sec[2]) + across * (coeff[2] * sec[3] - coeff[0] * sec[1])
            )
            around[1] = around[1] + (
                (along * (sec[1] + sec[3]) + across * (sec[4] - sec[0]))
                + (along_side * sec[2] + across_side * (sec[3] - sec[1]))
            )
        row_w = ghost[1, 0, pl.ds(y, 1), :] * jnp.where(x == 1, -weight_x, 0.0)
        row_e = ghost[1, 1, pl.ds(y, 1), :] * jnp.where(x == cols - 2, weight_x, 0.0)
        around[1] = around[1] + (jnp.where(hit_w, row_w, 0.0) + jnp.where(hit_e, row_e, 0.0))
        sums = []
        for i in range(2):
            below = jnp.where(sub_p == 0, 0.0, pltpu.roll(plain[i], 1, 0))
            above = jnp.where(sub_p == planes - 1, 0.0, pltpu.roll(plain[i], parts - 1, 0))
            move = scaled[i] - half_kin * (around[i] + (below + above))
            sums.append(jnp.sum(mean[i] + swap_parts(move), axis=1, keepdims=True))
        return jnp.where(lane_p == slot, sums[0], out_u), jnp.where(lane_p == slot, sums[1], out_d)

    def surface(target, is_now):
        zero = jnp.zeros((parts, 128), f32)
        out_u, out_d = lax.fori_loop(
            0, slots, take if is_now else take_next, (zero, zero), unroll=8
        )
        turned = jnp.transpose(
            jnp.concatenate([out_u, out_d, jnp.zeros((128 - 2 * parts, 128), f32)], axis=0)
        )
        if not is_now:
            target[gy, gx] = (turned[0:4] + pltpu.roll(turned[4:8], 32, 1)) + (
                pltpu.roll(turned[8:12], 64, 1) + pltpu.roll(turned[12:16], 96, 1)
            )
        if is_now:
            packed = jnp.where(lane8 < 64, turned[0:8], pltpu.roll(turned[8:16], 64, 1))
            for slot in range(slots):
                cell = cells_ref[0, 0, slot]
                y = cell // cols
                x = cell - y * cols
                px = spacing * ((gx * cols + x).astype(f32) - (0.5 * cols * x_count - 0.5))
                py = spacing * ((gy * rows + y).astype(f32) - (0.5 * rows * y_count - 0.5))
                base = 64 * (slot // 8) + 2 * parts
                row = sub8 == slot % 8
                packed = jnp.where(row & (lane8 == base), px, packed)
                packed = jnp.where(row & (lane8 == base + 1), py, packed)
            packed = jnp.where(lane8 == 2 * parts + 2, count_ref[0, 0].astype(f32), packed)
            target[column, gy, chip] = packed

    def chip_copy(buf, phase, k, source):
        return pltpu.make_async_remote_copy(
            src_ref=buf.at[column, gy, source],
            dst_ref=buf.at[column, gy, source],
            send_sem=x_send.at[phase, k],
            recv_sem=x_recv.at[phase, k],
            device_id=(wrap(gx + 2 * k, x_count), gy),
            device_id_type=MESH,
        )

    def y_copy(buf, phase, k, source):
        return pltpu.make_async_remote_copy(
            src_ref=buf.at[column, source],
            dst_ref=buf.at[column, source],
            send_sem=y_send.at[phase, k],
            recv_sem=y_recv.at[phase, k],
            device_id=(gx, wrap(gy + k, y_count)),
            device_id_type=MESH,
        )

    def pair_copy(buf, phase, which):
        return pltpu.make_async_remote_copy(
            src_ref=buf.at[which],
            dst_ref=buf.at[which],
            send_sem=x_send.at[phase, 0],
            recv_sem=x_recv.at[phase, 0],
            device_id=(partner, gy),
            device_id_type=MESH,
        )

    def hop_1(buf, phase):
        for k in range(1, chips):
            chip_copy(buf, phase, k, chip).start()

    def hop_2(buf, phase):
        for k in range(1, chips):
            chip_copy(buf, phase, k, wrap(chip - k, chips)).wait_recv()
        for k in range(1, y_count):
            y_copy(buf, phase, k, gy).start()

    def hop_3(buf, phase):
        for k in range(1, y_count):
            y_copy(buf, phase, k, wrap(gy - k, y_count)).wait_recv()
        pair_copy(buf, phase, column).start()

    def hop_end(buf, phase):
        pair_copy(buf, phase, 1 - column).wait_recv()

    def line_copy(k, source):
        return pltpu.make_async_remote_copy(
            src_ref=gather_1.at[gy, source],
            dst_ref=gather_1.at[gy, source],
            send_sem=x_send.at[1, k],
            recv_sem=x_recv.at[1, k],
            device_id=(wrap(gx + k, x_count), gy),
            device_id_type=MESH,
        )

    def sheet_copy(k, source):
        return pltpu.make_async_remote_copy(
            src_ref=gather_1.at[source],
            dst_ref=gather_1.at[source],
            send_sem=y_send.at[1, k],
            recv_sem=y_recv.at[1, k],
            device_id=(gx, wrap(gy + k, y_count)),
            device_id_type=MESH,
        )

    def sends_wait(buf, phase):
        for k in range(1, chips):
            chip_copy(buf, phase, k, chip).wait_send()
        for k in range(1, y_count):
            y_copy(buf, phase, k, gy).wait_send()
        pair_copy(buf, phase, column).wait_send()

    field_1 = field_at(start_time)
    field_2 = field_at(later_time)
    first = lane8 == 0
    last = lane8 == 127

    def edges(stage, p, b):
        at = pl.ds(pl.multiple_of(b * 8, 8), 8)
        edge_w = pltpu.roll(ghost[stage, 0, at, :], (128 - (2 * p + 1)) % 128, 1)
        edge_e = pltpu.roll(ghost[stage, 1, at, :], (127 - 2 * p) % 128, 1)
        return edge_w, edge_e

    def spread(src, p, r0, stage, b):
        rows_b = pl.ds(r0, 8)
        cur = [src[j, p, rows_b, :] for j in range(lane_blocks)]
        right = [pltpu.roll(c, 1, 1) for c in cur]
        left = [pltpu.roll(c, 127, 1) for c in cur]
        if stage == 0:
            edge_w = edge_e = 0.0
        else:
            edge_w, edge_e = edges(1, p, b)
        out = []
        for j in range(lane_blocks):
            up = src[j, p, pl.ds(r0 - 1, 8), :]
            down = src[j, p, pl.ds(r0 + 1, 8), :]
            w = jnp.where(first, edge_w if j == 0 else right[j - 1], right[j])
            e = jnp.where(last, edge_e if j == lane_blocks - 1 else left[j + 1], left[j])
            out.append((up + down) + (w + e))
        return cur, out

    def stage_block(src, stage, b, finish):
        r0 = pl.multiple_of(b * 8 + top, 8)
        rows_b = pl.ds(r0, 8)
        dt = step_dt if stage == 0 else half_dt
        field = field_1 if stage == 0 else field_2
        for z in range(planes):
            found = [spread(src, part * planes + z, r0, stage, b) for part in range(2)]
            shift = dt * (field * spacing * (z - 0.5 * (planes - 1)) + 6.0 * kinetic)
            for j in range(lane_blocks):
                coeff = dt * pot_v[j, z, pl.ds(pl.multiple_of(b * 8, 8), 8), :] + shift
                moves = []
                for part in range(2):
                    cur, beside = found[part]
                    p = part * planes + z
                    total = beside[j]
                    if z > 0:
                        total = total + src[j, p - 1, rows_b, :]
                    if z < planes - 1:
                        total = total + src[j, p + 1, rows_b, :]
                    moves.append(coeff * cur[j] - (dt * kinetic) * total)
                finish(z, rows_b, j, found[0][0][j], found[1][0][j], moves)

    def finish_section(z, rows_b, j, real, imag, moves):
        sec_v[j, z, rows_b, :] = real + moves[1]
        sec_v[j, planes + z, rows_b, :] = imag - moves[0]

    def finish_next(z, rows_b, j, real, imag, moves):
        psi_v[j, z, rows_b, :] = 0.5 * (psi_v[j, z, rows_b, :] + real) + moves[1]
        psi_v[j, planes + z, rows_b, :] = 0.5 * (psi_v[j, planes + z, rows_b, :] + imag) - moves[0]

    def run_section(b, carry):
        stage_block(psi_v, 0, b, finish_section)
        return carry

    def run_next(b, carry):
        stage_block(sec_v, 1, b, finish_next)
        return carry

    def fix_columns(b, carry):
        rows_b = pl.ds(pl.multiple_of(b * 8 + top, 8), 8)
        sides = []
        for p in range(parts):
            other = (p + planes) % parts
            edge_w, edge_e = edges(0, p, b)
            scale = step_dt * kinetic if p < planes else -step_dt * kinetic
            sides.append(
                (
                    other,
                    sec_v[0, other, rows_b, :] + jnp.where(first, scale * edge_w, 0.0),
                    sec_v[lane_blocks - 1, other, rows_b, :] + jnp.where(last, scale * edge_e, 0.0),
                )
            )
        for other, low, high in sides:
            sec_v[0, other, rows_b, :] = low
            sec_v[lane_blocks - 1, other, rows_b, :] = high
        return carry

    surface(gather_0, True)
    hop_1(gather_0, 0)
    clear = jnp.zeros((1, 128), f32)
    for j in range(lane_blocks):
        for p in range(parts):
            psi_v[j, p, top - 1 : top, :] = clear
            psi_v[j, p, top + rows : top + rows + 1, :] = clear
    lax.fori_loop(0, blocks, run_section, 0)
    hop_2(gather_0, 0)

    for copy in halo:
        copy.wait_recv()

    keep_n = jnp.where(gy > 0, 1.0, 0.0).astype(f32)
    keep_s = jnp.where(gy < y_count - 1, 1.0, 0.0).astype(f32)
    keep_w = jnp.where(gx > 0, 1.0, 0.0).astype(f32)
    keep_e = jnp.where(gx < x_count - 1, 1.0, 0.0).astype(f32)

    def height(index):
        return spacing * (index.astype(f32) - 0.5 * (planes - 1))

    corner_cols = []
    for sy, keep_y in enumerate((keep_n, keep_s)):
        for sx, keep_x in enumerate((keep_w, keep_e)):
            lane = 127 if sx == 0 else 0
            corner_cols.append(corner_got[2 * sy + sx][:, lane : lane + 1] * (keep_y * keep_x))
    lane_row = iota((planes, cols), 1)
    sub_row = iota((planes, cols), 0)
    for side, keep in enumerate((keep_n, keep_s)):
        coeff = step_dt * (
            row_got[side, 2 * parts : 2 * parts + planes, :] + field_1 * height(sub_row) + 6.0 * kinetic
        )
        nears = []
        moves = []
        for part in range(2):
            sl = slice(part * planes, (part + 1) * planes)
            near = row_got[side, sl, :] * keep
            far = row_got[side, parts + part * planes : parts + (part + 1) * planes, :] * keep
            own = row_msg[side, sl, :]
            left = jnp.where(lane_row == 0, corner_cols[2 * side][sl], pltpu.roll(near, 1, 1))
            right = jnp.where(lane_row == cols - 1, corner_cols[2 * side + 1][sl], pltpu.roll(near, cols - 1, 1))
            below = jnp.where(sub_row == 0, 0.0, pltpu.roll(near, 1, 0))
            above = jnp.where(sub_row == planes - 1, 0.0, pltpu.roll(near, planes - 1, 0))
            beside = (far + own) + (left + right) + (below + above)
            nears.append(near)
            moves.append(coeff * near - (step_dt * kinetic) * beside)
        ghost_rows = (nears[0] + moves[1]) * keep, (nears[1] - moves[0]) * keep
        at = top - 1 if side == 0 else top + rows
        edge = top if side == 0 else top + rows - 1
        for part in range(2):
            for z in range(planes):
                for j in range(lane_blocks):
                    sl = slice(128 * j, 128 * j + 128)
                    p = part * planes + z
                    sec_v[j, p, at : at + 1, :] = ghost_rows[part][z : z + 1, sl]
                    share = (step_dt * kinetic) * nears[1 - part][z : z + 1, sl]
                    old = sec_v[j, p, edge : edge + 1, :]
                    sec_v[j, p, edge : edge + 1, :] = old - share if part == 0 else old + share

    lane_c = iota((rows, 128), 1)
    sub_c = iota((rows, 128), 0)
    diag_lane = iota((parts, 128), 1)
    diag_sub = iota((parts, 128), 0)
    plane_c = (lane_c % (2 * planes)) // 2
    for side, keep in enumerate((keep_w, keep_e)):
        got = col_got[side] * keep
        mine = col_msg[side]
        inner = 1 if side == 0 else 127
        odd = 1 if side == 0 else 0
        hit = diag_lane == 2 * diag_sub + odd
        ends = [
            jnp.sum(jnp.where(hit, corner_cols[2 * sy + side], 0.0), axis=0, keepdims=True)
            for sy in range(2)
        ]
        upper = jnp.where(sub_c == 0, ends[0], pltpu.roll(got, 1, 0))
        lower = jnp.where(sub_c == rows - 1, ends[1], pltpu.roll(got, rows - 1, 0))
        below = jnp.where(plane_c == 0, 0.0, pltpu.roll(got, 2, 1))
        above = jnp.where(plane_c == planes - 1, 0.0, pltpu.roll(got, 126, 1))
        beside = (
            (pltpu.roll(got, inner, 1) + pltpu.roll(mine, inner, 1)) + (upper + lower) + (below + above)
        )
        volts = pltpu.roll(got, 64, 1)
        volts = jnp.where(lane_c < 2 * planes, volts, pltpu.roll(volts, 2 * planes, 1))
        coeff = step_dt * (volts + field_1 * height(plane_c) + 6.0 * kinetic)
        move = coeff * got - (step_dt * kinetic) * beside
        ghost[0, side] = got
        ghost[1, side] = (
            got
            + jnp.where(
                lane_c < 2 * planes, pltpu.roll(move, 128 - 2 * planes, 1), -pltpu.roll(move, 2 * planes, 1)
            )
        ) * keep

    lax.fori_loop(0, blocks, fix_columns, 0, unroll=4)
    surface(gather_1, False)
    for k in range(1, x_count):
        line_copy(k, gx).start()
    stores = []
    pieces = 4
    per = blocks // pieces
    for q in range(pieces):
        lax.fori_loop(q * per, (q + 1) * per, run_next, 0)
        for j in range(lane_blocks):
            stores.append(
                pltpu.make_async_copy(
                    psi_v.at[j, :, top + 8 * per * q : top + 8 * per * (q + 1), :],
                    next_hbm.at[:, 8 * per * q : 8 * per * (q + 1), 128 * j : 128 * j + 128],
                    store_sem.at[q, j],
                )
            )
            stores[-1].start()
        if q == 0:
            for k in range(1, x_count):
                line_copy(k, wrap(gx - k, x_count)).wait_recv()
            for k in range(1, y_count):
                sheet_copy(k, gy).start()
            hop_3(gather_0, 0)
    hop_end(gather_0, 0)

    def count_row(i, total):
        for k in range(x_count):
            got = gather_0[i // (y_count // 2), lax.rem(i, y_count // 2) * 2 + k // chips, k % chips]
            total = jnp.where(lane8 == i * x_count + k, got[:, 2 * parts + 2 : 2 * parts + 3], total)
        return total

    live_ref[...] = lax.fori_loop(0, y_count, count_row, jnp.zeros((8, 128), f32))
    for copy in halo:
        copy.wait_send()
    for copy in stores:
        copy.wait()
    for k in range(1, y_count):
        sheet_copy(k, wrap(gy - k, y_count)).wait_recv()
    sends_wait(gather_0, 0)
    for k in range(1, x_count):
        line_copy(k, gx).wait_send()
    for k in range(1, y_count):
        sheet_copy(k, gy).wait_send()


def turns(phase):
    quarter = jnp.floor(phase * 0.6366197723675814 + 0.5)
    rest = phase - quarter * 1.5703125
    rest = rest - quarter * 4.83751296997e-4
    rest = rest - quarter * 7.5497899548918821e-8
    square = rest * rest
    sine = rest + rest * square * (
        -1.6666654611e-1 + square * (8.3321608736e-3 + square * -1.9515295891e-4)
    )
    cosine = (
        1.0
        - 0.5 * square
        + square * square * (4.166664568298827e-2 + square * (-1.388731625493765e-3 + square * 2.443315711809948e-5))
    )
    which = quarter.astype(jnp.int32)
    swap = (which & 1) == 1
    sin_out = jnp.where(swap, cosine, sine)
    cos_out = jnp.where(swap, sine, cosine)
    sin_out = jnp.where((which & 2) == 2, -sin_out, sin_out)
    cos_out = jnp.where(((which + 1) & 2) == 2, -cos_out, cos_out)
    return cos_out, sin_out


def flux_kernel(
    x_count,
    y_count,
    live_ref,
    count_ref,
    order_ref,
    gather_0,
    gather_1,
    weight_ref,
    amp_ref,
    tmp_hbm,
    next_hbm,
    out_ref,
    comp_0,
    comp_1,
    total,
    held,
    fetch_sem,
    copy_sem,
):
    copies = []
    parts = tmp_hbm.shape[0]
    quarter = parts // 4
    for q in range(4):
        sl = slice(q * quarter, (q + 1) * quarter)
        fetch = pltpu.make_async_copy(tmp_hbm.at[sl], held.at[sl], fetch_sem.at[q])
        fetch.start()
        copies.append((fetch, pltpu.make_async_copy(held.at[sl], next_hbm.at[sl], copy_sem.at[q])))
    me = lax.axis_index("gx") * y_count + lax.axis_index("gy")
    groups = count_ref.shape[0]
    slots = amp_ref.shape[0]
    features = weight_ref.shape[1] // 8
    feature = iota((128, 128), 1) < features

    def offset(i, at):
        return at + jnp.where(i < me, count_ref[i], 0)

    own_start = lax.fori_loop(0, groups, offset, 0, unroll=True)
    own_count = count_ref[me]
    waves = []
    for s in range(slots):
        plane = order_ref[jnp.minimum(own_start + s, groups - 1)]
        waves.append((plane.astype(f32) - 0.5 * (groups - 1)) * (k_span / groups))

    tiles = x_count * y_count
    chips = x_count // 2

    def gather_tile(t, n):
        c = live_ref[0, t].astype(jnp.int32)
        at = pl.ds(pl.multiple_of(t * 8, 8), 8)
        block_0 = gather_0[at, :]
        half, row, chip = t // (tiles // 2), (t // chips) % y_count, t % chips
        block_1 = gather_1[row * x_count + 2 * chip + half]
        comp_0[pl.ds(n, 8), :] = block_0
        comp_1[pl.ds(n, 4), :] = block_1
        comp_1[pl.ds(n + 4, 4), :] = pltpu.roll(block_1, 96, 1)
        n = n + jnp.minimum(c, 8)
        comp_0[pl.ds(n, 8), :] = pltpu.roll(block_0, 64, 1)
        comp_1[pl.ds(n, 4), :] = pltpu.roll(block_1, 64, 1)
        comp_1[pl.ds(n + 4, 4), :] = pltpu.roll(block_1, 32, 1)
        return n + jnp.maximum(c - 8, 0)

    live = lax.fori_loop(0, x_count * y_count, gather_tile, 0, unroll=True)

    def clear(i, carry):
        to = pl.ds(live + i * 8, 8)
        comp_0[to, :] = jnp.zeros((8, 128), f32)
        comp_1[to, :] = jnp.zeros((8, 128), f32)
        return carry

    lax.fori_loop(0, 16, clear, 0)
    total[...] = jnp.zeros_like(total)
    kx = (iota((128, 128), 0).astype(f32) - 63.5) * (k_span / 128)
    sub8 = iota((8, 128), 0)
    ky = jnp.zeros((8, 128), f32)
    for s in range(slots):
        ky = jnp.where(sub8 // 2 == s, waves[s], ky)
    moment8 = jnp.where(sub8 % 2 == 0, start_time, later_time).astype(f32)

    def chunk(c, carry):
        at = pl.ds(pl.multiple_of(c * 128, 128), 128)
        rows = (comp_0[at, :], comp_1[at, :])
        place = jnp.transpose(rows[0])
        px, py = place[features : features + 1, :], place[features + 1 : features + 2, :]
        col_x, col_y = rows[0][:, features : features + 1], rows[0][:, features + 1 : features + 2]
        square = col_x * col_x + col_y * col_y
        radius = jnp.sqrt(jnp.where(square > 0.0, square, 1.0))
        nx, ny = col_x / radius, col_y / radius
        right = []
        left = []
        for t, moment in enumerate((start_time, later_time)):
            raw = jnp.where(feature, rows[t], 0.0)
            high = raw.astype(jnp.bfloat16).astype(f32)
            mid = (raw - high).astype(jnp.bfloat16).astype(f32)
            low = (raw - high) - mid
            side = (
                (high + pltpu.roll(mid, features, 1))
                + (pltpu.roll(low, 2 * features, 1) + pltpu.roll(high, 3 * features, 1))
            ).astype(jnp.bfloat16)
            modes = jnp.dot(
                jnp.concatenate([side, side], axis=1), weight_ref[t], preferred_element_type=f32
            )
            ur, ui, dr, di = (modes[:, 128 * i : 128 * i + 128] for i in range(4))
            right.append(
                jnp.concatenate([nx * ur, ny * ur, dr, nx * ui, ny * ui, di], axis=1).astype(jnp.bfloat16)
            )
            left.append(turns(0.5 * kx * kx * moment - kx * px))
        right = jnp.concatenate(right, axis=0)
        rot_cos, rot_sin = turns(0.5 * ky * ky * moment8 - ky * py)

        for first in range(0, slots, 2):

            @pl.when(first < own_count)
            def _():
                sides = []
                pair = range(first, min(first + 2, slots))
                for s in pair:
                    real = []
                    imag = []
                    for t in range(2):
                        bc, bs = rot_cos[2 * s + t : 2 * s + t + 1], rot_sin[2 * s + t : 2 * s + t + 1]
                        ac, as_ = left[t]
                        real.append((ac * bc - as_ * bs).astype(jnp.bfloat16))
                        imag.append((ac * bs + as_ * bc).astype(jnp.bfloat16))
                    sides.append(jnp.concatenate(real, axis=1))
                    sides.append(jnp.concatenate(imag, axis=1))
                prod = jnp.dot(jnp.concatenate(sides, axis=0), right, preferred_element_type=f32)
                for i, s in enumerate(pair):
                    m = [prod[256 * i : 256 * i + 128, 128 * k : 128 * k + 128] for k in range(6)]
                    w = [prod[256 * i + 128 : 256 * i + 256, 128 * k : 128 * k + 128] for k in range(6)]
                    hy = waves[s]
                    total[s, 0] += kx * (m[0] - w[3]) + hy * (m[1] - w[4]) + (m[5] + w[2])
                    total[s, 1] += kx * (m[3] + w[0]) + hy * (m[4] + w[1]) - (m[2] - w[5])

        return carry

    chunks = (live + 127) // 128
    lax.fori_loop(0, jnp.minimum(chunks, 1), chunk, 0)
    for fetch, copy in copies:
        fetch.wait()
        copy.start()
    lax.fori_loop(1, chunks, chunk, 0)
    for s in range(slots):
        for part in range(2):
            sl = pl.ds(part, 128, stride=2)
            inc = jnp.where(s < own_count, (0.5 * flux_weight) * total[s, part], 0.0)
            out_ref[s, sl, :] = amp_ref[s, sl, :] + inc
    for fetch, copy in copies:
        copy.wait()


def shards(psi_now, potential, surf_cells, surf_count, block_count, block_order, amplitude):
    x_count = lax.axis_size("gx")
    y_count = lax.axis_size("gy")
    planes, rows, cols = potential.shape
    parts = 2 * planes
    slots = surf_cells.shape[2]
    own, modes_x, _, modes_z = amplitude.shape
    any_spec = pl.BlockSpec(memory_space=pl.ANY)
    vmem = pl.BlockSpec(memory_space=pltpu.VMEM)
    smem = pl.BlockSpec(memory_space=pltpu.SMEM)
    hbm = pl.BlockSpec(memory_space=pltpu.HBM)
    dma = pltpu.SemaphoreType.DMA
    gathered = jax.ShapeDtypeStruct((2, y_count, x_count // 2, 8, 128), f32)
    sheet = jax.ShapeDtypeStruct((y_count, x_count, 4, 128), f32)
    field = jax.ShapeDtypeStruct((parts, rows, cols), f32)
    staged, gather_0, gather_1, live = pl.pallas_call(
        functools.partial(step_kernel, x_count, y_count),
        out_shape=(field, gathered, sheet, jax.ShapeDtypeStruct((8, 128), f32)),
        in_specs=[smem, smem, hbm, hbm],
        out_specs=(any_spec, vmem, vmem, vmem),
        scratch_shapes=[
            pltpu.VMEM((cols // 128, parts, rows + 16, 128), f32),
            pltpu.VMEM((cols // 128, parts, rows + 16, 128), f32),
            pltpu.VMEM((cols // 128, planes, rows, 128), f32),
            pltpu.VMEM((2, 2 * parts + planes, cols), f32),
            pltpu.VMEM((2, 2 * parts + planes, cols), f32),
            pltpu.VMEM((2, rows, 128), f32),
            pltpu.VMEM((2, rows, 128), f32),
            pltpu.VMEM((4, parts, 128), f32),
            pltpu.VMEM((2, 2, rows, 128), f32),
            dma((2, 2, cols // 128)),
            dma((4, cols // 128)),
            dma((2,)),
            dma((2,)),
            dma((2,)),
            dma((2,)),
            dma((4,)),
            dma((4,)),
            dma((2, x_count)),
            dma((2, x_count)),
            dma((2, y_count)),
            dma((2, y_count)),
        ],
        compiler_params=pltpu.CompilerParams(
            collective_id=0, has_side_effects=True, vmem_limit_bytes=52 * 1024 * 1024
        ),
        name="step",
    )(
        surf_cells,
        surf_count,
        psi_now.reshape(parts, rows, cols),
        potential,
    )
    tiles = x_count * y_count
    psi_next, amplitude_next = pl.pallas_call(
        functools.partial(flux_kernel, x_count, y_count),
        out_shape=(field, jax.ShapeDtypeStruct((own, 2 * modes_x, modes_z), f32)),
        in_specs=[smem, smem, smem, vmem, vmem, vmem, vmem, any_spec],
        out_specs=(any_spec, vmem),
        scratch_shapes=[
            pltpu.VMEM((slots * tiles + 144, 128), f32),
            pltpu.VMEM((slots * tiles + 144, 128), f32),
            pltpu.VMEM((own, 2, modes_x, modes_z), f32),
            pltpu.VMEM((parts, rows, cols), f32),
            dma((4,)),
            dma((4,)),
        ],
        compiler_params=pltpu.CompilerParams(vmem_limit_bytes=52 * 1024 * 1024),
        name="flux",
    )(
        live,
        block_count,
        block_order,
        gather_0.reshape(tiles * 8, 128),
        gather_1.reshape(tiles, 4, 128),
        jnp.asarray(mode_weights(planes, modes_z)),
        amplitude.reshape(own, 2 * modes_x, modes_z),
        staged,
    )
    return psi_next.reshape(psi_now.shape), amplitude_next.reshape(amplitude.shape)


def solution(mesh):
    return jax.shard_map(
        shards,
        mesh=mesh,
        in_specs=(
            P(None, None, "gy", "gx"),
            P(None, "gy", "gx"),
            P("gy", "gx", None),
            P("gy", "gx"),
            P(),
            P(),
            P(("gx", "gy"), None, None, None),
        ),
        out_specs=(P(None, None, "gy", "gx"), P(("gx", "gy"), None, None, None)),
        check_vma=False,
    )
```

```python
import functools
import math

import jax
import jax.numpy as jnp
import numpy as np
from jax import lax
from jax.experimental import pallas as pl
from jax.experimental.pallas import tpu as pltpu
from jax.sharding import PartitionSpec as P

spacing = 0.2
kinetic = 12.5
step_dt = 0.016
half_dt = 0.008
start_time = 100.0
later_time = start_time + step_dt
field_peak = 0.05
field_freq = 0.057
k_span = 4.0
flux_weight = 0.0078125
MESH = pl.DeviceIdType.MESH
f32 = jnp.float32


def field_at(moment):
    return field_peak * math.sin(field_freq * moment)


def drift_at(moment):
    return field_peak / (field_freq * field_freq) * math.sin(field_freq * moment)


def mode_weights(planes, modes):
    wave = ((np.arange(modes) - 0.5 * (modes - 1)) * (k_span / modes)).astype(np.float32)
    height = np.float32(spacing) * (np.arange(planes) - 0.5 * (planes - 1)).astype(np.float32)
    out = np.zeros((2, 4 * planes, 4 * modes), np.float32)
    for t, moment in enumerate((start_time, later_time)):
        phase = (
            np.float32(0.5) * wave * wave * np.float32(moment) + wave * np.float32(drift_at(moment))
        )[None, :] - wave[None, :] * height[:, None]
        cos = np.cos(phase.astype(np.float64)).astype(np.float32)
        sin = np.sin(phase.astype(np.float64)).astype(np.float32)
        block = np.block([[cos, sin], [-sin, cos]])
        out[t, : 2 * planes, : 2 * modes] = block
        out[t, 2 * planes :, 2 * modes :] = block
    high = out.astype(jnp.bfloat16).astype(np.float32)
    mid = (out - high).astype(jnp.bfloat16).astype(np.float32)
    low = out - high - mid
    none = np.zeros_like(out)
    return np.concatenate([high, high, high, mid, low, mid, none, none], axis=1).astype(jnp.bfloat16)


def iota(shape, dim):
    return lax.broadcasted_iota(jnp.int32, shape, dim)


def step_kernel(
    x_count,
    y_count,
    cells_ref,
    count_ref,
    psi_hbm,
    pot_hbm,
    next_hbm,
    gather_0,
    gather_1,
    live_ref,
    psi_v,
    sec_v,
    pot_v,
    row_msg,
    row_got,
    col_msg,
    col_got,
    corner_got,
    ghost,
    load_sem,
    store_sem,
    row_send,
    row_recv,
    col_send,
    col_recv,
    corner_send,
    corner_recv,
    x_send,
    x_recv,
    y_send,
    y_recv,
):
    gx = lax.axis_index("gx")
    gy = lax.axis_index("gy")
    parts, rows, cols = psi_hbm.shape
    planes = parts // 2
    blocks = rows // 8
    lane_blocks = cols // 128
    top = 8

    def wrap(value, count):
        return lax.rem(value + count, count)

    west, east = wrap(gx - 1, x_count), wrap(gx + 1, x_count)
    north, south = wrap(gy - 1, y_count), wrap(gy + 1, y_count)
    loads = []
    halves = 2
    part_rows = rows // halves
    load_parts = [(j, h) for h in range(halves) for j in (0, lane_blocks - 1)]
    load_parts += [(j, h) for j in range(1, lane_blocks - 1) for h in range(halves)]
    for j, h in load_parts:
        sl = slice(128 * j, 128 * j + 128)
        lo, hi = h * part_rows, (h + 1) * part_rows
        loads.append(
            pltpu.make_async_copy(
                psi_hbm.at[:, lo:hi, sl], psi_v.at[j, :, top + lo : top + hi, :], load_sem.at[0, h, j]
            )
        )
        loads.append(
            pltpu.make_async_copy(pot_hbm.at[:, lo:hi, sl], pot_v.at[j, :, lo:hi, :], load_sem.at[1, h, j])
        )
    for copy in loads:
        copy.start()

    barrier = pltpu.get_barrier_semaphore()
    partner = gx + 1 - 2 * lax.rem(gx, 2)
    column = lax.rem(gx, 2)
    chip = gx // 2
    chips = x_count // 2
    signals = 0
    for k in range(1, x_count):
        pl.semaphore_signal(barrier, inc=1, device_id=(wrap(gx + k, x_count), gy), device_id_type=MESH)
        signals += 1
    for k in range(1, y_count):
        pl.semaphore_signal(barrier, inc=1, device_id=(gx, wrap(gy + k, y_count)), device_id_type=MESH)
        signals += 1
    for sx in (west, east):
        for sy in (north, south):
            pl.semaphore_signal(barrier, inc=1, device_id=(sx, sy), device_id_type=MESH)
            signals += 1


    lane8 = iota((8, 128), 1)
    sub8 = iota((8, 128), 0)

    def pack(b, carry):
        r0 = pl.multiple_of(b * 8, 8)
        for side in range(2):
            j = 0 if side == 0 else lane_blocks - 1
            base = 0 if side == 0 else 2
            moved = [
                (p, pltpu.roll(psi_v[j, p, pl.ds(r0 + top, 8), :], (2 * p + base) % 128, 1))
                for p in range(parts)
            ] + [
                (32 + z, pltpu.roll(pot_v[j, z, pl.ds(r0, 8), :], (64 + 2 * z + base) % 128, 1))
                for z in range(planes)
            ]
            while len(moved) > 1:
                joined = []
                for i in range(0, len(moved) - 1, 2):
                    (at_a, part_a), (at_b, part_b) = moved[i], moved[i + 1]
                    joined.append((at_a, jnp.where(lane8 < 2 * at_b, part_a, part_b)))
                if len(moved) % 2:
                    joined.append(moved[-1])
                moved = joined
            packed = moved[0][1]
            col_msg[side, pl.ds(r0, 8), :] = packed
        return carry

    for h in range(halves):
        for copy in loads[4 * h : 4 * h + 4]:
            copy.wait()
        lax.fori_loop(h * (blocks // halves), (h + 1) * (blocks // halves), pack, 0, unroll=4)

    pl.semaphore_wait(barrier, signals)

    halo = []
    for side, target in enumerate((west, east)):
        halo.append(
            pltpu.make_async_remote_copy(
                src_ref=col_msg.at[side],
                dst_ref=col_got.at[1 - side],
                send_sem=col_send.at[side],
                recv_sem=col_recv.at[1 - side],
                device_id=(target, gy),
                device_id_type=MESH,
            )
        )
    for copy in halo:
        copy.start()
    for copy in loads[4 * halves :]:
        copy.wait()
    for side, (near, far) in enumerate(((top, top + 1), (top + rows - 1, top + rows - 2))):
        for j in range(lane_blocks):
            sl = slice(128 * j, 128 * j + 128)
            for p in range(parts):
                row_msg[side, p : p + 1, sl] = psi_v[j, p, near : near + 1, :]
                row_msg[side, parts + p : parts + p + 1, sl] = psi_v[j, p, far : far + 1, :]
            for z in range(planes):
                row_msg[side, 2 * parts + z : 2 * parts + z + 1, sl] = pot_v[
                    j, z, near - top : near - top + 1, :
                ]

    for side, target in enumerate((north, south)):
        halo.append(
            pltpu.make_async_remote_copy(
                src_ref=row_msg.at[side],
                dst_ref=row_got.at[1 - side],
                send_sem=row_send.at[side],
                recv_sem=row_recv.at[1 - side],
                device_id=(gx, target),
                device_id_type=MESH,
            )
        )
    for sy, ty in enumerate((north, south)):
        for sx, tx in enumerate((west, east)):
            lo = 0 if sx == 0 else cols - 128
            halo.append(
                pltpu.make_async_remote_copy(
                    src_ref=row_msg.at[sy, 0:parts, lo : lo + 128],
                    dst_ref=corner_got.at[2 * (1 - sy) + 1 - sx],
                    send_sem=corner_send.at[2 * sy + sx],
                    recv_sem=corner_recv.at[2 * (1 - sy) + 1 - sx],
                    device_id=(tx, ty),
                    device_id_type=MESH,
                )
            )
    for copy in halo[2:]:
        copy.start()

    lane_p = iota((parts, 128), 1)

    def take(slot, carry):
        out_u, out_d = carry
        cell = cells_ref[0, 0, slot]
        y = cell // cols
        x = cell - y * cols
        alive = jnp.where(slot < count_ref[0, 0], 1.0, 0.0).astype(f32)
        px = jnp.full((1, 128), spacing * ((gx * cols + x).astype(f32) - (0.5 * cols * x_count - 0.5)), f32)
        py = jnp.full((1, 128), spacing * ((gy * rows + y).astype(f32) - (0.5 * rows * y_count - 0.5)), f32)
        radius = jnp.sqrt(px * px + py * py)
        weight_x = px / radius / (2.0 * spacing) * alive
        weight_y = py / radius / (2.0 * spacing) * alive
        total_u = jnp.zeros((parts, 128), f32)
        total_d = jnp.zeros((parts, 128), f32)
        low = jnp.minimum(jnp.maximum(x - 1, 0) // 128, max(lane_blocks - 2, 0))
        for j in [low + i for i in range(min(lane_blocks, 2))]:
            lane = iota((1, 128), 1) + 128 * j
            at = jnp.where(lane == x, alive, 0.0)
            along = jnp.where(lane == x + 1, weight_x, 0.0) - jnp.where(lane == x - 1, weight_x, 0.0)
            across = jnp.where(lane == x, weight_y, 0.0)
            flat = psi_v.at[j].reshape(parts * (rows + 16), 128)
            middle = flat[pl.ds(y + top, parts, stride=rows + 16), :]
            after = flat[pl.ds(y + top + 1, parts, stride=rows + 16), :]
            before = flat[pl.ds(y + top - 1, parts, stride=rows + 16), :]
            total_u = total_u + middle * at
            total_d = total_d + (middle * along + (after - before) * across)
        out_u = jnp.where(lane_p == slot, jnp.sum(total_u, axis=1, keepdims=True), out_u)
        out_d = jnp.where(lane_p == slot, jnp.sum(total_d, axis=1, keepdims=True), out_d)
        return out_u, out_d

    slots = cells_ref.shape[2]

    half_kin = half_dt * kinetic

    def swap_parts(value):
        return jnp.concatenate([value[planes:], -value[:planes]], axis=0)

    sub_p = lax.rem(iota((parts, 128), 0), planes)
    hit_w = lane_p == 2 * iota((parts, 128), 0) + 1
    hit_e = lane_p == 2 * iota((parts, 128), 0)

    def take_next(slot, carry):
        out_u, out_d = carry
        cell = cells_ref[0, 0, slot]
        row = cell // cols
        x = cell - row * cols
        y = jnp.maximum(row, 1)
        alive = jnp.where(slot < count_ref[0, 0], 1.0, 0.0).astype(f32)
        px = jnp.full((1, 128), spacing * ((gx * cols + x).astype(f32) - (0.5 * cols * x_count - 0.5)), f32)
        py = jnp.full((1, 128), spacing * ((gy * rows + y).astype(f32) - (0.5 * rows * y_count - 0.5)), f32)
        radius = jnp.sqrt(px * px + py * py)
        weight_x = px / radius / (2.0 * spacing) * alive
        weight_y = py / radius / (2.0 * spacing) * alive
        shift = half_dt * (
            field_2 * (spacing * (sub_p.astype(f32) - 0.5 * (planes - 1))) + 6.0 * kinetic
        )
        zero = jnp.zeros((parts, 128), f32)
        mean = [zero, zero]
        plain = [zero, zero]
        scaled = [zero, zero]
        around = [zero, zero]
        low = jnp.minimum(jnp.maximum(x - 2, 0) // 128, max(lane_blocks - 2, 0))
        for j in [low + i for i in range(min(lane_blocks, 2))]:
            lane = iota((1, 128), 1) + 128 * j
            at = jnp.where(lane == x, alive, 0.0)
            at_side = jnp.where((lane == x + 1) | (lane == x - 1), alive, 0.0)
            along = jnp.where(lane == x + 1, weight_x, 0.0) - jnp.where(lane == x - 1, weight_x, 0.0)
            along_side = jnp.where(lane == x + 2, weight_x, 0.0) - jnp.where(
                lane == x - 2, weight_x, 0.0
            )
            across = jnp.where(lane == x, weight_y, 0.0)
            across_side = jnp.where((lane == x + 1) | (lane == x - 1), weight_y, 0.0)
            flat_s = sec_v.at[j].reshape(parts * (rows + 16), 128)
            flat_f = psi_v.at[j].reshape(parts * (rows + 16), 128)
            flat_p = pot_v.at[j].reshape(planes * rows, 128)
            sec = [flat_s[pl.ds(y + top + r, parts, stride=rows + 16), :] for r in range(-2, 3)]
            psi = [flat_f[pl.ds(y + top + r, parts, stride=rows + 16), :] for r in range(-1, 2)]
            pot = [flat_p[pl.ds(y + r, planes, stride=rows), :] for r in range(-1, 2)]
            coeff = [jnp.concatenate([v, v], axis=0) * half_dt + shift for v in pot]
            mean[0] = mean[0] + (0.5 * at) * (psi[1] + sec[2])
            plain[0] = plain[0] + at * sec[2]
            scaled[0] = scaled[0] + at * (coeff[1] * sec[2])
            around[0] = around[0] + (at * (sec[1] + sec[3]) + at_side * sec[2])
            mean[1] = mean[1] + 0.5 * (
                along * (psi[1] + sec[2]) + across * ((psi[2] + sec[3]) - (psi[0] + sec[1]))
            )
            plain[1] = plain[1] + (along * sec[2] + across * (sec[3] - sec[1]))
            scaled[1] = scaled[1] + (
                along * (coeff[1] * sec[2]) + across * (coeff[2] * sec[3] - coeff[0] * sec[1])
            )
            around[1] = around[1] + (
                (along * (sec[1] + sec[3]) + across * (sec[4] - sec[0]))
                + (along_side * sec[2] + across_side * (sec[3] - sec[1]))
            )
        row_w = ghost[1, 0, pl.ds(y, 1), :] * jnp.where(x == 1, -weight_x, 0.0)
        row_e = ghost[1, 1, pl.ds(y, 1), :] * jnp.where(x == cols - 2, weight_x, 0.0)
        around[1] = around[1] + (jnp.where(hit_w, row_w, 0.0) + jnp.where(hit_e, row_e, 0.0))
        sums = []
        for i in range(2):
            below = jnp.where(sub_p == 0, 0.0, pltpu.roll(plain[i], 1, 0))
            above = jnp.where(sub_p == planes - 1, 0.0, pltpu.roll(plain[i], parts - 1, 0))
            move = scaled[i] - half_kin * (around[i] + (below + above))
            sums.append(jnp.sum(mean[i] + swap_parts(move), axis=1, keepdims=True))
        return jnp.where(lane_p == slot, sums[0], out_u), jnp.where(lane_p == slot, sums[1], out_d)

    def surface(target, is_now):
        zero = jnp.zeros((parts, 128), f32)
        out_u, out_d = lax.fori_loop(
            0, slots, take if is_now else take_next, (zero, zero), unroll=True
        )
        turned = jnp.transpose(
            jnp.concatenate([out_u, out_d, jnp.zeros((128 - 2 * parts, 128), f32)], axis=0)
        )
        if not is_now:
            target[gy, gx] = (turned[0:4] + pltpu.roll(turned[4:8], 32, 1)) + (
                pltpu.roll(turned[8:12], 64, 1) + pltpu.roll(turned[12:16], 96, 1)
            )
        if is_now:
            packed = jnp.where(lane8 < 64, turned[0:8], pltpu.roll(turned[8:16], 64, 1))
            for slot in range(slots):
                cell = cells_ref[0, 0, slot]
                y = cell // cols
                x = cell - y * cols
                px = spacing * ((gx * cols + x).astype(f32) - (0.5 * cols * x_count - 0.5))
                py = spacing * ((gy * rows + y).astype(f32) - (0.5 * rows * y_count - 0.5))
                base = 64 * (slot // 8) + 2 * parts
                row = sub8 == slot % 8
                packed = jnp.where(row & (lane8 == base), px, packed)
                packed = jnp.where(row & (lane8 == base + 1), py, packed)
            packed = jnp.where(lane8 == 2 * parts + 2, count_ref[0, 0].astype(f32), packed)
            target[column, gy, chip] = packed

    def chip_copy(buf, phase, k, source):
        return pltpu.make_async_remote_copy(
            src_ref=buf.at[column, gy, source],
            dst_ref=buf.at[column, gy, source],
            send_sem=x_send.at[phase, k],
            recv_sem=x_recv.at[phase, k],
            device_id=(wrap(gx + 2 * k, x_count), gy),
            device_id_type=MESH,
        )

    def y_copy(buf, phase, k, source):
        return pltpu.make_async_remote_copy(
            src_ref=buf.at[column, source],
            dst_ref=buf.at[column, source],
            send_sem=y_send.at[phase, k],
            recv_sem=y_recv.at[phase, k],
            device_id=(gx, wrap(gy + k, y_count)),
            device_id_type=MESH,
        )

    def pair_copy(buf, phase, which):
        return pltpu.make_async_remote_copy(
            src_ref=buf.at[which],
            dst_ref=buf.at[which],
            send_sem=x_send.at[phase, 0],
            recv_sem=x_recv.at[phase, 0],
            device_id=(partner, gy),
            device_id_type=MESH,
        )

    def hop_1(buf, phase):
        for k in range(1, chips):
            chip_copy(buf, phase, k, chip).start()

    def hop_2(buf, phase):
        for k in range(1, chips):
            chip_copy(buf, phase, k, wrap(chip - k, chips)).wait_recv()
        for k in range(1, y_count):
            y_copy(buf, phase, k, gy).start()

    def hop_3(buf, phase):
        for k in range(1, y_count):
            y_copy(buf, phase, k, wrap(gy - k, y_count)).wait_recv()
        pair_copy(buf, phase, column).start()

    def hop_end(buf, phase):
        pair_copy(buf, phase, 1 - column).wait_recv()

    def line_copy(k, source):
        return pltpu.make_async_remote_copy(
            src_ref=gather_1.at[gy, source],
            dst_ref=gather_1.at[gy, source],
            send_sem=x_send.at[1, k],
            recv_sem=x_recv.at[1, k],
            device_id=(wrap(gx + k, x_count), gy),
            device_id_type=MESH,
        )

    def sheet_copy(k, source):
        return pltpu.make_async_remote_copy(
            src_ref=gather_1.at[source],
            dst_ref=gather_1.at[source],
            send_sem=y_send.at[1, k],
            recv_sem=y_recv.at[1, k],
            device_id=(gx, wrap(gy + k, y_count)),
            device_id_type=MESH,
        )

    def sends_wait(buf, phase):
        for k in range(1, chips):
            chip_copy(buf, phase, k, chip).wait_send()
        for k in range(1, y_count):
            y_copy(buf, phase, k, gy).wait_send()
        pair_copy(buf, phase, column).wait_send()

    field_1 = field_at(start_time)
    field_2 = field_at(later_time)
    first = lane8 == 0
    last = lane8 == 127

    def edges(stage, p, b):
        at = pl.ds(pl.multiple_of(b * 8, 8), 8)
        edge_w = pltpu.roll(ghost[stage, 0, at, :], (128 - (2 * p + 1)) % 128, 1)
        edge_e = pltpu.roll(ghost[stage, 1, at, :], (127 - 2 * p) % 128, 1)
        return edge_w, edge_e

    def spread(src, p, r0, stage, b):
        rows_b = pl.ds(r0, 8)
        cur = [src[j, p, rows_b, :] for j in range(lane_blocks)]
        right = [pltpu.roll(c, 1, 1) for c in cur]
        left = [pltpu.roll(c, 127, 1) for c in cur]
        if stage == 0:
            edge_w = edge_e = 0.0
        else:
            edge_w, edge_e = edges(1, p, b)
        out = []
        for j in range(lane_blocks):
            up = src[j, p, pl.ds(r0 - 1, 8), :]
            down = src[j, p, pl.ds(r0 + 1, 8), :]
            w = jnp.where(first, edge_w if j == 0 else right[j - 1], right[j])
            e = jnp.where(last, edge_e if j == lane_blocks - 1 else left[j + 1], left[j])
            out.append((up + down) + (w + e))
        return cur, out

    def stage_block(src, stage, b, finish):
        r0 = pl.multiple_of(b * 8 + top, 8)
        rows_b = pl.ds(r0, 8)
        dt = step_dt if stage == 0 else half_dt
        field = field_1 if stage == 0 else field_2
        for z in range(planes):
            found = [spread(src, part * planes + z, r0, stage, b) for part in range(2)]
            shift = dt * (field * spacing * (z - 0.5 * (planes - 1)) + 6.0 * kinetic)
            for j in range(lane_blocks):
                coeff = dt * pot_v[j, z, pl.ds(pl.multiple_of(b * 8, 8), 8), :] + shift
                moves = []
                for part in range(2):
                    cur, beside = found[part]
                    p = part * planes + z
                    total = beside[j]
                    if z > 0:
                        total = total + src[j, p - 1, rows_b, :]
                    if z < planes - 1:
                        total = total + src[j, p + 1, rows_b, :]
                    moves.append(coeff * cur[j] - (dt * kinetic) * total)
                finish(z, rows_b, j, found[0][0][j], found[1][0][j], moves)

    def finish_section(z, rows_b, j, real, imag, moves):
        sec_v[j, z, rows_b, :] = real + moves[1]
        sec_v[j, planes + z, rows_b, :] = imag - moves[0]

    def finish_next(z, rows_b, j, real, imag, moves):
        psi_v[j, z, rows_b, :] = 0.5 * (psi_v[j, z, rows_b, :] + real) + moves[1]
        psi_v[j, planes + z, rows_b, :] = 0.5 * (psi_v[j, planes + z, rows_b, :] + imag) - moves[0]

    def run_section(b, carry):
        stage_block(psi_v, 0, b, finish_section)
        return carry

    def run_next(b, carry):
        stage_block(sec_v, 1, b, finish_next)
        return carry

    def fix_columns(b, carry):
        rows_b = pl.ds(pl.multiple_of(b * 8 + top, 8), 8)
        sides = []
        for p in range(parts):
            other = (p + planes) % parts
            edge_w, edge_e = edges(0, p, b)
            scale = step_dt * kinetic if p < planes else -step_dt * kinetic
            sides.append(
                (
                    other,
                    sec_v[0, other, rows_b, :] + jnp.where(first, scale * edge_w, 0.0),
                    sec_v[lane_blocks - 1, other, rows_b, :] + jnp.where(last, scale * edge_e, 0.0),
                )
            )
        for other, low, high in sides:
            sec_v[0, other, rows_b, :] = low
            sec_v[lane_blocks - 1, other, rows_b, :] = high
        return carry

    surface(gather_0, True)
    hop_1(gather_0, 0)
    clear = jnp.zeros((1, 128), f32)
    for j in range(lane_blocks):
        for p in range(parts):
            psi_v[j, p, top - 1 : top, :] = clear
            psi_v[j, p, top + rows : top + rows + 1, :] = clear
    lax.fori_loop(0, blocks, run_section, 0)
    hop_2(gather_0, 0)

    for copy in halo:
        copy.wait_recv()

    keep_n = jnp.where(gy > 0, 1.0, 0.0).astype(f32)
    keep_s = jnp.where(gy < y_count - 1, 1.0, 0.0).astype(f32)
    keep_w = jnp.where(gx > 0, 1.0, 0.0).astype(f32)
    keep_e = jnp.where(gx < x_count - 1, 1.0, 0.0).astype(f32)

    def height(index):
        return spacing * (index.astype(f32) - 0.5 * (planes - 1))

    corner_cols = []
    for sy, keep_y in enumerate((keep_n, keep_s)):
        for sx, keep_x in enumerate((keep_w, keep_e)):
            lane = 127 if sx == 0 else 0
            corner_cols.append(corner_got[2 * sy + sx][:, lane : lane + 1] * (keep_y * keep_x))
    lane_row = iota((planes, cols), 1)
    sub_row = iota((planes, cols), 0)
    for side, keep in enumerate((keep_n, keep_s)):
        coeff = step_dt * (
            row_got[side, 2 * parts : 2 * parts + planes, :] + field_1 * height(sub_row) + 6.0 * kinetic
        )
        nears = []
        moves = []
        for part in range(2):
            sl = slice(part * planes, (part + 1) * planes)
            near = row_got[side, sl, :] * keep
            far = row_got[side, parts + part * planes : parts + (part + 1) * planes, :] * keep
            own = row_msg[side, sl, :]
            left = jnp.where(lane_row == 0, corner_cols[2 * side][sl], pltpu.roll(near, 1, 1))
            right = jnp.where(lane_row == cols - 1, corner_cols[2 * side + 1][sl], pltpu.roll(near, cols - 1, 1))
            below = jnp.where(sub_row == 0, 0.0, pltpu.roll(near, 1, 0))
            above = jnp.where(sub_row == planes - 1, 0.0, pltpu.roll(near, planes - 1, 0))
            beside = (far + own) + (left + right) + (below + above)
            nears.append(near)
            moves.append(coeff * near - (step_dt * kinetic) * beside)
        ghost_rows = (nears[0] + moves[1]) * keep, (nears[1] - moves[0]) * keep
        at = top - 1 if side == 0 else top + rows
        edge = top if side == 0 else top + rows - 1
        for part in range(2):
            for z in range(planes):
                for j in range(lane_blocks):
                    sl = slice(128 * j, 128 * j + 128)
                    p = part * planes + z
                    sec_v[j, p, at : at + 1, :] = ghost_rows[part][z : z + 1, sl]
                    share = (step_dt * kinetic) * nears[1 - part][z : z + 1, sl]
                    old = sec_v[j, p, edge : edge + 1, :]
                    sec_v[j, p, edge : edge + 1, :] = old - share if part == 0 else old + share

    lane_c = iota((rows, 128), 1)
    sub_c = iota((rows, 128), 0)
    diag_lane = iota((parts, 128), 1)
    diag_sub = iota((parts, 128), 0)
    plane_c = (lane_c % (2 * planes)) // 2
    for side, keep in enumerate((keep_w, keep_e)):
        got = col_got[side] * keep
        mine = col_msg[side]
        inner = 1 if side == 0 else 127
        odd = 1 if side == 0 else 0
        hit = diag_lane == 2 * diag_sub + odd
        ends = [
            jnp.sum(jnp.where(hit, corner_cols[2 * sy + side], 0.0), axis=0, keepdims=True)
            for sy in range(2)
        ]
        upper = jnp.where(sub_c == 0, ends[0], pltpu.roll(got, 1, 0))
        lower = jnp.where(sub_c == rows - 1, ends[1], pltpu.roll(got, rows - 1, 0))
        below = jnp.where(plane_c == 0, 0.0, pltpu.roll(got, 2, 1))
        above = jnp.where(plane_c == planes - 1, 0.0, pltpu.roll(got, 126, 1))
        beside = (
            (pltpu.roll(got, inner, 1) + pltpu.roll(mine, inner, 1)) + (upper + lower) + (below + above)
        )
        volts = pltpu.roll(got, 64, 1)
        volts = jnp.where(lane_c < 2 * planes, volts, pltpu.roll(volts, 2 * planes, 1))
        coeff = step_dt * (volts + field_1 * height(plane_c) + 6.0 * kinetic)
        move = coeff * got - (step_dt * kinetic) * beside
        ghost[0, side] = got
        ghost[1, side] = (
            got
            + jnp.where(
                lane_c < 2 * planes, pltpu.roll(move, 128 - 2 * planes, 1), -pltpu.roll(move, 2 * planes, 1)
            )
        ) * keep

    lax.fori_loop(0, blocks, fix_columns, 0, unroll=4)
    surface(gather_1, False)
    for k in range(1, x_count):
        line_copy(k, gx).start()
    stores = []
    pieces = 4
    per = blocks // pieces
    for q in range(pieces):
        lax.fori_loop(q * per, (q + 1) * per, run_next, 0)
        for j in range(lane_blocks):
            stores.append(
                pltpu.make_async_copy(
                    psi_v.at[j, :, top + 8 * per * q : top + 8 * per * (q + 1), :],
                    next_hbm.at[:, 8 * per * q : 8 * per * (q + 1), 128 * j : 128 * j + 128],
                    store_sem.at[q, j],
                )
            )
            stores[-1].start()
        if q == 0:
            for k in range(1, x_count):
                line_copy(k, wrap(gx - k, x_count)).wait_recv()
            for k in range(1, y_count):
                sheet_copy(k, gy).start()
            hop_3(gather_0, 0)
    hop_end(gather_0, 0)

    def count_row(i, total):
        for k in range(x_count):
            got = gather_0[i // (y_count // 2), lax.rem(i, y_count // 2) * 2 + k // chips, k % chips]
            total = jnp.where(lane8 == i * x_count + k, got[:, 2 * parts + 2 : 2 * parts + 3], total)
        return total

    live_ref[...] = lax.fori_loop(0, y_count, count_row, jnp.zeros((8, 128), f32))
    for copy in halo:
        copy.wait_send()
    for copy in stores:
        copy.wait()
    for k in range(1, y_count):
        sheet_copy(k, wrap(gy - k, y_count)).wait_recv()
    sends_wait(gather_0, 0)
    for k in range(1, x_count):
        line_copy(k, gx).wait_send()
    for k in range(1, y_count):
        sheet_copy(k, gy).wait_send()


def turns(phase):
    quarter = jnp.floor(phase * 0.6366197723675814 + 0.5)
    rest = phase - quarter * 1.5703125
    rest = rest - quarter * 4.83751296997e-4
    rest = rest - quarter * 7.5497899548918821e-8
    square = rest * rest
    sine = rest + rest * square * (
        -1.6666654611e-1 + square * (8.3321608736e-3 + square * -1.9515295891e-4)
    )
    cosine = (
        1.0
        - 0.5 * square
        + square * square * (4.166664568298827e-2 + square * (-1.388731625493765e-3 + square * 2.443315711809948e-5))
    )
    which = quarter.astype(jnp.int32)
    swap = (which & 1) == 1
    sin_out = jnp.where(swap, cosine, sine)
    cos_out = jnp.where(swap, sine, cosine)
    sin_out = jnp.where((which & 2) == 2, -sin_out, sin_out)
    cos_out = jnp.where(((which + 1) & 2) == 2, -cos_out, cos_out)
    return cos_out, sin_out


def flux_kernel(
    x_count,
    y_count,
    live_ref,
    count_ref,
    order_ref,
    gather_0,
    gather_1,
    weight_ref,
    amp_ref,
    tmp_hbm,
    next_hbm,
    out_ref,
    comp_0,
    comp_1,
    total,
    held,
    fetch_sem,
    copy_sem,
):
    copies = []
    parts = tmp_hbm.shape[0]
    quarter = parts // 4
    for q in range(4):
        sl = slice(q * quarter, (q + 1) * quarter)
        fetch = pltpu.make_async_copy(tmp_hbm.at[sl], held.at[sl], fetch_sem.at[q])
        fetch.start()
        copies.append((fetch, pltpu.make_async_copy(held.at[sl], next_hbm.at[sl], copy_sem.at[q])))
    me = lax.axis_index("gx") * y_count + lax.axis_index("gy")
    groups = count_ref.shape[0]
    slots = amp_ref.shape[0]
    features = weight_ref.shape[1] // 8
    feature = iota((128, 128), 1) < features

    def offset(i, at):
        return at + jnp.where(i < me, count_ref[i], 0)

    own_start = lax.fori_loop(0, groups, offset, 0, unroll=True)
    own_count = count_ref[me]
    waves = []
    for s in range(slots):
        plane = order_ref[jnp.minimum(own_start + s, groups - 1)]
        waves.append((plane.astype(f32) - 0.5 * (groups - 1)) * (k_span / groups))

    tiles = x_count * y_count
    chips = x_count // 2

    def gather_tile(t, n):
        c = live_ref[0, t].astype(jnp.int32)
        at = pl.ds(pl.multiple_of(t * 8, 8), 8)
        block_0 = gather_0[at, :]
        half, row, chip = t // (tiles // 2), (t // chips) % y_count, t % chips
        block_1 = gather_1[row * x_count + 2 * chip + half]
        comp_0[pl.ds(n, 8), :] = block_0
        comp_1[pl.ds(n, 4), :] = block_1
        comp_1[pl.ds(n + 4, 4), :] = pltpu.roll(block_1, 96, 1)
        n = n + jnp.minimum(c, 8)
        comp_0[pl.ds(n, 8), :] = pltpu.roll(block_0, 64, 1)
        comp_1[pl.ds(n, 4), :] = pltpu.roll(block_1, 64, 1)
        comp_1[pl.ds(n + 4, 4), :] = pltpu.roll(block_1, 32, 1)
        return n + jnp.maximum(c - 8, 0)

    live = lax.fori_loop(0, x_count * y_count, gather_tile, 0, unroll=True)

    def clear(i, carry):
        to = pl.ds(live + i * 8, 8)
        comp_0[to, :] = jnp.zeros((8, 128), f32)
        comp_1[to, :] = jnp.zeros((8, 128), f32)
        return carry

    lax.fori_loop(0, 16, clear, 0)
    total[...] = jnp.zeros_like(total)
    kx = (iota((128, 128), 0).astype(f32) - 63.5) * (k_span / 128)
    sub8 = iota((8, 128), 0)
    ky = jnp.zeros((8, 128), f32)
    for s in range(slots):
        ky = jnp.where(sub8 // 2 == s, waves[s], ky)
    moment8 = jnp.where(sub8 % 2 == 0, start_time, later_time).astype(f32)

    def chunk(c, carry):
        at = pl.ds(pl.multiple_of(c * 128, 128), 128)
        rows = (comp_0[at, :], comp_1[at, :])
        place = jnp.transpose(rows[0])
        px, py = place[features : features + 1, :], place[features + 1 : features + 2, :]
        col_x, col_y = rows[0][:, features : features + 1], rows[0][:, features + 1 : features + 2]
        square = col_x * col_x + col_y * col_y
        radius = jnp.sqrt(jnp.where(square > 0.0, square, 1.0))
        nx, ny = col_x / radius, col_y / radius
        right = []
        left = []
        for t, moment in enumerate((start_time, later_time)):
            raw = jnp.where(feature, rows[t], 0.0)
            high = raw.astype(jnp.bfloat16).astype(f32)
            mid = (raw - high).astype(jnp.bfloat16).astype(f32)
            low = (raw - high) - mid
            side = (
                (high + pltpu.roll(mid, features, 1))
                + (pltpu.roll(low, 2 * features, 1) + pltpu.roll(high, 3 * features, 1))
            ).astype(jnp.bfloat16)
            modes = jnp.dot(
                jnp.concatenate([side, side], axis=1), weight_ref[t], preferred_element_type=f32
            )
            ur, ui, dr, di = (modes[:, 128 * i : 128 * i + 128] for i in range(4))
            right.append(
                jnp.concatenate([nx * ur, ny * ur, dr, nx * ui, ny * ui, di], axis=1).astype(jnp.bfloat16)
            )
            left.append(turns(0.5 * kx * kx * moment - kx * px))
        right = jnp.concatenate(right, axis=0)
        rot_cos, rot_sin = turns(0.5 * ky * ky * moment8 - ky * py)

        for first in range(0, slots, 2):

            @pl.when(first < own_count)
            def _():
                sides = []
                pair = range(first, min(first + 2, slots))
                for s in pair:
                    real = []
                    imag = []
                    for t in range(2):
                        bc, bs = rot_cos[2 * s + t : 2 * s + t + 1], rot_sin[2 * s + t : 2 * s + t + 1]
                        ac, as_ = left[t]
                        real.append((ac * bc - as_ * bs).astype(jnp.bfloat16))
                        imag.append((ac * bs + as_ * bc).astype(jnp.bfloat16))
                    sides.append(jnp.concatenate(real, axis=1))
                    sides.append(jnp.concatenate(imag, axis=1))
                prod = jnp.dot(jnp.concatenate(sides, axis=0), right, preferred_element_type=f32)
                for i, s in enumerate(pair):
                    m = [prod[256 * i : 256 * i + 128, 128 * k : 128 * k + 128] for k in range(6)]
                    w = [prod[256 * i + 128 : 256 * i + 256, 128 * k : 128 * k + 128] for k in range(6)]
                    hy = waves[s]
                    total[s, 0] += kx * (m[0] - w[3]) + hy * (m[1] - w[4]) + (m[5] + w[2])
                    total[s, 1] += kx * (m[3] + w[0]) + hy * (m[4] + w[1]) - (m[2] - w[5])

        return carry

    chunks = (live + 127) // 128
    lax.fori_loop(0, jnp.minimum(chunks, 1), chunk, 0)
    for fetch, copy in copies:
        fetch.wait()
        copy.start()
    lax.fori_loop(1, chunks, chunk, 0)
    for s in range(slots):
        for part in range(2):
            sl = pl.ds(part, 128, stride=2)
            inc = jnp.where(s < own_count, (0.5 * flux_weight) * total[s, part], 0.0)
            out_ref[s, sl, :] = amp_ref[s, sl, :] + inc
    for fetch, copy in copies:
        copy.wait()


def shards(psi_now, potential, surf_cells, surf_count, block_count, block_order, amplitude):
    x_count = lax.axis_size("gx")
    y_count = lax.axis_size("gy")
    planes, rows, cols = potential.shape
    parts = 2 * planes
    slots = surf_cells.shape[2]
    own, modes_x, _, modes_z = amplitude.shape
    any_spec = pl.BlockSpec(memory_space=pl.ANY)
    vmem = pl.BlockSpec(memory_space=pltpu.VMEM)
    smem = pl.BlockSpec(memory_space=pltpu.SMEM)
    hbm = pl.BlockSpec(memory_space=pltpu.HBM)
    dma = pltpu.SemaphoreType.DMA
    gathered = jax.ShapeDtypeStruct((2, y_count, x_count // 2, 8, 128), f32)
    sheet = jax.ShapeDtypeStruct((y_count, x_count, 4, 128), f32)
    field = jax.ShapeDtypeStruct((parts, rows, cols), f32)
    staged, gather_0, gather_1, live = pl.pallas_call(
        functools.partial(step_kernel, x_count, y_count),
        out_shape=(field, gathered, sheet, jax.ShapeDtypeStruct((8, 128), f32)),
        in_specs=[smem, smem, hbm, hbm],
        out_specs=(any_spec, vmem, vmem, vmem),
        scratch_shapes=[
            pltpu.VMEM((cols // 128, parts, rows + 16, 128), f32),
            pltpu.VMEM((cols // 128, parts, rows + 16, 128), f32),
            pltpu.VMEM((cols // 128, planes, rows, 128), f32),
            pltpu.VMEM((2, 2 * parts + planes, cols), f32),
            pltpu.VMEM((2, 2 * parts + planes, cols), f32),
            pltpu.VMEM((2, rows, 128), f32),
            pltpu.VMEM((2, rows, 128), f32),
            pltpu.VMEM((4, parts, 128), f32),
            pltpu.VMEM((2, 2, rows, 128), f32),
            dma((2, 2, cols // 128)),
            dma((4, cols // 128)),
            dma((2,)),
            dma((2,)),
            dma((2,)),
            dma((2,)),
            dma((4,)),
            dma((4,)),
            dma((2, x_count)),
            dma((2, x_count)),
            dma((2, y_count)),
            dma((2, y_count)),
        ],
        compiler_params=pltpu.CompilerParams(
            collective_id=0, has_side_effects=True, vmem_limit_bytes=52 * 1024 * 1024
        ),
        name="step",
    )(
        surf_cells,
        surf_count,
        psi_now.reshape(parts, rows, cols),
        potential,
    )
    tiles = x_count * y_count
    psi_next, amplitude_next = pl.pallas_call(
        functools.partial(flux_kernel, x_count, y_count),
        out_shape=(field, jax.ShapeDtypeStruct((own, 2 * modes_x, modes_z), f32)),
        in_specs=[smem, smem, smem, vmem, vmem, vmem, vmem, any_spec],
        out_specs=(any_spec, vmem),
        scratch_shapes=[
            pltpu.VMEM((slots * tiles + 144, 128), f32),
            pltpu.VMEM((slots * tiles + 144, 128), f32),
            pltpu.VMEM((own, 2, modes_x, modes_z), f32),
            pltpu.VMEM((parts, rows, cols), f32),
            dma((4,)),
            dma((4,)),
        ],
        compiler_params=pltpu.CompilerParams(vmem_limit_bytes=52 * 1024 * 1024),
        name="flux",
    )(
        live,
        block_count,
        block_order,
        gather_0.reshape(tiles * 8, 128),
        gather_1.reshape(tiles, 4, 128),
        jnp.asarray(mode_weights(planes, modes_z)),
        amplitude.reshape(own, 2 * modes_x, modes_z),
        staged,
    )
    return psi_next.reshape(psi_now.shape), amplitude_next.reshape(amplitude.shape)


def solution(mesh):
    return jax.shard_map(
        shards,
        mesh=mesh,
        in_specs=(
            P(None, None, "gy", "gx"),
            P(None, "gy", "gx"),
            P("gy", "gx", None),
            P("gy", "gx"),
            P(),
            P(),
            P(("gx", "gy"), None, None, None),
        ),
        out_specs=(P(None, None, "gy", "gx"), P(("gx", "gy"), None, None, None)),
        check_vma=False,
    )
```
